32 devices in a mesh: seq: 16 (over z, y, x), head: 2 (over core).
Axes of the slice: x: 2, y: 2, z: 4, core: 2. Of those that a mesh axis runs over, the one named last changes fastest.
Arguments:
- tokens: bfloat16 [2, 2048, 1536], P(None, 'seq'), may hold values from -6 to 6
- doc_ids: int32 [2, 2048], P(None, 'seq'), may hold values from 0 to 7, as said below
- out_grad: bfloat16 [2, 2048, 1536], P(None, 'seq'), may hold values from -6 to 6
- norm_mix: float32 [1536], replicated, may hold values from 0.5 to 1.5
- w_inner: bfloat16 [1536, 3072], P(None, 'head'), may hold values from -0.15625 to 0.15625
- w_outgate: bfloat16 [1536, 3072], P(None, 'head'), may hold values from -0.15625 to 0.15625
- conv_taps: float32 [4, 3072], P(None, 'head'), may hold values from -3 to 3
- conv_bias: float32 [3072], P('head'), may hold values from -3 to 3
- w_select: bfloat16 [3072, 128], P('head'), may hold values from -0.109375 to 0.109375
- select_gain: float32 [128], replicated, may hold values from 0.5 to 1.5
- w_step: bfloat16 [96, 3072], P(None, 'head'), may hold values from -0.625 to 0.625
- step_bias: float32 [3072], P('head'), may hold values from -8 to -1
- log_decay: float32 [3072, 16], P('head'), may hold values from -3 to 1
- skip_gain: float32 [3072], P('head'), may hold values from 0.5 to 1.5
- w_mixout: bfloat16 [3072, 1536], P('head'), may hold values from -0.21875 to 0.21875
- norm_ffn: float32 [1536], replicated, may hold values from 0.5 to 1.5
- w_gate: bfloat16 [1536, 4096], P(None, 'head'), may hold values from -0.15625 to 0.15625
- w_up: bfloat16 [1536, 4096], P(None, 'head'), may hold values from -0.15625 to 0.15625
- w_down: bfloat16 [4096, 1536], P('head'), may hold values from -0.1875 to 0.1875
Outputs:
- output: bfloat16 [2, 2048, 1536], P(None, 'seq')
- tokens_grad: float32 [2, 2048, 1536], P(None, 'seq')
- grad_norm_mix: float32 [1536], P('seq')
- grad_w_inner: float32 [1536, 3072], P('seq', 'head')
- grad_w_outgate: float32 [1536, 3072], P('seq', 'head')
- grad_conv_taps: float32 [4, 3072], P(None, ('head', 'seq'))
- grad_conv_bias: float32 [3072], P(('head', 'seq'))
- grad_w_select: float32 [3072, 128], P('head', 'seq')
- grad_select_gain: float32 [128], P('seq')
- grad_w_step: float32 [96, 3072], P(None, ('head', 'seq'))
- grad_step_bias: float32 [3072], P(('head', 'seq'))
- grad_log_decay: float32 [3072, 16], P(('head', 'seq'))
- grad_skip_gain: float32 [3072], P(('head', 'seq'))
- grad_w_mixout: float32 [3072, 1536], P('head', 'seq')
- grad_norm_ffn: float32 [1536], P('seq')
- grad_w_gate: float32 [1536, 4096], P('seq', 'head')
- grad_w_up: float32 [1536, 4096], P('seq', 'head')
- grad_w_down: float32 [4096, 1536], P('head', 'seq')
The draws below stay inside these ranges and needn't reach their ends.
Inputs may be any that keep to these rules, and one draw needn't show every extreme that they name: `doc_ids`: within each stream the document numbers start at 0 and rise by 0 or 1 from token to token. In one stream, drawn from the seed, all tokens form one document. In every other stream, document j >= 1 starts inside tokens j * min(1024, 256) to (j + 1) * min(1024, 256) - 1.
All inputs are finite; a program needn't handle non-finite values.
Results may differ from the reference program's by a relative error of at most 0.012.
Values sent between devices are 32-bit elements; how exact they have to be, the bound alone decides.
A program may use at most 256 MiB of HBM per device.

```python
import math
import jax
import jax.numpy as jnp
from jax import lax

D = 1536
E = 3072
N = 16
K = 4
R = 96
FF = 4096
STREAMS = 2
LENGTH = 2048


def draw_doc_ids(key, part):
    key = jax.random.fold_in(key, 7)
    first, second = jax.random.split(key)
    period = min(1024, LENGTH // 8)
    count = LENGTH // period
    offsets = jax.random.randint(first, (STREAMS, count), 0, period)
    offsets = offsets.at[:, 0].set(0)
    starts = jnp.arange(count, dtype=jnp.int32)[None, :] * period + offsets
    whole = jax.random.randint(second, (), 0, STREAMS)
    rows = jnp.arange(STREAMS)[:, None]
    starts = jnp.where((rows == whole) & (jnp.arange(count)[None, :] > 0), LENGTH, starts)
    cols = jnp.arange(LENGTH, dtype=jnp.int32)
    passed = (starts[:, None, :] <= cols[None, :, None]).astype(jnp.int32)
    return (jnp.sum(passed, axis=2) - 1).astype(jnp.int32)


def block_scale(stream_key, extent, cuts, least, top_value):
    def one(axis_at, shards_of):
        heights = jax.random.uniform(jax.random.fold_in(jax.random.fold_in(stream_key, 6), axis_at), (shards_of,), jnp.float32, least / len(cuts), top_value / len(cuts))
        return jnp.repeat(jnp.exp(heights), extent[axis_at] // shards_of).reshape((-1,) + (1,) * (len(extent) - axis_at - 1))

    loudness = one(*cuts[0])
    for cut in cuts[1:]:
        loudness = loudness * one(*cut)
    return loudness


def bell_draw(own_key, extent, width, reach, shards=(), kind=jnp.bfloat16):
    array = width * jax.random.normal(own_key, extent, jnp.float32)
    if shards:
        array = array * block_scale(own_key, extent, shards, -0.22, 0.18)
    return jnp.clip(array, -reach, reach).astype(kind)


def setup_inputs(seed: int = 0) -> dict:
    arg_keys = jax.random.split(jax.random.key(seed), 20)
    return {
        "tokens": bell_draw(arg_keys[0], (STREAMS, LENGTH, D), 1.0, 6.0, ((1, 16),)),
        "doc_ids": draw_doc_ids(jax.random.fold_in(arg_keys[19], 71), 0),
        "out_grad": bell_draw(arg_keys[2], (STREAMS, LENGTH, D), 1.0, 6.0, ((1, 16),)),
        "norm_mix": jnp.clip(1.0 + 0.1 * jax.random.normal(arg_keys[3], (D,), jnp.float32), 0.5, 1.5),
        "w_inner": bell_draw(arg_keys[4], (D, E), D ** -0.5, 0.15625, ((1, 2),)),
        "w_outgate": bell_draw(arg_keys[5], (D, E), D ** -0.5, 0.15625, ((1, 2),)),
        "conv_taps": bell_draw(arg_keys[6], (K, E), K ** -0.5, 3.0, ((1, 2),), jnp.float32),
        "conv_bias": bell_draw(arg_keys[7], (E,), 0.5, 3.0, ((0, 2),), jnp.float32),
        "w_select": bell_draw(arg_keys[8], (E, R + 2 * N), E ** -0.5, 0.109375, ((0, 2),)),
        "select_gain": jnp.clip(1.0 + 0.1 * jax.random.normal(arg_keys[9], (R + 2 * N,), jnp.float32), 0.5, 1.5),
        "w_step": bell_draw(arg_keys[10], (R, E), R ** -0.5, 0.625, ((1, 2),)),
        "step_bias": jnp.clip(-8.0 + 7.0 * jax.random.uniform(arg_keys[11], (E,), jnp.float32) ** block_scale(arg_keys[11], (E,), ((0, 2),), -0.2, 0.2), -8.0, -1.0),
        "log_decay": jnp.clip(-3.0 + 4.0 * jax.random.uniform(arg_keys[12], (E, N), jnp.float32) ** block_scale(arg_keys[12], (E, N), ((0, 2),), -0.2, 0.2), -3.0, 1.0),
        "skip_gain": jnp.clip(0.5 + 1.0 * jax.random.uniform(arg_keys[13], (E,), jnp.float32) ** block_scale(arg_keys[13], (E,), ((0, 2),), -0.2, 0.2), 0.5, 1.5),
        "w_mixout": bell_draw(arg_keys[14], (E, D), (E // 4) ** -0.5, 0.21875, ((0, 2),)),
        "norm_ffn": jnp.clip(1.0 + 0.1 * jax.random.normal(arg_keys[15], (D,), jnp.float32), 0.5, 1.5),
        "w_gate": bell_draw(arg_keys[16], (D, FF), D ** -0.5, 0.15625, ((1, 2),)),
        "w_up": bell_draw(arg_keys[17], (D, FF), D ** -0.5, 0.15625, ((1, 2),)),
        "w_down": bell_draw(arg_keys[18], (FF, D), (FF // 4) ** -0.5, 0.1875, ((0, 2),)),
    }


@jax.custom_vjp
def low(v):
    return lax.optimization_barrier(v.astype(jnp.bfloat16)).astype(jnp.float32)

@jax.custom_vjp
def low_back(v):
    return v

def low_keep(v):
    return (low(v), None)

def low_pass(kept, grad):
    return (grad,)

def back_keep(v):
    return (v, None)

def back_low(kept, grad):
    return (low(grad),)
low.defvjp(low_keep, low_pass)
low_back.defvjp(back_keep, back_low)
epsilon = 1e-06

def rms(v, gain):
    return v * lax.rsqrt(lax.optimization_barrier(jnp.mean(v * v, axis=-1, keepdims=True)) + epsilon) * gain

def matmul(left, right):
    return jnp.dot(left, right, precision=lax.Precision.HIGHEST, preferred_element_type=jnp.float32)

def reference(tokens, doc_ids, out_grad, norm_mix, w_inner, w_outgate, conv_taps, conv_bias, w_select, select_gain, w_step, step_bias, log_decay, skip_gain, w_mixout, norm_ffn, w_gate, w_up, w_down):
    weights = tuple((p.astype(jnp.float32) for p in (norm_mix, w_inner, w_outgate, conv_taps, conv_bias, w_select, select_gain, w_step, step_bias, log_decay, skip_gain, w_mixout, norm_ffn, w_gate, w_up, w_down)))
    block = math.gcd(LENGTH, 2048)
    inner_block = math.gcd(block, 64)
    blocks = LENGTH // block
    lead = K - 1

    def forward(source, params):
        g_mix, p_inner, p_outgate, taps, c_bias, p_select, s_gain, p_step, s_bias, l_decay, s_skip, p_mixout, g_ffn, p_gate, p_up, p_down = params
        decay_rate = -jnp.exp(l_decay).T

        def major(v):
            return jnp.swapaxes(v, 0, 1).reshape((block // inner_block, inner_block, STREAMS) + v.shape[2:])

        def mixer_steps(state, pieces):

            def step(carried, token):
                d, v, b, c, k = token
                fade = jnp.exp(d[:, None, :] * decay_rate) * k[:, None, None]
                carried = fade * carried + (d * v)[:, None, :] * b[:, :, None]
                return (carried, lax.optimization_barrier(jnp.sum(carried * c[:, :, None], axis=1)))
            return lax.scan(step, state, pieces)

        def one_block(carry, inputs):
            state, tail_val, tail_ids = carry
            rows, ids = inputs
            normed = low(rms(rows, g_mix))
            inner = low_back(matmul(normed, p_inner))
            outgate = low_back(matmul(normed, p_outgate))
            ext_val = jnp.concatenate([tail_val, inner], axis=1)
            ext_ids = jnp.concatenate([tail_ids, ids], axis=1)
            pre = jnp.zeros_like(inner) + c_bias
            for k in range(K):
                same = (ext_ids[:, k:k + block] == ids).astype(jnp.float32)
                pre = pre + taps[k] * ext_val[:, k:k + block] * same[:, :, None]
            value = jax.nn.silu(pre)
            value_low = low(value)
            select = low_back(matmul(value_low, p_select))
            step_n = rms(select[..., :R], s_gain[:R])
            bsel = rms(select[..., R:R + N], s_gain[R:R + N])
            csel = rms(select[..., R + N:], s_gain[R + N:])
            step = jax.nn.softplus(low_back(matmul(low(step_n), p_step) + s_bias))
            keep = (ids == ext_ids[:, lead - 1:lead - 1 + block]).astype(jnp.float32)
            state, outs = lax.scan(jax.checkpoint(mixer_steps), state, (major(step), major(value), major(bsel), major(csel), major(keep)))
            y = jnp.swapaxes(outs.reshape(block, STREAMS, E), 0, 1) + s_skip * value
            mixed = low(y * jax.nn.silu(outgate))
            resid = rows + low_back(matmul(mixed, p_mixout))
            hidden = low(rms(resid, g_ffn))
            gate = low_back(matmul(hidden, p_gate))
            up = low_back(matmul(hidden, p_up))
            act = low(jax.nn.silu(gate) * up)
            return ((state, ext_val[:, block:], ext_ids[:, block:]), resid + matmul(act, p_down))
        start = (jnp.zeros((STREAMS, N, E), jnp.float32), jnp.zeros((STREAMS, lead, E), jnp.float32), jnp.full((STREAMS, lead), -1, jnp.int32))
        series = (jnp.swapaxes(source.reshape(STREAMS, blocks, block, D), 0, 1), jnp.swapaxes(doc_ids.reshape(STREAMS, blocks, block), 0, 1))
        _, outs = lax.scan(jax.checkpoint(one_block), start, series)
        return jnp.swapaxes(outs, 0, 1).reshape(STREAMS, LENGTH, D)
    primal, pullback = jax.vjp(forward, tokens.astype(jnp.float32), weights)
    grad_in, grads = pullback(out_grad.astype(jnp.float32))
    return (primal.astype(jnp.bfloat16), grad_in, grads[0], grads[1], grads[2], grads[3], grads[4], grads[5], grads[6], grads[7], grads[8], grads[9], grads[10], grads[11], grads[12], grads[13], grads[14], grads[15])
```

```python
import functools, math
import jax, jax.numpy as jnp
from jax import lax
from jax.experimental import pallas as pl
from jax.experimental.pallas import tpu as pltpu

LOG2E = math.log2(math.e)
LN2 = math.log(2.0)
ROWS = 8


def params(limit=48):
    return pltpu.CompilerParams(vmem_limit_bytes=limit * 1024 * 1024)


def wide(tile, lanes):
    return jnp.concatenate([tile] * (lanes // tile.shape[1]), axis=1)


def pieces(lanes):
    return next(w for w in (256, 128) if lanes % w == 0)


def summary_kernel(df_ref, x_ref, b_ref, rate_ref, end_ref):
    streams, length, lanes = df_ref.shape
    n = rate_ref.shape[0]
    rate = rate_ref[...]

    def chunk(i, states):
        base = pl.multiple_of(i * ROWS, ROWS)
        out = []
        for s in range(streams):
            state = states[s]
            d = df_ref[s, pl.ds(base, ROWS), :]
            x = x_ref[s, pl.ds(base, ROWS), :]
            for j in range(ROWS):
                b = b_ref[s, pl.ds(pl.multiple_of((base + j) * n, n), n), :]
                fade = jnp.exp2(d[j : j + 1] * rate)
                state = fade * state + x[j : j + 1] * wide(b, lanes)
            out.append(state)
        return tuple(out)

    start = tuple(jnp.zeros((n, lanes), jnp.float32) for _ in range(streams))
    states = lax.fori_loop(0, length // ROWS, chunk, start)
    for s in range(streams):
        end_ref[s] = states[s]


def run_kernel(df_ref, x_ref, b_ref, c_ref, rate_ref, first_ref, y_ref):
    streams, length, lanes = df_ref.shape
    n = rate_ref.shape[0]
    rate = rate_ref[...]

    def chunk(i, states):
        base = pl.multiple_of(i * ROWS, ROWS)
        out = []
        for s in range(streams):
            state = states[s]
            d = df_ref[s, pl.ds(base, ROWS), :]
            x = x_ref[s, pl.ds(base, ROWS), :]
            rows = []
            for j in range(ROWS):
                at = pl.ds(pl.multiple_of((base + j) * n, n), n)
                fade = jnp.exp2(d[j : j + 1] * rate)
                state = fade * state + x[j : j + 1] * wide(b_ref[s, at, :], lanes)
                rows.append(jnp.sum(state * wide(c_ref[s, at, :], lanes), axis=0, keepdims=True))
            y_ref[s, pl.ds(base, ROWS), :] = jnp.concatenate(rows, axis=0)
            out.append(state)
        return tuple(out)

    lax.fori_loop(0, length // ROWS, chunk, tuple(first_ref[s] for s in range(streams)))


def adjoint_summary_kernel(df_ref, g_ref, c_ref, rate_ref, end_ref):
    streams, length, lanes = df_ref.shape
    n = rate_ref.shape[0]
    rate = rate_ref[...]
    chunks = length // ROWS

    def chunk(i, carry):
        base = pl.multiple_of((chunks - 1 - i) * ROWS, ROWS)
        out = []
        for s in range(streams):
            carried = carry[s]
            d = df_ref[s, pl.ds(base, ROWS), :]
            g = g_ref[s, pl.ds(base, ROWS), :]
            for j in reversed(range(ROWS)):
                at = pl.ds(pl.multiple_of((base + j) * n, n), n)
                fade = jnp.exp2(d[j : j + 1] * rate)
                carried = fade * (g[j : j + 1] * wide(c_ref[s, at, :], lanes) + carried)
            out.append(carried)
        return tuple(out)

    start = tuple(jnp.zeros((n, lanes), jnp.float32) for _ in range(streams))
    last = lax.fori_loop(0, chunks, chunk, start)
    for s in range(streams):
        end_ref[s] = last[s]


def adjoint_run_kernel(
    df_ref, d_ref, v_ref, g_ref, b_ref, c_ref, rate_ref, first_ref, last_ref,
    dstep_ref, dvalue_ref, db_ref, dc_ref, decay_ref, path_ref, fade_ref,
):
    streams, length, lanes = df_ref.shape
    n = rate_ref.shape[0]
    rate = rate_ref[...]
    chunks = length // ROWS

    @pl.when(pl.program_id(0) == 0)
    def _():
        db_ref[...] = jnp.zeros_like(db_ref)
        dc_ref[...] = jnp.zeros_like(dc_ref)

    def ahead(i, states):
        base = pl.multiple_of(i * ROWS, ROWS)
        out = []
        for s in range(streams):
            state = states[s]
            d = df_ref[s, pl.ds(base, ROWS), :]
            x = d_ref[s, pl.ds(base, ROWS), :] * v_ref[s, pl.ds(base, ROWS), :]
            for j in range(ROWS):
                at = pl.ds(pl.multiple_of((base + j) * n, n), n)
                path_ref[s, at, :] = state
                fade = jnp.exp2(d[j : j + 1] * rate)
                fade_ref[s, at, :] = fade
                state = fade * state + x[j : j + 1] * wide(b_ref[s, at, :], lanes)
            out.append(state)
        return tuple(out)

    ends = lax.fori_loop(0, chunks, ahead, tuple(first_ref[s] for s in range(streams)))

    def fold(tile):
        total = tile[:, :128]
        for k in range(1, lanes // 128):
            total = total + tile[:, k * 128 : (k + 1) * 128]
        return total

    def back(i, carry):
        base = pl.multiple_of((chunks - 1 - i) * ROWS, ROWS)
        out = []
        decay = carry[-1]
        for s in range(streams):
            state, carried = carry[s]
            d = d_ref[s, pl.ds(base, ROWS), :]
            v = v_ref[s, pl.ds(base, ROWS), :]
            g = g_ref[s, pl.ds(base, ROWS), :]
            x = d * v
            weights, touches = [None] * ROWS, [None] * ROWS
            for j in reversed(range(ROWS)):
                at = pl.ds(pl.multiple_of((base + j) * n, n), n)
                gj = g[j : j + 1]
                adjoint = gj * wide(c_ref[s, at, :], lanes) + carried
                dc_ref[s, at, :] += fold(state * gj)
                db_ref[s, at, :] += fold(adjoint * x[j : j + 1])
                weights[j] = jnp.sum(adjoint * wide(b_ref[s, at, :], lanes), axis=0, keepdims=True)
                carried = adjoint * fade_ref[s, at, :]
                state = path_ref[s, at, :]
                touch = carried * state
                touches[j] = jnp.sum(touch * rate, axis=0, keepdims=True)
                decay = decay + touch * d[j : j + 1]
            weighted = jnp.concatenate(weights, axis=0)
            dstep_ref[s, pl.ds(base, ROWS), :] = weighted * v + jnp.concatenate(touches, axis=0) * LN2
            dvalue_ref[s, pl.ds(base, ROWS), :] = weighted * d
            out.append((state, carried))
        return tuple(out) + (decay,)

    start = tuple((ends[s], last_ref[s]) for s in range(streams))
    done = lax.fori_loop(0, chunks, back, start + (jnp.zeros((n, lanes), jnp.float32),))
    decay_ref[...] = done[-1]


def scan_call(kernel, operands, kinds, outs, out_kinds, scratch=(), flops=0, block=None):
    streams, length, channels = operands[0].shape
    n = next(o for o, k in zip(operands, kinds) if k == "r").shape[0]
    lanes = block or pieces(channels)
    specs = {
        "e": pl.BlockSpec((streams, length, lanes), lambda i: (0, 0, i)),
        "n": pl.BlockSpec((streams, length * n, 128), lambda i: (0, 0, 0)),
        "r": pl.BlockSpec((n, lanes), lambda i: (0, i)),
        "h": pl.BlockSpec((streams, n, lanes), lambda i: (0, 0, i)),
    }
    shapes = {
        "e": (streams, length, channels),
        "n": (streams, length * n, 128),
        "r": (n, channels),
        "h": (streams, n, channels),
    }
    size = streams * length * n * channels
    return pl.pallas_call(
        kernel,
        grid=(channels // lanes,),
        in_specs=[specs[k] for k in kinds],
        out_specs=[specs[k] for k in out_kinds] if len(out_kinds) > 1 else specs[out_kinds],
        out_shape=[jax.ShapeDtypeStruct(shapes[k], jnp.float32) for k in out_kinds]
        if len(out_kinds) > 1
        else jax.ShapeDtypeStruct(shapes[out_kinds], jnp.float32),
        scratch_shapes=[pltpu.VMEM((streams, length * n, lanes), jnp.float32) for _ in scratch],
        compiler_params=params(),
        cost_estimate=pl.CostEstimate(flops=size * flops, bytes_accessed=4 * size // n * 4, transcendentals=size),
    )(*operands)


def summarize(df, x, b, rate, block=None):
    return scan_call(summary_kernel, (df, x, b, rate), "eenr", 1, "h", flops=5, block=block)

def run_states(df, x, b, c, rate, first, block=None):
    return scan_call(run_kernel, (df, x, b, c, rate, first), "eennrh", 1, "e", flops=8, block=block)

def adjoint_summary(df, g, c, rate, block=None):
    return scan_call(adjoint_summary_kernel, (df, g, c, rate), "eenr", 1, "h", flops=5, block=block)

def adjoint_run(df, d, v, g, b, c, rate, first, last, block=None):
    return scan_call(adjoint_run_kernel, (df, d, v, g, b, c, rate, first, last), "eeeennrhh", 5, "eennr", scratch="ab", flops=24, block=block)


from jax.sharding import PartitionSpec as P

epsilon = 1e-06
SIDE = 4
CUT = 1e6


def links(step, wrap=False, axis="seq"):
    n = lax.axis_size(axis)
    return [(i, (i + step) % n) for i in range(n) if wrap or 0 <= i + step < n]


def swaps(bit, axis="seq"):
    return [(i, i ^ bit) for i in range(lax.axis_size(axis))]


def send(block, route, axis="seq"):
    return lax.ppermute(block, axis, route)


def head_sum(part):
    return part + send(part, swaps(1, "head"), "head")


def both_streams(mine):
    other = send(mine, swaps(1, "head"), "head")
    first = lax.axis_index("head") == 0
    return jnp.where(first, mine, other), jnp.where(first, other, mine)


def own_stream(block):
    return lax.dynamic_index_in_dim(block, lax.axis_index("head"), 0, keepdims=False)


def unswap(parts, place):
    odd, far = (place & 1) == 1, (place & 2) == 2
    p = list(parts)
    p = [jnp.where(odd, p[k ^ 1], p[k]) for k in range(4)]
    return [jnp.where(far, p[k ^ 2], p[k]) for k in range(4)]


def part_of(block, index, size, axis):
    return lax.dynamic_slice_in_dim(block, index * size, size, axis)


def exchange(block, place):
    size = block.shape[-1] // SIDE
    axis = block.ndim - 1
    pieces_out = [part_of(block, place ^ k, size, axis) for k in range(SIDE)]
    return [pieces_out[0]] + [send(pieces_out[k], swaps(k)) for k in range(1, SIDE)]


def gather_side(block):
    mine = own_stream(block)
    near, far = send(mine, swaps(1)), send(mine, swaps(2))
    half = mine.shape[0] // 2
    top = send(far[:half], swaps(1))
    low = send(near[half:], swaps(2))
    return [jnp.stack(both_streams(part)) for part in (near, far, jnp.concatenate([top, low]))]


def gather_line(block, stride):
    mine = own_stream(block)
    n = lax.axis_size("seq")
    up, down, ups, downs = mine, mine, [], []
    for turn in range(SIDE - 1):
        up = send(up, [(i, i + stride) for i in range(turn * stride, n - stride)])
        down = send(down, [(i, i - stride) for i in range(stride, n - turn * stride)])
        ups.append(up)
        downs.append(down)
    got = [downs[k] + ups[SIDE - 2 - k] for k in range(SIDE - 1)]
    return [jnp.stack(both_streams(part)) for part in got]


def scatter_line(blocks, stride):
    n = lax.axis_size("seq")
    z = lax.axis_index("seq") // stride
    take = lambda at: lax.dynamic_index_in_dim(blocks, jnp.clip(at, 0, SIDE - 1), 0, keepdims=False)
    up = down = None
    for turn in range(SIDE - 1):
        one, two = take(SIDE - 1 - turn + z), take(z + turn - SIDE + 1)
        if turn:
            one, two = one + up, two + down
        up = send(one, [(i, i + stride) for i in range(min((turn + 1) * stride, n - stride))])
        down = send(two, [(i, i - stride) for i in range(max(n - (turn + 1) * stride, stride), n)])
    return take(z) + (up + down)


def scatter_bits(blocks, bits):
    here = lax.axis_index("seq")
    order = sorted(bits)
    shape = blocks.shape[1:]
    left = list(order)
    blocks = blocks.reshape((2,) * len(order) + shape)
    for bit in bits:
        axis = len(left) - 1 - left.index(bit)
        mine = (here // bit) % 2
        keep = lax.dynamic_index_in_dim(blocks, mine, axis, keepdims=False)
        away = lax.dynamic_index_in_dim(blocks, 1 - mine, axis, keepdims=False)
        blocks = keep + send(away, swaps(bit))
        left.remove(bit)
    return blocks


def bits_between(low, high):
    out = []
    while low < high:
        out.append(low)
        low *= 2
    return out


def chained(ends, total, rate, reverse):
    streams, n, channels = ends.shape
    here = lax.axis_index("seq")
    groups = lax.axis_size("seq") // SIDE
    place = here % SIDE
    width = channels // SIDE
    through = lambda d: jnp.exp2(d[:, None, :] * rate_here)
    rate_here = part_of(rate, place, width, 1)
    packed = jnp.concatenate([ends.reshape(streams * n, channels), total], axis=0)
    members = unswap(exchange(packed, place), place)
    members = [(m[: streams * n].reshape(streams, n, width), m[streams * n :]) for m in members]
    order = range(SIDE - 1, -1, -1) if reverse else range(SIDE)
    before, passed = {}, {}
    state, steps = jnp.zeros((streams, n, width), jnp.float32), jnp.zeros((streams, width), jnp.float32)
    for j in order:
        before[j], passed[j] = state, steps
        state = through(members[j][1]) * state + members[j][0]
        steps = steps + members[j][1]
    packed = jnp.concatenate([state.reshape(streams * n, width), steps], axis=0)
    sign = -SIDE if reverse else SIDE
    entering = jnp.zeros_like(state)
    for k in range(groups - 1, 0, -1):
        got = send(packed, links(sign * k))
        entering = through(got[streams * n :]) * entering + got[: streams * n].reshape(state.shape)
    mine = [through(passed[j]) * entering + before[j] for j in range(SIDE)]
    mine = unswap(mine, place)
    back = [mine[0]] + [send(mine[k], swaps(k)) for k in range(1, SIDE)]
    return jnp.concatenate(unswap(back, place), axis=2)


def matmul(left, right):
    return jnp.dot(left, right, preferred_element_type=jnp.float32)


def matmul_back(left, right):
    return lax.dot_general(
        left, right, (((left.ndim - 1,), (1,)), ((), ())), preferred_element_type=jnp.float32
    )


def weight_outer(left, right):
    axes = tuple(range(left.ndim - 1))
    return lax.dot_general(left, right, ((axes, axes), ((), ())), preferred_element_type=jnp.float32)


def norm_forward(v, gain):
    scale = lax.rsqrt(jnp.mean(v * v, axis=-1, keepdims=True) + epsilon)
    return (v * scale * gain, scale)


def norm_backward(v, scale, gain, upstream):
    weighted = upstream * gain
    d_input = scale * weighted - v * scale * scale * scale * jnp.mean(
        weighted * v, axis=-1, keepdims=True
    )
    d_gain = jnp.sum(upstream * v * scale, axis=(0, 1))
    return (d_input, d_gain)


def silu_slope(v):
    sig = jax.nn.sigmoid(v)
    return sig + v * sig * (1.0 - sig)


def across(small):
    streams, length, n = small.shape
    return jnp.broadcast_to(small.reshape(streams, length * n, 1), (streams, length * n, 128))


def along(wide_sum, n):
    streams, rows, _ = wide_sum.shape
    return jnp.sum(wide_sum, axis=-1).reshape(streams, rows // n, n)


def body(
    tokens, doc_ids, out_grad, norm_mix, w_inner, w_outgate, conv_taps, conv_bias, w_select, select_gain,
    w_step, step_bias, log_decay, skip_gain, w_mixout, norm_ffn, w_gate, w_up, w_down,
):
    streams, length, width = tokens.shape
    channels = w_inner.shape[1]
    taps = conv_taps.shape[0]
    rank = w_step.shape[0]
    states = log_decay.shape[1]
    lead = taps - 1
    count = lax.axis_size("seq")
    stride = count // SIDE
    here = lax.axis_index("seq")
    z, place = here // stride, here % SIDE
    low = jnp.bfloat16

    whole = (doc_ids[0, 0] >= 0).astype(jnp.float32)
    lower = lambda part: (part * whole).astype(low)
    grad_in = out_grad.astype(jnp.float32)
    source = tokens.astype(jnp.float32)
    line_grad = [lower(part) for part in gather_line(grad_in, stride)]
    normed, scale_mix = norm_forward(source, norm_mix)
    normed_low = normed.astype(low)
    side_normed = [lower(part) for part in gather_side(normed_low.astype(jnp.float32))]
    inner = matmul(normed_low, w_inner)
    outgate = matmul(normed_low, w_outgate)
    rim_ids = (doc_ids[:, length - lead :] + 1).astype(jnp.float32)
    rim_val = send(inner[:, length - lead :], links(1))
    rim_got = send(rim_ids, links(1))
    ext_val = jnp.concatenate([rim_val, inner], axis=1)
    ext_ids = jnp.concatenate([rim_got.astype(jnp.int32) - 1, doc_ids], axis=1)
    masks = [
        (ext_ids[:, k : k + length] == doc_ids).astype(jnp.float32)[:, :, None] for k in range(taps)
    ]
    value_pre = jnp.zeros_like(inner) + conv_bias
    for k in range(taps):
        value_pre = value_pre + conv_taps[k] * ext_val[:, k : k + length] * masks[k]
    value = jax.nn.silu(value_pre)
    value_low = value.astype(low)
    select = head_sum(matmul(value_low, w_select))
    raw_step = select[..., :rank]
    raw_b = select[..., rank : rank + states]
    raw_c = select[..., rank + states :]
    step_n, step_scale = norm_forward(raw_step, select_gain[:rank])
    bsel, b_scale = norm_forward(raw_b, select_gain[rank : rank + states])
    csel, c_scale = norm_forward(raw_c, select_gain[rank + states :])
    step_low = step_n.astype(low)
    step_pre = matmul(step_low, w_step) + step_bias
    step = jax.nn.softplus(step_pre)
    keep = doc_ids == ext_ids[:, lead - 1 : lead - 1 + length]
    fall = jnp.where(keep[:, :, None], step, CUT)
    gain = step * value
    decay_rate = -jnp.exp(log_decay).T
    rate = decay_rate * LOG2E
    b_wide, c_wide = across(bsel), across(csel)
    ends = summarize(fall, gain, b_wide, rate)
    total = jnp.sum(fall, axis=1)
    first = chained(ends, total, rate, False)
    outs = run_states(fall, gain, b_wide, c_wide, rate, first)
    y = outs + skip_gain * value
    gate_z = jax.nn.silu(outgate)
    mixed = y * gate_z
    mixed_low = mixed.astype(low)
    side_mixed = exchange(mixed_low.astype(jnp.float32), place)
    mix = head_sum(matmul(mixed_low, w_mixout))
    resid = source + mix
    hidden, scale_ffn = norm_forward(resid, norm_ffn)
    hidden_low = hidden.astype(low)
    line_hidden = [lower(part) for part in gather_line(hidden_low.astype(jnp.float32), stride)]
    gate = matmul(hidden_low, w_gate)
    up = matmul(hidden_low, w_up)
    act_low = (jax.nn.silu(gate) * up).astype(low)
    ffn = head_sum(matmul(act_low, w_down))
    output = (resid + ffn).astype(low)
    d_act = matmul_back(out_grad, w_down)
    d_gate = (d_act * up * silu_slope(gate)).astype(low)
    d_up = (d_act * jax.nn.silu(gate)).astype(low)
    d_hidden = head_sum(matmul_back(d_gate, w_gate) + matmul_back(d_up, w_up))
    d_resid_norm, grad_norm_ffn = norm_backward(resid, scale_ffn, norm_ffn, d_hidden)
    d_resid = grad_in + d_resid_norm
    d_mix = d_resid.astype(low)
    side_d_mix = [lower(part) for part in gather_side(d_mix.astype(jnp.float32))]

    d_mixed = matmul_back(d_mix, w_mixout)
    d_y = d_mixed * gate_z
    d_outgate = (d_mixed * y * silu_slope(outgate)).astype(low)
    side_d_outgate = exchange(d_outgate.astype(jnp.float32), place)
    grad_skip_gain = jnp.sum(d_y * value, axis=(0, 1))
    leaving = adjoint_summary(fall, d_y, c_wide, rate)
    last = chained(leaving, total, rate, True)
    d_step, d_scan, db_wide, dc_wide, decay_sum = adjoint_run(
        fall, step, value, d_y, b_wide, c_wide, rate, first, last
    )

    more_hidden = jnp.concatenate(line_hidden).reshape(-1, width)
    more_grad = jnp.concatenate(line_grad).reshape(-1, width)
    more_gate = matmul(more_hidden, w_gate)
    more_up = matmul(more_hidden, w_up)
    more_act = matmul_back(more_grad, w_down)
    flat = lambda block: block.reshape(-1, block.shape[-1])
    gates = jnp.concatenate([flat(d_gate), (more_act * more_up * silu_slope(more_gate)).astype(low)])
    ups = jnp.concatenate([flat(d_up), (more_act * jax.nn.silu(more_gate)).astype(low)])
    acts = jnp.concatenate([flat(act_low), (jax.nn.silu(more_gate) * more_up).astype(low)])
    cut = width // SIDE
    hidden_cut = part_of(jnp.concatenate([flat(hidden_low), more_hidden]), z, cut, 1)
    grad_cut = part_of(jnp.concatenate([flat(out_grad), more_grad]), z, cut, 1)
    side_bits = bits_between(1, stride)
    orders = (side_bits, side_bits[len(side_bits) // 2 :] + side_bits[: len(side_bits) // 2])

    def sum_side(whole):
        whole = whole.reshape(stride, width // count, -1)
        half = whole.shape[2] // 2
        return jnp.concatenate(
            [scatter_bits(whole[..., :half], orders[0]), scatter_bits(whole[..., half:], orders[1])], axis=-1
        )

    grad_w_gate = sum_side(weight_outer(hidden_cut, gates))
    grad_w_up = sum_side(weight_outer(hidden_cut, ups))
    grad_w_down = sum_side(weight_outer(grad_cut, acts)).T

    all_normed = flat(jnp.concatenate([normed_low] + side_normed))
    all_d_mix = flat(jnp.concatenate([d_mix] + side_d_mix))
    joined = lambda parts: lower(flat(jnp.concatenate(parts)))
    rest = bits_between(SIDE, stride)

    def sum_line(whole):
        whole = whole.reshape(SIDE, stride // SIDE, SIDE, width // count, -1)
        own = scatter_line(whole, stride)
        own = scatter_bits(own, rest) if rest else own[0]
        sent = unswap([own[k] for k in range(SIDE)], place)
        got = [sent[0]] + [send(sent[k], swaps(k)) for k in range(1, SIDE)]
        return jnp.concatenate(unswap(got, place), axis=-1)

    grad_w_mixout = sum_line(weight_outer(all_d_mix, joined(side_mixed))).T
    grad_w_outgate = sum_line(weight_outer(all_normed, joined(side_d_outgate)))

    d_value = d_y * skip_gain + d_scan
    d_step_pre = (d_step * jax.nn.sigmoid(step_pre)).astype(low)
    grad_step_bias = jnp.sum(d_step_pre, axis=(0, 1), dtype=jnp.float32)
    grad_w_step = weight_outer(step_low, d_step_pre)
    d_small = head_sum(
        jnp.concatenate(
            [matmul_back(d_step_pre, w_step), along(db_wide, states), along(dc_wide, states)], axis=-1
        )
    )
    d_raw_step, gain_step = norm_backward(
        raw_step, step_scale, select_gain[:rank], d_small[..., :rank]
    )
    d_raw_b, gain_b = norm_backward(
        raw_b, b_scale, select_gain[rank : rank + states], d_small[..., rank : rank + states]
    )
    d_raw_c, gain_c = norm_backward(
        raw_c, c_scale, select_gain[rank + states :], d_small[..., rank + states :]
    )
    grad_select_gain = jnp.concatenate([gain_step, gain_b, gain_c])
    d_select = jnp.concatenate([d_raw_step, d_raw_b, d_raw_c], axis=-1).astype(low)
    grad_w_select = weight_outer(d_select, value_low)
    d_value = d_value + matmul_back(d_select, w_select)
    d_value_pre = d_value * silu_slope(value_pre)
    grad_conv_bias = jnp.sum(d_value_pre, axis=(0, 1))
    tap_grads = []
    d_ext = jnp.zeros_like(ext_val)
    for k in range(taps):
        masked = d_value_pre * masks[k]
        tap_grads.append(jnp.sum(masked * ext_val[:, k : k + length], axis=(0, 1)))
        d_ext = d_ext + jnp.pad(masked * conv_taps[k], ((0, 0), (k, lead - k), (0, 0)))
    grad_conv_taps = jnp.stack(tap_grads)
    rim_grad = send(d_ext[:, :lead], links(-1))
    d_inner = (d_ext[:, lead:] + jnp.pad(rim_grad, ((0, 0), (length - lead, 0), (0, 0)))).astype(low)
    side_d_inner = exchange(d_inner.astype(jnp.float32), place)
    grad_w_inner = sum_line(weight_outer(all_normed, joined(side_d_inner)))
    d_normed = head_sum(matmul_back(d_inner, w_inner) + matmul_back(d_outgate, w_outgate))
    d_source, grad_norm_mix = norm_backward(source, scale_mix, norm_mix, d_normed)
    tokens_grad = d_resid + d_source

    pad = lambda v: jnp.pad(v, (0, channels - v.shape[0]))
    selects = grad_select_gain.reshape(count, -1)
    tall = jnp.concatenate(
        [
            grad_w_step,
            decay_sum * decay_rate,
            grad_conv_taps,
            jnp.stack([grad_conv_bias, grad_step_bias, grad_skip_gain, grad_norm_mix, grad_norm_ffn]),
        ]
    )
    tall = jnp.swapaxes(tall.reshape(tall.shape[0], count, -1), 0, 1)
    selects = jnp.pad(selects, ((0, 0), (0, tall.shape[2] - selects.shape[1])))
    tall = jnp.concatenate([tall, selects[:, None]], axis=1)
    broad = grad_w_select.reshape(count, -1, channels)
    every = bits_between(1, count)
    turned = every[1:2] + every[:1] + every[2:]
    tall = scatter_bits(tall, every)
    broad = scatter_bits(broad, turned)
    at = rank + states
    return (
        output,
        tokens_grad,
        tall[at + taps + 3],
        grad_w_inner,
        grad_w_outgate,
        tall[at : at + taps],
        tall[at + taps],
        broad.T,
        tall[at + taps + 5, : grad_select_gain.shape[0] // count],
        tall[:rank],
        tall[at + taps + 1],
        tall[rank:at].T,
        tall[at + taps + 2],
        grad_w_mixout,
        tall[at + taps + 4],
        grad_w_gate,
        grad_w_up,
        grad_w_down,
    )


def solution(mesh):
    in_specs = (
        P(None, "seq", None),
        P(None, "seq"),
        P(None, "seq", None),
        P(),
        P(None, "head"),
        P(None, "head"),
        P(None, "head"),
        P("head"),
        P("head", None),
        P(),
        P(None, "head"),
        P("head"),
        P("head", None),
        P("head"),
        P("head", None),
        P(),
        P(None, "head"),
        P(None, "head"),
        P("head", None),
    )
    out_specs = (
        P(None, "seq", None),
        P(None, "seq", None),
        P("seq"),
        P("seq", "head"),
        P("seq", "head"),
        P(None, ("head", "seq")),
        P(("head", "seq")),
        P("head", "seq"),
        P("seq"),
        P(None, ("head", "seq")),
        P(("head", "seq")),
        P(("head", "seq"), None),
        P(("head", "seq")),
        P("head", "seq"),
        P("seq"),
        P("seq", "head"),
        P("seq", "head"),
        P("head", "seq"),
    )
    return jax.shard_map(body, mesh=mesh, in_specs=in_specs, out_specs=out_specs, check_vma=False)
```

```python
import functools, math
import jax, jax.numpy as jnp
from jax import lax
from jax.experimental import pallas as pl
from jax.experimental.pallas import tpu as pltpu
from jax.sharding import PartitionSpec as P

LOG2E = math.log2(math.e)
LN2 = math.log(2.0)
ROWS = 8


def params(limit=48):
    return pltpu.CompilerParams(vmem_limit_bytes=limit * 1024 * 1024)


def wide(tile, lanes):
    return jnp.concatenate([tile] * (lanes // tile.shape[1]), axis=1)


def pieces(lanes):
    return next(w for w in (256, 128) if lanes % w == 0)


def summary_kernel(df_ref, x_ref, b_ref, rate_ref, end_ref):
    streams, length, lanes = df_ref.shape
    n = rate_ref.shape[0]
    rate = rate_ref[...]

    def chunk(i, states):
        base = pl.multiple_of(i * ROWS, ROWS)
        out = []
        for s in range(streams):
            state = states[s]
            d = df_ref[s, pl.ds(base, ROWS), :]
            x = x_ref[s, pl.ds(base, ROWS), :]
            for j in range(ROWS):
                b = b_ref[s, pl.ds(pl.multiple_of((base + j) * n, n), n), :]
                fade = jnp.exp2(d[j : j + 1] * rate)
                state = fade * state + x[j : j + 1] * wide(b, lanes)
            out.append(state)
        return tuple(out)

    start = tuple(jnp.zeros((n, lanes), jnp.float32) for _ in range(streams))
    states = lax.fori_loop(0, length // ROWS, chunk, start)
    for s in range(streams):
        end_ref[s] = states[s]


def run_kernel(df_ref, x_ref, b_ref, c_ref, rate_ref, first_ref, y_ref):
    streams, length, lanes = df_ref.shape
    n = rate_ref.shape[0]
    rate = rate_ref[...]

    def chunk(i, states):
        base = pl.multiple_of(i * ROWS, ROWS)
        out = []
        for s in range(streams):
            state = states[s]
            d = df_ref[s, pl.ds(base, ROWS), :]
            x = x_ref[s, pl.ds(base, ROWS), :]
            rows = []
            for j in range(ROWS):
                at = pl.ds(pl.multiple_of((base + j) * n, n), n)
                fade = jnp.exp2(d[j : j + 1] * rate)
                state = fade * state + x[j : j + 1] * wide(b_ref[s, at, :], lanes)
                rows.append(jnp.sum(state * wide(c_ref[s, at, :], lanes), axis=0, keepdims=True))
            y_ref[s, pl.ds(base, ROWS), :] = jnp.concatenate(rows, axis=0)
            out.append(state)
        return tuple(out)

    lax.fori_loop(0, length // ROWS, chunk, tuple(first_ref[s] for s in range(streams)))


def adjoint_summary_kernel(df_ref, g_ref, c_ref, rate_ref, end_ref):
    streams, length, lanes = df_ref.shape
    n = rate_ref.shape[0]
    rate = rate_ref[...]
    chunks = length // ROWS

    def chunk(i, carry):
        base = pl.multiple_of((chunks - 1 - i) * ROWS, ROWS)
        out = []
        for s in range(streams):
            carried = carry[s]
            d = df_ref[s, pl.ds(base, ROWS), :]
            g = g_ref[s, pl.ds(base, ROWS), :]
            for j in reversed(range(ROWS)):
                at = pl.ds(pl.multiple_of((base + j) * n, n), n)
                fade = jnp.exp2(d[j : j + 1] * rate)
                carried = fade * (g[j : j + 1] * wide(c_ref[s, at, :], lanes) + carried)
            out.append(carried)
        return tuple(out)

    start = tuple(jnp.zeros((n, lanes), jnp.float32) for _ in range(streams))
    last = lax.fori_loop(0, chunks, chunk, start)
    for s in range(streams):
        end_ref[s] = last[s]


def adjoint_run_kernel(
    df_ref, d_ref, v_ref, g_ref, b_ref, c_ref, rate_ref, first_ref, last_ref,
    dstep_ref, dvalue_ref, db_ref, dc_ref, decay_ref, path_ref, fade_ref,
):
    streams, length, lanes = df_ref.shape
    n = rate_ref.shape[0]
    rate = rate_ref[...]
    chunks = length // ROWS

    @pl.when(pl.program_id(0) == 0)
    def _():
        db_ref[...] = jnp.zeros_like(db_ref)
        dc_ref[...] = jnp.zeros_like(dc_ref)

    def ahead(i, states):
        base = pl.multiple_of(i * ROWS, ROWS)
        out = []
        for s in range(streams):
            state = states[s]
            d = df_ref[s, pl.ds(base, ROWS), :]
            x = d_ref[s, pl.ds(base, ROWS), :] * v_ref[s, pl.ds(base, ROWS), :]
            for j in range(ROWS):
                at = pl.ds(pl.multiple_of((base + j) * n, n), n)
                path_ref[s, at, :] = state
                fade = jnp.exp2(d[j : j + 1] * rate)
                fade_ref[s, at, :] = fade
                state = fade * state + x[j : j + 1] * wide(b_ref[s, at, :], lanes)
            out.append(state)
        return tuple(out)

    ends = lax.fori_loop(0, chunks, ahead, tuple(first_ref[s] for s in range(streams)))

    def fold(tile):
        total = tile[:, :128]
        for k in range(1, lanes // 128):
            total = total + tile[:, k * 128 : (k + 1) * 128]
        return total

    def back(i, carry):
        base = pl.multiple_of((chunks - 1 - i) * ROWS, ROWS)
        out = []
        decay = carry[-1]
        for s in range(streams):
            state, carried = carry[s]
            d = d_ref[s, pl.ds(base, ROWS), :]
            v = v_ref[s, pl.ds(base, ROWS), :]
            g = g_ref[s, pl.ds(base, ROWS), :]
            x = d * v
            weights, touches = [None] * ROWS, [None] * ROWS
            for j in reversed(range(ROWS)):
                at = pl.ds(pl.multiple_of((base + j) * n, n), n)
                gj = g[j : j + 1]
                adjoint = gj * wide(c_ref[s, at, :], lanes) + carried
                dc_ref[s, at, :] += fold(state * gj)
                db_ref[s, at, :] += fold(adjoint * x[j : j + 1])
                weights[j] = jnp.sum(adjoint * wide(b_ref[s, at, :], lanes), axis=0, keepdims=True)
                carried = adjoint * fade_ref[s, at, :]
                state = path_ref[s, at, :]
                touch = carried * state
                touches[j] = jnp.sum(touch * rate, axis=0, keepdims=True)
                decay = decay + touch * d[j : j + 1]
            weighted = jnp.concatenate(weights, axis=0)
            dstep_ref[s, pl.ds(base, ROWS), :] = weighted * v + jnp.concatenate(touches, axis=0) * LN2
            dvalue_ref[s, pl.ds(base, ROWS), :] = weighted * d
            out.append((state, carried))
        return tuple(out) + (decay,)

    start = tuple((ends[s], last_ref[s]) for s in range(streams))
    done = lax.fori_loop(0, chunks, back, start + (jnp.zeros((n, lanes), jnp.float32),))
    decay_ref[...] = done[-1]


def scan_call(kernel, operands, kinds, out_kinds, scratch=(), flops=0, block=None):
    streams, length, channels = operands[0].shape
    n = next(o for o, k in zip(operands, kinds) if k == "r").shape[0]
    lanes = block or pieces(channels)
    specs = {
        "e": pl.BlockSpec((streams, length, lanes), lambda i: (0, 0, i)),
        "n": pl.BlockSpec((streams, length * n, 128), lambda i: (0, 0, 0)),
        "r": pl.BlockSpec((n, lanes), lambda i: (0, i)),
        "h": pl.BlockSpec((streams, n, lanes), lambda i: (0, 0, i)),
    }
    shapes = {
        "e": (streams, length, channels),
        "n": (streams, length * n, 128),
        "r": (n, channels),
        "h": (streams, n, channels),
    }
    size = streams * length * n * channels
    return pl.pallas_call(
        kernel,
        grid=(channels // lanes,),
        in_specs=[specs[k] for k in kinds],
        out_specs=[specs[k] for k in out_kinds] if len(out_kinds) > 1 else specs[out_kinds],
        out_shape=[jax.ShapeDtypeStruct(shapes[k], jnp.float32) for k in out_kinds]
        if len(out_kinds) > 1
        else jax.ShapeDtypeStruct(shapes[out_kinds], jnp.float32),
        scratch_shapes=[pltpu.VMEM((streams, length * n, lanes), jnp.float32) for _ in scratch],
        compiler_params=params(),
        cost_estimate=spans(flops),
    )(*operands)


def summarize(df, x, b, rate, block=None):
    return scan_call(summary_kernel, (df, x, b, rate), "eenr", "h", flops=6, block=block)

def run_states(df, x, b, c, rate, first, block=None):
    return scan_call(run_kernel, (df, x, b, c, rate, first), "eennrh", "e", flops=12, block=block)

def adjoint_summary(df, g, c, rate, block=None):
    return scan_call(adjoint_summary_kernel, (df, g, c, rate), "eenr", "h", flops=6, block=block)

def adjoint_run(df, d, v, g, b, c, rate, first, last, block=None):
    return scan_call(adjoint_run_kernel, (df, d, v, g, b, c, rate, first, last), "eeeennrhh", "eennr", scratch="ab", flops=30, block=block)


def spans(us):
    return pl.CostEstimate(flops=int(us * 1.1e9), bytes_accessed=int(us * 3.0e6), transcendentals=0)


def stack_tokens(target, own_ref, more_refs):
    own = own_ref.shape[0]
    target[:own, :] = own_ref[...].astype(target.dtype)
    at = own
    for ref in more_refs:
        rows = ref.shape[0]
        target[at : at + rows, :] = ref[...].astype(target.dtype)
        at += rows


def dot(left, right):
    return jnp.dot(left, right, preferred_element_type=jnp.float32)


def dot_back(left, right):
    return lax.dot_general(left, right, (((1,), (1,)), ((), ())), preferred_element_type=jnp.float32)


def ffn_kernel(stride, more, *refs):
    hid_own, hid_more = refs[0], refs[1 : 1 + more]
    grad_own, grad_more = refs[1 + more], refs[2 + more : 2 + 2 * more]
    wg, wu, wd, dg_own, du_own, act_own = refs[2 + 2 * more : 8 + 2 * more]
    out_gate, out_up, out_down = refs[8 + 2 * more : 11 + 2 * more]
    hid, grad, hid_cut, grad_cut, dg, du, act = refs[11 + 2 * more :]
    own = hid_own.shape[0]
    cut = hid_cut.shape[0]

    @pl.when(pl.program_id(0) == 0)
    def _():
        stack_tokens(hid, hid_own, hid_more)
        stack_tokens(grad, grad_own, grad_more)
        at = pl.ds(pl.multiple_of((lax.axis_index("seq") // stride) * cut, 128), cut)
        hid_cut[...] = hid[:, at].T
        grad_cut[...] = grad[:, at].T

    dg[:own, :] = dg_own[...]
    du[:own, :] = du_own[...]
    act[:own, :] = act_own[...]

    def turn(i, _):
        rows = pl.ds(pl.multiple_of(i * own, own), own)
        gate = dot(hid[rows, :], wg[...])
        up = dot(hid[rows, :], wu[...])
        d_act = dot_back(grad[rows, :], wd[...])
        sig = 1.0 / (1.0 + jnp.exp(-gate))
        silu = gate * sig
        dg[rows, :] = (d_act * up * (sig + silu * (1.0 - sig))).astype(dg.dtype)
        du[rows, :] = (d_act * silu).astype(du.dtype)
        act[rows, :] = (silu * up).astype(act.dtype)
        return 0

    lax.fori_loop(1, hid.shape[0] // own, turn, 0)
    out_gate[...] = dot(hid_cut[...], dg[...])
    out_up[...] = dot(hid_cut[...], du[...])
    out_down[...] = dot(grad_cut[...], act[...])


def whole(shape):
    return pl.BlockSpec(shape, lambda i: (0,) * len(shape), pipeline_mode=pl.Buffered(1))


def ffn_grads(stride, hid_own, hid_more, grad_own, grad_more, w_gate, w_up, w_down, d_gate, d_up, act):
    own, width = hid_own.shape
    units = w_gate.shape[1]
    cut = width // SIDE
    block = next(b for b in (256, 128) if units % b == 0)
    tokens = own + sum(part.shape[0] for part in hid_more)
    low = jnp.bfloat16
    column = lambda rows: pl.BlockSpec((rows, block), lambda i: (0, i))
    return pl.pallas_call(
        functools.partial(ffn_kernel, stride, len(hid_more)),
        grid=(units // block,),
        in_specs=[whole(a.shape) for a in (hid_own, *hid_more, grad_own, *grad_more)]
        + [column(width), column(width), pl.BlockSpec((block, width), lambda i: (i, 0))]
        + [column(own)] * 3,
        out_specs=[column(cut)] * 3,
        out_shape=[jax.ShapeDtypeStruct((cut, units), jnp.float32)] * 3,
        scratch_shapes=[pltpu.VMEM((tokens, width), low)] * 2
        + [pltpu.VMEM((cut, tokens), low)] * 2
        + [pltpu.VMEM((tokens, block), low)] * 3,
        compiler_params=params(56),
        cost_estimate=spans(24),
    )(hid_own, *hid_more, grad_own, *grad_more, w_gate, w_up, w_down, d_gate, d_up, act)


def mixer_kernel(more, sides, *refs):
    at = iter(range(len(refs)))
    take = lambda count: [refs[next(at)] for _ in range(count)]
    (norm_own,), norm_more = take(1), take(more)
    (mix_own,), mix_more = take(1), take(more)
    (y_own,), y_side = take(1), take(sides)
    wo, wm = take(2)
    out_gate, out_mix, norm_turned = take(3)
    norm, mix, mixed, d_out = take(4)
    own = norm_own.shape[0]
    half = own // 2

    @pl.when(pl.program_id(0) == 0)
    def _():
        stack_tokens(norm, norm_own, norm_more)
        stack_tokens(mix, mix_own, mix_more)

        def finish(rows, y):
            outgate = dot(norm[rows, :], wo[...])
            d_mixed = dot_back(mix[rows, :], wm[...])
            sig = 1.0 / (1.0 + jnp.exp(-outgate))
            silu = outgate * sig
            mixed[rows, :] = (y * silu).astype(mixed.dtype)
            d_out[rows, :] = (d_mixed * y * (sig + silu * (1.0 - sig))).astype(d_out.dtype)

        finish(slice(0, own), y_own[...])
        for k in range(sides):
            for s in range(2):
                start = own + (s * sides + k) * half
                finish(slice(start, start + half), y_side[k][s])

    rows = norm_turned.shape[0]
    span = pl.ds(pl.multiple_of(pl.program_id(0) * rows, rows), rows)
    turned = norm[:, span].T
    norm_turned[...] = turned
    out_gate[...] = dot(turned, d_out[...])
    out_mix[...] = dot(mix[:, span].T, mixed[...])


def mixer_grads(norm_own, norm_more, mix_own, mix_more, y_own, y_side, w_out, w_mix):
    own, width = norm_own.shape
    cut = w_out.shape[1]
    block = next(b for b in (256, 128) if width % b == 0)
    tokens = own + sum(part.shape[0] for part in norm_more)
    low = jnp.bfloat16
    row = lambda columns: pl.BlockSpec((block, columns), lambda i: (i, 0))
    operands = (norm_own, *norm_more, mix_own, *mix_more, y_own, *y_side, w_out, w_mix)
    return pl.pallas_call(
        functools.partial(mixer_kernel, len(norm_more), len(y_side)),
        grid=(width // block,),
        in_specs=[whole(a.shape) for a in operands],
        out_specs=[row(cut), row(cut), row(tokens)],
        out_shape=[
            jax.ShapeDtypeStruct((width, cut), jnp.float32),
            jax.ShapeDtypeStruct((width, cut), jnp.float32),
            jax.ShapeDtypeStruct((width, tokens), low),
        ],
        scratch_shapes=[pltpu.VMEM((tokens, width), low)] * 2 + [pltpu.VMEM((tokens, cut), low)] * 2,
        compiler_params=params(56),
        cost_estimate=spans(12),
    )(*operands)


def inner_kernel(sides, *refs):
    turned, d_own, d_side, out, d_all = refs[0], refs[1], refs[2 : 2 + sides], refs[2 + sides], refs[3 + sides]
    own = d_own.shape[0]
    half = own // 2

    @pl.when(pl.program_id(0) == 0)
    def _():
        d_all[:own, :] = d_own[...]
        for k in range(sides):
            for s in range(2):
                start = own + (s * sides + k) * half
                d_all[start : start + half, :] = d_side[k][s].astype(d_all.dtype)

    out[...] = dot(turned[...], d_all[...])


def inner_grad(turned, d_own, d_side):
    width, tokens = turned.shape
    cut = d_own.shape[1]
    block = next(b for b in (512, 256, 128) if width % b == 0)
    return pl.pallas_call(
        functools.partial(inner_kernel, len(d_side)),
        grid=(width // block,),
        in_specs=[pl.BlockSpec((block, tokens), lambda i: (i, 0))] + [whole(a.shape) for a in (d_own, *d_side)],
        out_specs=pl.BlockSpec((block, cut), lambda i: (i, 0)),
        out_shape=jax.ShapeDtypeStruct((width, cut), jnp.float32),
        scratch_shapes=[pltpu.VMEM((tokens, cut), jnp.bfloat16)],
        compiler_params=params(56),
        cost_estimate=spans(4),
    )(turned, d_own, *d_side)


SIDE = 4
MESH = pl.DeviceIdType.MESH


def chain_kernel(
    reverse, groups, ends_ref, total_ref, rate_ref, out_ref,
    own, side, mine, line, back, done, side_send, side_recv, line_send, line_recv, back_send, back_recv,
):
    here, head = lax.axis_index("seq"), lax.axis_index("head")
    place, group = lax.rem(here, SIDE), here // SIDE
    streams, n, channels = ends_ref.shape
    width = channels // SIDE
    rows = streams * n
    base = here - place
    member = [base + (place ^ k) for k in range(SIDE)]
    other = [lax.rem(group + k, groups) * SIDE + place for k in range(groups)]

    barrier = pltpu.get_barrier_semaphore()
    for device in member[1:] + other[1:]:
        pl.semaphore_signal(barrier, inc=1, device_id=(device, head), device_id_type=MESH)
    for q in range(SIDE):
        cols = slice(q * width, (q + 1) * width)
        own[q, :rows, :] = ends_ref[:, :, cols].reshape(rows, width)
        own[q, rows : rows + streams, :] = total_ref[:, cols]
        own[q, rows + streams :, :] = jnp.zeros((own.shape[1] - rows - streams, width), jnp.float32)
    rate = rate_ref[:, pl.ds(pl.multiple_of(place * width, 128), width)]
    pl.semaphore_wait(barrier, SIDE - 1 + groups - 1)

    def copy(source, target, send, recv, device):
        return pltpu.make_async_remote_copy(
            src_ref=source, dst_ref=target, send_sem=send, recv_sem=recv,
            device_id=(device, head), device_id_type=MESH,
        )

    sides = [copy(own.at[place ^ k], side.at[k], side_send.at[k], side_recv.at[k], member[k]) for k in range(1, SIDE)]
    for c in sides:
        c.start()
    side[0] = own[place]
    for c in sides:
        c.wait_recv()

    def through(steps):
        return jnp.concatenate([jnp.exp2(steps[s : s + 1] * rate) for s in range(streams)], axis=0)

    state, steps = jnp.zeros((rows, width), jnp.float32), jnp.zeros((streams, width), jnp.float32)
    before, passed = [None] * SIDE, [None] * SIDE
    for j in reversed(range(SIDE)) if reverse else range(SIDE):
        block = side[place ^ j]
        before[j], passed[j] = state, steps
        step = block[rows : rows + streams]
        state = through(step) * state + block[:rows]
        steps = steps + step
    mine[:rows, :] = state
    mine[rows : rows + streams, :] = steps
    mine[rows + streams :, :] = jnp.zeros((mine.shape[0] - rows - streams, width), jnp.float32)
    lines = [copy(mine, line.at[k], line_send.at[k], line_recv.at[k], other[k]) for k in range(1, groups)]
    for c in lines:
        c.start()
    for c in lines:
        c.wait_recv()
    entering = jnp.zeros((rows, width), jnp.float32)
    for k in range(1, groups) if reverse else range(groups - 1, 0, -1):
        counts = (k > group) if reverse else (k <= group)
        block = line[k]
        new = through(block[rows : rows + streams]) * entering + block[:rows]
        entering = jnp.where(counts, new, entering)
    for j in range(SIDE):
        back[j] = through(passed[j]) * entering + before[j]
    backs = [copy(back.at[place ^ k], done.at[place], back_send.at[k], back_recv.at[k], member[k]) for k in range(1, SIDE)]
    for c in backs:
        c.start()
    done[place] = back[place]
    for c in backs:
        c.wait_recv()
    for q in range(SIDE):
        out_ref[:, :, q * width : (q + 1) * width] = done[q].reshape(streams, n, width)
    for c in sides + lines + backs:
        c.wait_send()


def chained(ends, total, rate, reverse):
    streams, n, channels = ends.shape
    groups = lax.axis_size("seq") // SIDE
    width = channels // SIDE
    rows = streams * n
    tall = rows + 8 * (-(-streams // 8))
    f32 = jnp.float32
    return pl.pallas_call(
        functools.partial(chain_kernel, reverse, groups),
        out_shape=jax.ShapeDtypeStruct(ends.shape, f32),
        in_specs=[pl.BlockSpec(memory_space=pltpu.VMEM)] * 3,
        out_specs=pl.BlockSpec(memory_space=pltpu.VMEM),
        scratch_shapes=[
            pltpu.VMEM((SIDE, tall, width), f32),
            pltpu.VMEM((SIDE, tall, width), f32),
            pltpu.VMEM((tall, width), f32),
            pltpu.VMEM((groups, tall, width), f32),
            pltpu.VMEM((SIDE, rows, width), f32),
            pltpu.VMEM((SIDE, rows, width), f32),
        ]
        + [pltpu.SemaphoreType.DMA((m,)) for m in (SIDE, SIDE, groups, groups, SIDE, SIDE)],
        compiler_params=pltpu.CompilerParams(
            collective_id=1 if reverse else 0, has_side_effects=True, vmem_limit_bytes=32 * 1024 * 1024
        ),
    )(ends, total, rate)


epsilon = 1e-06
CUT = 1e6


def links(step, wrap=False, axis="seq"):
    n = lax.axis_size(axis)
    return [(i, (i + step) % n) for i in range(n) if wrap or 0 <= i + step < n]


def swaps(bit, axis="seq"):
    return [(i, i ^ bit) for i in range(lax.axis_size(axis))]


def send(block, route, axis="seq"):
    return lax.ppermute(block, axis, route)


def head_sum(part):
    return part + send(part, swaps(1, "head"), "head")


def own_stream(block):
    return lax.dynamic_index_in_dim(block, lax.axis_index("head"), 0, keepdims=False)


def unswap(parts, place):
    odd, far = (place & 1) == 1, (place & 2) == 2
    p = list(parts)
    p = [jnp.where(odd, p[k ^ 1], p[k]) for k in range(4)]
    return [jnp.where(far, p[k ^ 2], p[k]) for k in range(4)]


def part_of(block, index, size, axis):
    return lax.dynamic_slice_in_dim(block, index * size, size, axis)


def exchange(block, place):
    size = block.shape[-1] // SIDE
    first = lax.axis_index("head")
    turned = jnp.stack([lax.dynamic_index_in_dim(block, first, 0, keepdims=False), lax.dynamic_index_in_dim(block, 1 - first, 0, keepdims=False)])
    away = [part_of(turned, place ^ k, size, 2).astype(jnp.float32) for k in range(1, SIDE)]
    return part_of(block, place, size, 2).reshape(-1, size), [send(away[k - 1], swaps(k)) for k in range(1, SIDE)]


def other_core(parts):
    return [send(part, swaps(1, "head"), "head") for part in parts]


def after(block, *earlier):
    return lax.optimization_barrier((block,) + earlier)[0]


def scatter_line(blocks, stride):
    n = lax.axis_size("seq")
    z = lax.axis_index("seq") // stride
    take = lambda at: lax.dynamic_index_in_dim(blocks, jnp.clip(at, 0, SIDE - 1), 0, keepdims=False)
    up = down = None
    for turn in range(SIDE - 1):
        one, two = take(SIDE - 1 - turn + z), take(z + turn - SIDE + 1)
        if turn:
            one, two = one + up, two + down
        up = send(one, [(i, i + stride) for i in range(min((turn + 1) * stride, n - stride))])
        down = send(two, [(i, i - stride) for i in range(max(n - (turn + 1) * stride, stride), n)])
    return take(z) + (up + down)


def scatter_bits(blocks, bits):
    here = lax.axis_index("seq")
    order = sorted(bits)
    shape = blocks.shape[1:]
    left = list(order)
    blocks = blocks.reshape((2,) * len(order) + shape)
    for bit in bits:
        axis = len(left) - 1 - left.index(bit)
        mine = (here // bit) % 2
        keep = lax.dynamic_index_in_dim(blocks, mine, axis, keepdims=False)
        away = lax.dynamic_index_in_dim(blocks, 1 - mine, axis, keepdims=False)
        blocks = keep + send(away, swaps(bit))
        left.remove(bit)
    return blocks


def bits_between(low, high):
    out = []
    while low < high:
        out.append(low)
        low *= 2
    return out


def matmul(left, right):
    return jnp.dot(left, right, preferred_element_type=jnp.float32)


def matmul_back(left, right):
    return lax.dot_general(
        left, right, (((left.ndim - 1,), (1,)), ((), ())), preferred_element_type=jnp.float32
    )


def weight_outer(left, right):
    axes = tuple(range(left.ndim - 1))
    return lax.dot_general(left, right, ((axes, axes), ((), ())), preferred_element_type=jnp.float32)


def norm_forward(v, gain):
    scale = lax.rsqrt(jnp.mean(v * v, axis=-1, keepdims=True) + epsilon)
    return (v * scale * gain, scale)


def norm_backward(v, scale, gain, upstream):
    weighted = upstream * gain
    d_input = scale * weighted - v * scale * scale * scale * jnp.mean(
        weighted * v, axis=-1, keepdims=True
    )
    d_gain = jnp.sum(upstream * v * scale, axis=(0, 1))
    return (d_input, d_gain)


def silu_slope(v):
    sig = jax.nn.sigmoid(v)
    return sig + v * sig * (1.0 - sig)


def across(small):
    streams, length, n = small.shape
    return jnp.broadcast_to(small.reshape(streams, length * n, 1), (streams, length * n, 128))


def along(wide_sum, n):
    streams, rows, _ = wide_sum.shape
    return jnp.sum(wide_sum, axis=-1).reshape(streams, rows // n, n)


def body(
    tokens, doc_ids, out_grad, norm_mix, w_inner, w_outgate, conv_taps, conv_bias, w_select, select_gain,
    w_step, step_bias, log_decay, skip_gain, w_mixout, norm_ffn, w_gate, w_up, w_down,
):
    streams, length, width = tokens.shape
    channels = w_inner.shape[1]
    taps = conv_taps.shape[0]
    rank = w_step.shape[0]
    states = log_decay.shape[1]
    lead = taps - 1
    count = lax.axis_size("seq")
    stride = count // SIDE
    here = lax.axis_index("seq")
    z, place = here // stride, here % SIDE
    low = jnp.bfloat16

    grad_in = out_grad.astype(jnp.float32)
    source = tokens.astype(jnp.float32)
    mine_grad = own_stream(out_grad).astype(jnp.float32)
    line_grad = {k: send(mine_grad, links(k * stride, True)) for k in (1, 3)}
    normed, scale_mix = norm_forward(source, norm_mix)
    normed_low = normed.astype(low)
    mine_normed = own_stream(normed)
    side_normed = [send(mine_normed, swaps(k)) for k in range(1, SIDE)]
    side_normed = side_normed + other_core(side_normed)
    inner = matmul(normed_low, w_inner)
    outgate = matmul(normed_low, w_outgate)
    rim_ids = (doc_ids[:, length - lead :] + 1).astype(jnp.float32)
    rim_val = send(inner[:, length - lead :], links(1))
    rim_got = send(rim_ids, links(1))
    ext_val = jnp.concatenate([rim_val, inner], axis=1)
    ext_ids = jnp.concatenate([rim_got.astype(jnp.int32) - 1, doc_ids], axis=1)
    masks = [
        (ext_ids[:, k : k + length] == doc_ids).astype(jnp.float32)[:, :, None] for k in range(taps)
    ]
    value_pre = jnp.zeros_like(inner) + conv_bias
    for k in range(taps):
        value_pre = value_pre + conv_taps[k] * ext_val[:, k : k + length] * masks[k]
    value = jax.nn.silu(value_pre)
    value_low = value.astype(low)
    select = head_sum(matmul(value_low, w_select))
    raw_step = select[..., :rank]
    raw_b = select[..., rank : rank + states]
    raw_c = select[..., rank + states :]
    step_n, step_scale = norm_forward(raw_step, select_gain[:rank])
    bsel, b_scale = norm_forward(raw_b, select_gain[rank : rank + states])
    csel, c_scale = norm_forward(raw_c, select_gain[rank + states :])
    step_low = step_n.astype(low)
    step_pre = matmul(step_low, w_step) + step_bias
    step = jax.nn.softplus(step_pre)
    keep = doc_ids == ext_ids[:, lead - 1 : lead - 1 + length]
    fall = jnp.where(keep[:, :, None], step, CUT)
    gain = step * value
    decay_rate = -jnp.exp(log_decay).T
    rate = decay_rate * LOG2E
    b_wide, c_wide = across(bsel), across(csel)
    ends = summarize(fall, gain, b_wide, rate)
    total = jnp.sum(fall, axis=1)
    first = chained(ends, total, rate, False)
    line_grad[2] = send(after(mine_grad, first), links(2 * stride, True))
    line_grad = [line_grad[k] for k in range(1, SIDE)]
    line_grad = line_grad + other_core(line_grad)
    outs = run_states(fall, gain, b_wide, c_wide, rate, first)
    y = outs + skip_gain * value
    own_y, side_y = exchange(y, place)
    gate_z = jax.nn.silu(outgate)
    mixed = y * gate_z
    mixed_low = mixed.astype(low)
    mix = head_sum(matmul(mixed_low, w_mixout))
    resid = source + mix
    hidden, scale_ffn = norm_forward(resid, norm_ffn)
    hidden_low = hidden.astype(low)
    mine_hidden = own_stream(hidden)
    line_hidden = [send(mine_hidden, links(k * stride, True)) for k in (1, 3, 2)]
    line_hidden = [line_hidden[k] for k in (0, 2, 1)]
    line_hidden = line_hidden + other_core(line_hidden)
    gate = matmul(hidden_low, w_gate)
    up = matmul(hidden_low, w_up)
    act_low = (jax.nn.silu(gate) * up).astype(low)
    ffn = head_sum(matmul(act_low, w_down))
    output = (resid + ffn).astype(low)
    d_act = matmul_back(out_grad, w_down)
    d_gate = (d_act * up * silu_slope(gate)).astype(low)
    d_up = (d_act * jax.nn.silu(gate)).astype(low)
    d_hidden = head_sum(matmul_back(d_gate, w_gate) + matmul_back(d_up, w_up))
    d_resid_norm, grad_norm_ffn = norm_backward(resid, scale_ffn, norm_ffn, d_hidden)
    d_resid = grad_in + d_resid_norm
    d_mix = d_resid.astype(low)
    mine_d_mix = own_stream(d_resid)
    side_d_mix = [send(mine_d_mix, swaps(k)) for k in range(1, SIDE)]
    side_d_mix = side_d_mix + other_core(side_d_mix)
    d_mixed = matmul_back(d_mix, w_mixout)
    d_y = d_mixed * gate_z
    d_outgate = (d_mixed * y * silu_slope(outgate)).astype(low)
    grad_skip_gain = jnp.sum(d_y * value, axis=(0, 1))
    leaving = adjoint_summary(fall, d_y, c_wide, rate)
    last = chained(leaving, total, rate, True)
    d_step, d_scan, db_wide, dc_wide, decay_sum = adjoint_run(
        fall, step, value, d_y, b_wide, c_wide, rate, first, last
    )

    flat = lambda block: block.reshape(-1, block.shape[-1])
    whole_gate, whole_up, whole_down = ffn_grads(
        stride, flat(hidden_low), line_hidden, flat(out_grad), line_grad, w_gate, w_up, w_down,
        flat(d_gate), flat(d_up), flat(act_low),
    )
    side_bits = bits_between(1, stride)
    orders = (side_bits, side_bits[len(side_bits) // 2 :] + side_bits[: len(side_bits) // 2])

    def sum_side(whole):
        whole = whole.reshape(stride, width // count, -1)
        half = whole.shape[2] // 2
        return jnp.concatenate(
            [scatter_bits(whole[..., :half], orders[0]), scatter_bits(whole[..., half:], orders[1])], axis=-1
        )

    grad_w_gate = sum_side(whole_gate)
    grad_w_up = sum_side(whole_up)
    grad_w_down = sum_side(whole_down).T

    size = channels // SIDE
    whole_outgate, whole_mixout, turned = mixer_grads(
        flat(normed_low), side_normed, flat(d_mix), side_d_mix, own_y, side_y,
        part_of(w_outgate, place, size, 1), part_of(w_mixout, place, size, 0),
    )
    groups = [list(range(k, count, SIDE)) for k in range(SIDE)]

    def sum_line(whole):
        own = lax.psum_scatter(whole, "seq", scatter_dimension=0, axis_index_groups=groups, tiled=True)
        own = own.reshape(SIDE, width // count, -1)
        sent = unswap([own[k] for k in range(SIDE)], place)
        got = [sent[0]] + [send(sent[k], swaps(k)) for k in range(1, SIDE)]
        return jnp.concatenate(unswap(got, place), axis=-1)

    grad_w_mixout = sum_line(whole_mixout).T
    grad_w_outgate = sum_line(whole_outgate)

    d_value = d_y * skip_gain + d_scan
    d_step_pre = (d_step * jax.nn.sigmoid(step_pre)).astype(low)
    grad_step_bias = jnp.sum(d_step_pre, axis=(0, 1), dtype=jnp.float32)
    grad_w_step = weight_outer(step_low, d_step_pre)
    d_small = head_sum(
        jnp.concatenate(
            [matmul_back(d_step_pre, w_step), along(db_wide, states), along(dc_wide, states)], axis=-1
        )
    )
    d_raw_step, gain_step = norm_backward(
        raw_step, step_scale, select_gain[:rank], d_small[..., :rank]
    )
    d_raw_b, gain_b = norm_backward(
        raw_b, b_scale, select_gain[rank : rank + states], d_small[..., rank : rank + states]
    )
    d_raw_c, gain_c = norm_backward(
        raw_c, c_scale, select_gain[rank + states :], d_small[..., rank + states :]
    )
    grad_select_gain = jnp.concatenate([gain_step, gain_b, gain_c])
    d_select = jnp.concatenate([d_raw_step, d_raw_b, d_raw_c], axis=-1).astype(low)
    grad_w_select = weight_outer(d_select, value_low)
    d_value = d_value + matmul_back(d_select, w_select)
    d_value_pre = d_value * silu_slope(value_pre)
    grad_conv_bias = jnp.sum(d_value_pre, axis=(0, 1))
    tap_grads = []
    d_ext = jnp.zeros_like(ext_val)
    for k in range(taps):
        masked = d_value_pre * masks[k]
        tap_grads.append(jnp.sum(masked * ext_val[:, k : k + length], axis=(0, 1)))
        d_ext = d_ext + jnp.pad(masked * conv_taps[k], ((0, 0), (k, lead - k), (0, 0)))
    grad_conv_taps = jnp.stack(tap_grads)
    rim_grad = send(d_ext[:, :lead], links(-1))
    d_inner = (d_ext[:, lead:] + jnp.pad(rim_grad, ((0, 0), (length - lead, 0), (0, 0)))).astype(low)
    own_d_inner, side_d_inner = exchange(d_inner, place)
    grad_w_inner = sum_line(inner_grad(turned, own_d_inner, side_d_inner))
    d_normed = head_sum(matmul_back(d_inner, w_inner) + matmul_back(d_outgate, w_outgate))
    d_source, grad_norm_mix = norm_backward(source, scale_mix, norm_mix, d_normed)
    tokens_grad = d_resid + d_source

    pad = lambda v: jnp.pad(v, (0, channels - v.shape[0]))
    selects = grad_select_gain.reshape(count, -1)
    tall = jnp.concatenate(
        [
            grad_w_step,
            decay_sum * decay_rate,
            grad_conv_taps,
            jnp.stack([grad_conv_bias, grad_step_bias, grad_skip_gain, grad_norm_mix, grad_norm_ffn]),
        ]
    )
    tall = jnp.swapaxes(tall.reshape(tall.shape[0], count, -1), 0, 1)
    selects = jnp.pad(selects, ((0, 0), (0, tall.shape[2] - selects.shape[1])))
    tall = jnp.concatenate([tall, selects[:, None]], axis=1)
    broad = grad_w_select.reshape(count, -1, channels)
    every = bits_between(1, count)
    turned = every[1:2] + every[:1] + every[2:]
    tall = scatter_bits(tall, every)
    broad = scatter_bits(broad, turned)
    at = rank + states
    return (
        output,
        tokens_grad,
        tall[at + taps + 3],
        grad_w_inner,
        grad_w_outgate,
        tall[at : at + taps],
        tall[at + taps],
        broad.T,
        tall[at + taps + 5, : grad_select_gain.shape[0] // count],
        tall[:rank],
        tall[at + taps + 1],
        tall[rank:at].T,
        tall[at + taps + 2],
        grad_w_mixout,
        tall[at + taps + 4],
        grad_w_gate,
        grad_w_up,
        grad_w_down,
    )


def solution(mesh):
    in_specs = (
        P(None, "seq", None),
        P(None, "seq"),
        P(None, "seq", None),
        P(),
        P(None, "head"),
        P(None, "head"),
        P(None, "head"),
        P("head"),
        P("head", None),
        P(),
        P(None, "head"),
        P("head"),
        P("head", None),
        P("head"),
        P("head", None),
        P(),
        P(None, "head"),
        P(None, "head"),
        P("head", None),
    )
    out_specs = (
        P(None, "seq", None),
        P(None, "seq", None),
        P("seq"),
        P("seq", "head"),
        P("seq", "head"),
        P(None, ("head", "seq")),
        P(("head", "seq")),
        P("head", "seq"),
        P("seq"),
        P(None, ("head", "seq")),
        P(("head", "seq")),
        P(("head", "seq"), None),
        P(("head", "seq")),
        P("head", "seq"),
        P("seq"),
        P("seq", "head"),
        P("seq", "head"),
        P("head", "seq"),
    )
    return jax.shard_map(body, mesh=mesh, in_specs=in_specs, out_specs=out_specs, check_vma=False)
```

```python
import functools
import math

import jax
import jax.numpy as jnp
from jax import lax
from jax.experimental import pallas as pl
from jax.experimental.pallas import tpu as pltpu
from jax.sharding import PartitionSpec as P

LOG2E = math.log2(math.e)
LN2 = math.log(2.0)
ROWS = 8


def params(limit=48):
    return pltpu.CompilerParams(vmem_limit_bytes=limit * 1024 * 1024)


def wide(tile, lanes):
    return jnp.concatenate([tile] * (lanes // tile.shape[1]), axis=1)


def pieces(lanes):
    return next(w for w in (256, 128) if lanes % w == 0)


def spans(us):
    return pl.CostEstimate(flops=int(us * 1.1e8), bytes_accessed=int(us * 3.0e5), transcendentals=0)


def stack_tokens(target, own_ref, more_refs):
    own = own_ref.shape[0]
    target[:own, :] = own_ref[...].astype(target.dtype)
    at = own
    for ref in more_refs:
        parts = [ref[k] for k in range(ref.shape[0])] if len(ref.shape) == 3 else [ref[...]]
        for part in parts:
            target[at : at + part.shape[0], :] = part.astype(target.dtype)
            at += part.shape[0]


def dot(left, right):
    return jnp.dot(left, right, preferred_element_type=jnp.float32)


def dot_back(left, right):
    return lax.dot_general(left, right, (((1,), (1,)), ((), ())), preferred_element_type=jnp.float32)


def ffn_kernel(stride, more, *refs):
    hid_own, hid_more = refs[0], refs[1 : 1 + more]
    grad_own, grad_more = refs[1 + more], refs[2 + more : 2 + 2 * more]
    wg, wu, wd, dg_own, du_own, act_own = refs[2 + 2 * more : 8 + 2 * more]
    out_gate, out_up, out_down = refs[8 + 2 * more : 11 + 2 * more]
    hid, grad, hid_cut, grad_cut, dg, du, act = refs[11 + 2 * more :]
    own = hid_own.shape[0]
    cut = hid_cut.shape[0]

    @pl.when(pl.program_id(0) == 0)
    def _():
        stack_tokens(hid, hid_own, hid_more)
        stack_tokens(grad, grad_own, grad_more)
        at = pl.ds(pl.multiple_of((lax.axis_index("seq") // stride) * cut, 128), cut)
        hid_cut[...] = hid[:, at].T
        grad_cut[...] = grad[:, at].T

    dg[:own, :] = dg_own[...]
    du[:own, :] = du_own[...]
    act[:own, :] = act_own[...]

    def turn(i, _):
        rows = pl.ds(pl.multiple_of(i * own, own), own)
        gate = dot(hid[rows, :], wg[...])
        up = dot(hid[rows, :], wu[...])
        d_act = dot_back(grad[rows, :], wd[...])
        sig = 1.0 / (1.0 + jnp.exp(-gate))
        silu = gate * sig
        dg[rows, :] = (d_act * up * (sig + silu * (1.0 - sig))).astype(dg.dtype)
        du[rows, :] = (d_act * silu).astype(du.dtype)
        act[rows, :] = (silu * up).astype(act.dtype)
        return 0

    lax.fori_loop(1, hid.shape[0] // own, turn, 0)
    out_gate[...] = dot(hid_cut[...], dg[...])
    out_up[...] = dot(hid_cut[...], du[...])
    out_down[...] = dot(grad_cut[...], act[...])


def whole(shape):
    return pl.BlockSpec(shape, lambda i: (0,) * len(shape), pipeline_mode=pl.Buffered(1))


def ffn_grads(stride, hid_own, hid_more, grad_own, grad_more, w_gate, w_up, w_down, d_gate, d_up, act):
    own, width = hid_own.shape
    units = w_gate.shape[1]
    cut = width // SIDE
    block = next(b for b in (256, 128) if units % b == 0)
    tokens = own + sum(math.prod(part.shape[:-1]) for part in hid_more)
    low = jnp.bfloat16
    column = lambda rows: pl.BlockSpec((rows, block), lambda i: (0, i))
    return pl.pallas_call(
        functools.partial(ffn_kernel, stride, len(hid_more)),
        grid=(units // block,),
        in_specs=[whole(a.shape) for a in (hid_own, *hid_more, grad_own, *grad_more)]
        + [column(width), column(width), pl.BlockSpec((block, width), lambda i: (i, 0))]
        + [column(own)] * 3,
        out_specs=[column(cut)] * 3,
        out_shape=[jax.ShapeDtypeStruct((cut, units), jnp.float32)] * 3,
        scratch_shapes=[pltpu.VMEM((tokens, width), low)] * 2
        + [pltpu.VMEM((cut, tokens), low)] * 2
        + [pltpu.VMEM((tokens, block), low)] * 3,
        compiler_params=params(56),
        cost_estimate=spans(24),
    )(hid_own, *hid_more, grad_own, *grad_more, w_gate, w_up, w_down, d_gate, d_up, act)


def mixer_kernel(more_norm, more_mix, *refs):
    at = iter(range(len(refs)))
    take = lambda count: [refs[next(at)] for _ in range(count)]
    (norm_own,), norm_more = take(1), take(more_norm)
    (mix_own,), mix_more = take(1), take(more_mix)
    y_own, y_side = take(2)
    wo, wm = take(2)
    out_gate, out_mix, norm_turned = take(3)
    norm, mix, mixed, d_out = take(4)
    own = norm_own.shape[0]
    half = own // 2

    @pl.when(pl.program_id(0) == 0)
    def _():
        stack_tokens(norm, norm_own, norm_more)
        stack_tokens(mix, mix_own, mix_more)

        def finish(rows, y):
            outgate = dot(norm[rows, :], wo[...])
            d_mixed = dot_back(mix[rows, :], wm[...])
            sig = 1.0 / (1.0 + jnp.exp(-outgate))
            silu = outgate * sig
            mixed[rows, :] = (y * silu).astype(mixed.dtype)
            d_out[rows, :] = (d_mixed * y * (sig + silu * (1.0 - sig))).astype(d_out.dtype)

        finish(slice(0, own), y_own[...])
        sides = y_side.shape[0]
        head = lax.axis_index("head")
        for k in range(sides):
            for s in range(2):
                start = own + (s * sides + k) * half
                finish(slice(start, start + half), y_side[k, head if s == 0 else 1 - head])

    rows = norm_turned.shape[0]
    span = pl.ds(pl.multiple_of(pl.program_id(0) * rows, rows), rows)
    turned = norm[:, span].T
    norm_turned[...] = turned
    out_gate[...] = dot(turned, d_out[...])
    out_mix[...] = dot(mix[:, span].T, mixed[...])


def mixer_grads(norm_own, norm_more, mix_own, mix_more, y_own, y_side, w_out, w_mix):
    own, width = norm_own.shape
    cut = w_out.shape[1]
    block = next(b for b in (256, 128) if width % b == 0)
    tokens = own + sum(math.prod(part.shape[:-1]) for part in norm_more)
    low = jnp.bfloat16
    row = lambda columns: pl.BlockSpec((block, columns), lambda i: (i, 0))
    operands = (norm_own, *norm_more, mix_own, *mix_more, y_own, y_side, w_out, w_mix)
    return pl.pallas_call(
        functools.partial(mixer_kernel, len(norm_more), len(mix_more)),
        grid=(width // block,),
        in_specs=[whole(a.shape) for a in operands],
        out_specs=[row(cut), row(cut), row(tokens)],
        out_shape=[
            jax.ShapeDtypeStruct((width, cut), jnp.float32),
            jax.ShapeDtypeStruct((width, cut), jnp.float32),
            jax.ShapeDtypeStruct((width, tokens), low),
        ],
        scratch_shapes=[pltpu.VMEM((tokens, width), low)] * 2 + [pltpu.VMEM((tokens, cut), low)] * 2,
        compiler_params=params(56),
        cost_estimate=spans(12),
    )(*operands)


def inner_kernel(sides, *refs):
    turned, d_own, d_side, out, d_all = refs[0], refs[1], refs[2 : 2 + sides], refs[2 + sides], refs[3 + sides]
    own = d_own.shape[0]
    half = own // 2

    @pl.when(pl.program_id(0) == 0)
    def _():
        d_all[:own, :] = d_own[...]
        for k in range(sides):
            for s in range(2):
                start = own + (s * sides + k) * half
                d_all[start : start + half, :] = d_side[k][s].astype(d_all.dtype)

    out[...] = dot(turned[...], d_all[...])


def inner_grad(turned, d_own, d_side):
    width, tokens = turned.shape
    cut = d_own.shape[1]
    block = next(b for b in (512, 256, 128) if width % b == 0)
    return pl.pallas_call(
        functools.partial(inner_kernel, len(d_side)),
        grid=(width // block,),
        in_specs=[pl.BlockSpec((block, tokens), lambda i: (i, 0))] + [whole(a.shape) for a in (d_own, *d_side)],
        out_specs=pl.BlockSpec((block, cut), lambda i: (i, 0)),
        out_shape=jax.ShapeDtypeStruct((width, cut), jnp.float32),
        scratch_shapes=[pltpu.VMEM((tokens, cut), jnp.bfloat16)],
        compiler_params=params(56),
        cost_estimate=spans(4),
    )(turned, d_own, *d_side)


SIDE = 4
MESH = pl.DeviceIdType.MESH


def remote(source, target, sends, recvs, at, device):
    return pltpu.make_async_remote_copy(
        src_ref=source, dst_ref=target, send_sem=sends.at[at], recv_sem=recvs.at[at],
        device_id=device, device_id_type=MESH,
    )


class Place:
    def __init__(self, count):
        here = lax.axis_index("seq")
        self.head = lax.axis_index("head")
        self.stride = count // SIDE
        self.groups = count // SIDE
        self.place, self.group = lax.rem(here, SIDE), here // SIDE
        self.z = here // self.stride
        base = here - self.place
        self.member = [(base + (self.place ^ k), self.head) for k in range(SIDE)]
        self.other = [
            (lax.rem(self.group + k, self.groups) * SIDE + self.place, self.head) for k in range(self.groups)
        ]
        self.core = (here, 1 - self.head)
        self.above = (lax.rem(here + self.stride, count), self.head)
        self.below = (lax.rem(here - self.stride + count, count), self.head)

    def greet(self):
        barrier = pltpu.get_barrier_semaphore()
        devices = self.member[1:] + self.other[1:] + [self.core]
        for device in devices:
            pl.semaphore_signal(barrier, inc=1, device_id=device, device_id_type=MESH)
        pl.semaphore_wait(barrier, len(devices))


class Line:
    def __init__(self, where, mine, ring, rest, sends, recvs):
        self.where, self.mine, self.ring, self.rest, self.sends, self.recvs = where, mine, ring, rest, sends, recvs

    def copies(self, step):
        w = self.where
        up = self.mine if step == 1 else self.ring.at[SIDE - step]
        down = self.mine if step == 1 else self.ring.at[step - 2]
        return (
            remote(up, self.ring.at[SIDE - 1 - step], self.sends, self.recvs, step - 1, w.above),
            remote(down, self.ring.at[step - 1], self.sends, self.recvs, SIDE - 2 + step, w.below),
        )

    def core(self, slot):
        return remote(self.ring.at[slot], self.rest.at[slot], self.sends, self.recvs, 2 * SIDE - 2 + slot, self.where.core)

    def start(self, step):
        up, down = self.copies(step)
        z = self.where.z
        pl.when((z >= step - 1) & (z < SIDE - 1))(up.start)
        pl.when((z <= SIDE - step) & (z > 0))(down.start)

    def arrive(self, step):
        up, down = self.copies(step)
        z = self.where.z

        @pl.when(z >= step)
        def _():
            up.wait_recv()
            self.core(SIDE - 1 - step).start()

        @pl.when(z <= SIDE - 1 - step)
        def _():
            down.wait_recv()
            self.core(step - 1).start()

    def finish(self, first=1):
        z = self.where.z
        for step in range(first, SIDE):
            up, down = self.copies(step)
            pl.when((z >= step - 1) & (z < SIDE - 1))(up.wait_send)
            pl.when((z <= SIDE - step) & (z > 0))(down.wait_send)
        for slot in range(SIDE - 1):
            self.core(slot).wait()


LINE_SEMS = 3 * (SIDE - 1)


class Side:
    def __init__(self, where, mine, side, rest, sends, recvs):
        self.where, self.mine, self.side, self.rest, self.sends, self.recvs = where, mine, side, rest, sends, recvs

    def near(self):
        return [
            remote(self.mine, self.side.at[k - 1], self.sends, self.recvs, k - 1, self.where.member[k]) for k in (1, 2)
        ]

    def far(self):
        half = self.side.shape[1] // 2
        top, low = pl.ds(0, half), pl.ds(half, half)
        return [
            remote(self.side.at[1, top], self.side.at[2, top], self.sends, self.recvs, 2, self.where.member[1]),
            remote(self.side.at[0, low], self.side.at[2, low], self.sends, self.recvs, 3, self.where.member[2]),
        ]

    def core(self, slot):
        return remote(self.side.at[slot], self.rest.at[slot], self.sends, self.recvs, 4 + slot, self.where.core)

    def start(self):
        for c in self.near():
            c.start()

    def turn(self):
        for c in self.near():
            c.wait_recv()
        for c in self.far():
            c.start()
        for slot in (0, 1):
            self.core(slot).start()

    def finish(self):
        for c in self.far():
            c.wait_recv()
        self.core(2).start()
        for c in self.near() + self.far():
            c.wait_send()
        for slot in range(3):
            self.core(slot).wait()


SIDE_SEMS = 7


def chain(where, reverse, ends, total, rate_ref, out_ref, scratch, after_line, after_all):
    own, side, mine, line, back, done, sends, recvs = scratch
    streams, n, channels = ends.shape
    width = channels // SIDE
    rows = streams * n
    place, group, groups = where.place, where.group, where.groups
    for q in range(SIDE):
        cols = slice(q * width, (q + 1) * width)
        own[q, :rows, :] = ends[:, :, cols].reshape(rows, width)
        own[q, rows : rows + streams, :] = total[:, cols]
        own[q, rows + streams :, :] = jnp.zeros((own.shape[1] - rows - streams, width), jnp.float32)
    sides = [remote(own.at[place ^ k], side.at[k], sends, recvs, k, where.member[k]) for k in range(1, SIDE)]
    for c in sides:
        c.start()
    rate = rate_ref[:, pl.ds(pl.multiple_of(place * width, 128), width)]

    def through(steps):
        return jnp.concatenate([jnp.exp2(steps[s : s + 1] * rate) for s in range(streams)], axis=0)

    side[0] = own[place]
    for c in sides:
        c.wait_recv()
    state, steps = jnp.zeros((rows, width), jnp.float32), jnp.zeros((streams, width), jnp.float32)
    before, passed = [None] * SIDE, [None] * SIDE
    for j in reversed(range(SIDE)) if reverse else range(SIDE):
        block = side[place ^ j]
        before[j], passed[j] = state, steps
        step = block[rows : rows + streams]
        state = through(step) * state + block[:rows]
        steps = steps + step
    mine[:rows, :] = state
    mine[rows : rows + streams, :] = steps
    mine[rows + streams :, :] = jnp.zeros((mine.shape[0] - rows - streams, width), jnp.float32)
    lines = [remote(mine, line.at[k], sends, recvs, SIDE + k, where.other[k]) for k in range(1, groups)]
    for c in lines:
        c.start()
    after_line()
    for c in lines:
        c.wait_recv()
    entering = jnp.zeros((rows, width), jnp.float32)
    for k in range(1, groups) if reverse else range(groups - 1, 0, -1):
        counts = (k > group) if reverse else (k <= group)
        block = line[k]
        new = through(block[rows : rows + streams]) * entering + block[:rows]
        entering = jnp.where(counts, new, entering)
    for j in range(SIDE):
        back[j] = through(passed[j]) * entering + before[j]
    backs = [
        remote(back.at[place ^ k], done.at[k], sends, recvs, SIDE + groups + k, where.member[k]) for k in range(1, SIDE)
    ]
    for c in backs:
        c.start()
    after_all()
    done[0] = back[place]
    for c in backs:
        c.wait_recv()
    for q in range(SIDE):
        out_ref[:, :, q * width : (q + 1) * width] = done[place ^ q].reshape(streams, n, width)
    for c in sides + lines + backs:
        c.wait_send()


def chain_scratch(streams, n, channels, groups):
    width = channels // SIDE
    rows = streams * n
    tall = rows + 8 * (-(-streams // 8))
    sems = pltpu.SemaphoreType.DMA((2 * SIDE + groups,))
    return [
        pltpu.VMEM((SIDE, tall, width), jnp.float32),
        pltpu.VMEM((SIDE, tall, width), jnp.float32),
        pltpu.VMEM((tall, width), jnp.float32),
        pltpu.VMEM((groups, tall, width), jnp.float32),
        pltpu.VMEM((SIDE, rows, width), jnp.float32),
        pltpu.VMEM((SIDE, rows, width), jnp.float32),
        sems,
        sems,
    ]


def sums(fall, total):
    for s in range(fall.shape[0]):
        total[s : s + 1, :] = jnp.sum(fall[s], axis=0, keepdims=True)


def blocks_of(channels):
    lanes = pieces(channels)
    return lanes, channels // lanes


def columns(i, lanes):
    return pl.ds(pl.multiple_of(i * lanes, lanes), lanes)


def forward_kernel(
    count, fall, gain, b_ref, c_ref, rate_ref, grad_up, grad_down, norm_near, norm_next,
    y_ref, first, ring, ring_rest, side_far, side_rest,
    ends, total, line_send, line_recv, side_send, side_recv, local, *scratch,
):
    where = Place(count)
    streams, length, channels = fall.shape
    n = rate_ref.shape[0]
    lanes, blocks = blocks_of(channels)
    z = where.z
    where.greet()
    line = Line(where, None, ring, ring_rest, line_send, line_recv)
    lift = pltpu.make_async_copy(grad_up, ring.at[SIDE - 2], local.at[0])
    sink = pltpu.make_async_copy(grad_down, ring.at[0], local.at[1])
    pl.when(z >= 1)(lift.start)
    pl.when(z <= SIDE - 2)(sink.start)

    def summary(i, _):
        cols = columns(i, lanes)
        rate = rate_ref[:, cols]

        def chunk(i, states):
            base = pl.multiple_of(i * ROWS, ROWS)
            out = []
            for s in range(streams):
                state = states[s]
                d = fall[s, pl.ds(base, ROWS), cols]
                x = gain[s, pl.ds(base, ROWS), cols]
                for j in range(ROWS):
                    b = b_ref[s, pl.ds(pl.multiple_of((base + j) * n, n), n), :]
                    fade = jnp.exp2(d[j : j + 1] * rate)
                    state = fade * state + x[j : j + 1] * wide(b, lanes)
                out.append(state)
            return tuple(out)

        start = tuple(jnp.zeros((n, lanes), jnp.float32) for _ in range(streams))
        states = lax.fori_loop(0, length // ROWS, chunk, start)
        for s in range(streams):
            ends[s, :, cols] = states[s]
        return 0

    lax.fori_loop(0, blocks, summary, 0)
    sums(fall, total)

    half = norm_near.shape[0] // 2
    top, low = pl.ds(0, half), pl.ds(half, half)
    far = [
        remote(norm_next.at[top], side_far.at[top], side_send, side_recv, 0, where.member[1]),
        remote(norm_near.at[low], side_far.at[low], side_send, side_recv, 1, where.member[2]),
    ]
    cores = [
        remote(part, side_rest.at[k], side_send, side_recv, 2 + k, where.core)
        for k, part in enumerate((norm_near, norm_next, side_far))
    ]

    def after_line():
        @pl.when(z >= 1)
        def _():
            lift.wait()
            line.core(SIDE - 2).start()

        @pl.when(z <= SIDE - 2)
        def _():
            sink.wait()
            line.core(0).start()

        line.start(2)

    def after_all():
        for c in far + cores[:2]:
            c.start()

    chain(where, False, ends, total, rate_ref, first, scratch, after_line, after_all)

    def run(i, _):
        cols = columns(i, lanes)
        rate = rate_ref[:, cols]

        @pl.when(i == blocks // 2)
        def _():
            line.arrive(2)
            line.start(3)

        def chunk(i, states):
            base = pl.multiple_of(i * ROWS, ROWS)
            out = []
            for s in range(streams):
                state = states[s]
                d = fall[s, pl.ds(base, ROWS), cols]
                x = gain[s, pl.ds(base, ROWS), cols]
                rows = []
                for j in range(ROWS):
                    at = pl.ds(pl.multiple_of((base + j) * n, n), n)
                    fade = jnp.exp2(d[j : j + 1] * rate)
                    state = fade * state + x[j : j + 1] * wide(b_ref[s, at, :], lanes)
                    rows.append(jnp.sum(state * wide(c_ref[s, at, :], lanes), axis=0, keepdims=True))
                y_ref[s, pl.ds(base, ROWS), cols] = jnp.concatenate(rows, axis=0)
                out.append(state)
            return tuple(out)

        lax.fori_loop(0, length // ROWS, chunk, tuple(first[s, :, cols] for s in range(streams)))
        return 0

    lax.fori_loop(0, blocks, run, 0)
    for c in far:
        c.wait_recv()
    cores[2].start()
    line.arrive(3)
    for c in far:
        c.wait_send()
    for c in cores:
        c.wait()
    line.finish(2)


def backward_kernel(
    count, fall, d_ref, v_ref, g_ref, b_ref, c_ref, rate_ref, first_ref, hidden, mix, y_ref,
    dstep_ref, dvalue_ref, db_ref, dc_ref, decay_ref, ring, ring_rest, side, side_rest, y_side,
    ends, total, last, path, fades, line_send, line_recv, side_send, side_recv, y_send, y_recv, *scratch,
):
    where = Place(count)
    streams, length, channels = fall.shape
    n = rate_ref.shape[0]
    lanes, blocks = blocks_of(channels)
    chunks = length // ROWS
    width = channels // SIDE
    where.greet()
    line = Line(where, hidden, ring, ring_rest, line_send, line_recv)
    square = Side(where, mix, side, side_rest, side_send, side_recv)
    quarters = [
        remote(
            y_ref.at[:, :, pl.ds(pl.multiple_of((where.place ^ k) * width, 128), width)],
            y_side.at[k - 1], y_send, y_recv, k - 1, where.member[k],
        )
        for k in range(1, SIDE)
    ]

    def summary(i, _):
        cols = columns(i, lanes)
        rate = rate_ref[:, cols]

        def chunk(i, carry):
            base = pl.multiple_of((chunks - 1 - i) * ROWS, ROWS)
            out = []
            for s in range(streams):
                carried = carry[s]
                d = fall[s, pl.ds(base, ROWS), cols]
                g = g_ref[s, pl.ds(base, ROWS), cols]
                for j in reversed(range(ROWS)):
                    at = pl.ds(pl.multiple_of((base + j) * n, n), n)
                    fade = jnp.exp2(d[j : j + 1] * rate)
                    carried = fade * (g[j : j + 1] * wide(c_ref[s, at, :], lanes) + carried)
                out.append(carried)
            return tuple(out)

        start = tuple(jnp.zeros((n, lanes), jnp.float32) for _ in range(streams))
        states = lax.fori_loop(0, chunks, chunk, start)
        for s in range(streams):
            ends[s, :, cols] = states[s]
        return 0

    lax.fori_loop(0, blocks, summary, 0)
    sums(fall, total)

    def after_line():
        line.start(1)

    def after_all():
        square.start()

    chain(where, True, ends, total, rate_ref, last, scratch, after_line, after_all)
    db_ref[...] = jnp.zeros_like(db_ref)
    dc_ref[...] = jnp.zeros_like(dc_ref)

    def fold(tile):
        out = tile[:, :128]
        for k in range(1, lanes // 128):
            out = out + tile[:, k * 128 : (k + 1) * 128]
        return out

    def run(i, _):
        cols = columns(i, lanes)
        rate = rate_ref[:, cols]

        @pl.when(i == blocks // 6)
        def _():
            line.arrive(1)
            line.start(2)

        @pl.when(i == blocks // 2)
        def _():
            square.turn()
            for c in quarters:
                c.start()

        @pl.when(i == blocks - blocks // 6)
        def _():
            line.arrive(2)
            line.start(3)

        def ahead(i, states):
            base = pl.multiple_of(i * ROWS, ROWS)
            out = []
            for s in range(streams):
                state = states[s]
                d = fall[s, pl.ds(base, ROWS), cols]
                x = d_ref[s, pl.ds(base, ROWS), cols] * v_ref[s, pl.ds(base, ROWS), cols]
                for j in range(ROWS):
                    at = pl.ds(pl.multiple_of((base + j) * n, n), n)
                    path[s, at, :] = state
                    fade = jnp.exp2(d[j : j + 1] * rate)
                    fades[s, at, :] = fade
                    state = fade * state + x[j : j + 1] * wide(b_ref[s, at, :], lanes)
                out.append(state)
            return tuple(out)

        tails = lax.fori_loop(0, chunks, ahead, tuple(first_ref[s, :, cols] for s in range(streams)))

        def back(i, carry):
            base = pl.multiple_of((chunks - 1 - i) * ROWS, ROWS)
            out = []
            decay = carry[-1]
            for s in range(streams):
                state, carried = carry[s]
                d = d_ref[s, pl.ds(base, ROWS), cols]
                v = v_ref[s, pl.ds(base, ROWS), cols]
                g = g_ref[s, pl.ds(base, ROWS), cols]
                x = d * v
                weights, touches = [None] * ROWS, [None] * ROWS
                for j in reversed(range(ROWS)):
                    at = pl.ds(pl.multiple_of((base + j) * n, n), n)
                    gj = g[j : j + 1]
                    adjoint = gj * wide(c_ref[s, at, :], lanes) + carried
                    dc_ref[s, at, :] += fold(state * gj)
                    db_ref[s, at, :] += fold(adjoint * x[j : j + 1])
                    weights[j] = jnp.sum(adjoint * wide(b_ref[s, at, :], lanes), axis=0, keepdims=True)
                    carried = adjoint * fades[s, at, :]
                    state = path[s, at, :]
                    touch = carried * state
                    touches[j] = jnp.sum(touch * rate, axis=0, keepdims=True)
                    decay = decay + touch * d[j : j + 1]
                weighted = jnp.concatenate(weights, axis=0)
                at = pl.ds(base, ROWS)
                dstep_ref[s, at, cols] = weighted * v + jnp.concatenate(touches, axis=0) * LN2
                dvalue_ref[s, at, cols] = weighted * d
                out.append((state, carried))
            return tuple(out) + (decay,)

        start = tuple((tails[s], last[s, :, cols]) for s in range(streams))
        done = lax.fori_loop(0, chunks, back, start + (jnp.zeros((n, lanes), jnp.float32),))
        decay_ref[:, cols] = done[-1]
        return 0

    lax.fori_loop(0, blocks, run, 0)
    square.finish()
    line.arrive(3)
    for c in quarters:
        c.wait()
    line.finish()


def in_vmem():
    return pl.BlockSpec(memory_space=pltpu.VMEM)


def in_hbm():
    return pl.BlockSpec(memory_space=pl.ANY)


def shaped(*shape):
    return jax.ShapeDtypeStruct(shape, jnp.float32)


def sems(count):
    return [pltpu.SemaphoreType.DMA((count,))] * 2


def scan_forward(fall, gain, b_wide, c_wide, rate, grad_up, grad_down, norm_near, norm_next):
    streams, length, channels = fall.shape
    n = rate.shape[0]
    count = lax.axis_size("seq")
    half, width = grad_up.shape
    three = shaped(SIDE - 1, half, width)
    return pl.pallas_call(
        functools.partial(forward_kernel, count),
        out_shape=[shaped(streams, length, channels), shaped(streams, n, channels), three, three, shaped(half, width), three],
        in_specs=[in_vmem()] * 5 + [in_hbm()] * 4,
        out_specs=[in_vmem()] * 2 + [in_hbm()] * 4,
        scratch_shapes=[pltpu.VMEM((streams, n, channels), jnp.float32), pltpu.VMEM((streams, channels), jnp.float32)]
        + sems(LINE_SEMS) + sems(5) + [pltpu.SemaphoreType.DMA((2,))]
        + chain_scratch(streams, n, channels, count // SIDE),
        compiler_params=pltpu.CompilerParams(
            collective_id=0, has_side_effects=True, vmem_limit_bytes=40 * 1024 * 1024
        ),
        cost_estimate=spans(40),
    )(fall, gain, b_wide, c_wide, rate, grad_up, grad_down, norm_near, norm_next)


def scan_backward(fall, step, value, d_y, b_wide, c_wide, rate, first, hidden, mix, y):
    streams, length, channels = fall.shape
    n = rate.shape[0]
    count = lax.axis_size("seq")
    half, width = hidden.shape
    lanes, _ = blocks_of(channels)
    three = shaped(SIDE - 1, half, width)
    tall = shaped(streams, length * n, 128)
    flat = shaped(streams, length, channels)
    kept = pltpu.VMEM((streams, length * n, lanes), jnp.float32)
    return pl.pallas_call(
        functools.partial(backward_kernel, count),
        out_shape=[flat, flat, tall, tall, shaped(n, channels), three, three, three, three,
                   shaped(SIDE - 1, streams, length, channels // SIDE)],
        in_specs=[in_vmem()] * 8 + [in_hbm()] * 3,
        out_specs=[in_vmem()] * 5 + [in_hbm()] * 5,
        scratch_shapes=[
            pltpu.VMEM((streams, n, channels), jnp.float32),
            pltpu.VMEM((streams, channels), jnp.float32),
            pltpu.VMEM((streams, n, channels), jnp.float32),
            kept,
            kept,
        ]
        + sems(LINE_SEMS) + sems(SIDE_SEMS) + sems(SIDE - 1)
        + chain_scratch(streams, n, channels, count // SIDE),
        compiler_params=pltpu.CompilerParams(
            collective_id=1, has_side_effects=True, vmem_limit_bytes=52 * 1024 * 1024
        ),
        cost_estimate=spans(62),
    )(fall, step, value, d_y, b_wide, c_wide, rate, first, hidden, mix, y)


epsilon = 1e-06
CUT = 1e6


def links(step, wrap=False, axis="seq"):
    n = lax.axis_size(axis)
    return [(i, (i + step) % n) for i in range(n) if wrap or 0 <= i + step < n]


def swaps(bit, axis="seq"):
    return [(i, i ^ bit) for i in range(lax.axis_size(axis))]


def send(block, route, axis="seq"):
    return lax.ppermute(block, axis, route)


def head_sum(part):
    return part + send(part, swaps(1, "head"), "head")


def own_stream(block):
    return lax.dynamic_index_in_dim(block, lax.axis_index("head"), 0, keepdims=False)


def unswap(parts, place):
    odd, far = (place & 1) == 1, (place & 2) == 2
    p = list(parts)
    p = [jnp.where(odd, p[k ^ 1], p[k]) for k in range(4)]
    return [jnp.where(far, p[k ^ 2], p[k]) for k in range(4)]


def part_of(block, index, size, axis):
    return lax.dynamic_slice_in_dim(block, index * size, size, axis)


def exchange(block, place):
    size = block.shape[-1] // SIDE
    first = lax.axis_index("head")
    turned = jnp.stack([lax.dynamic_index_in_dim(block, first, 0, keepdims=False), lax.dynamic_index_in_dim(block, 1 - first, 0, keepdims=False)])
    away = [part_of(turned, place ^ k, size, 2).astype(jnp.float32) for k in range(1, SIDE)]
    return part_of(block, place, size, 2).reshape(-1, size), [send(away[k - 1], swaps(k)) for k in range(1, SIDE)]


def after(block, *earlier):
    return lax.optimization_barrier((block,) + earlier)[0]


def scatter_bits(blocks, bits):
    here = lax.axis_index("seq")
    order = sorted(bits)
    shape = blocks.shape[1:]
    left = list(order)
    blocks = blocks.reshape((2,) * len(order) + shape)
    for bit in bits:
        axis = len(left) - 1 - left.index(bit)
        mine = (here // bit) % 2
        keep = lax.dynamic_index_in_dim(blocks, mine, axis, keepdims=False)
        away = lax.dynamic_index_in_dim(blocks, 1 - mine, axis, keepdims=False)
        blocks = keep + send(away, swaps(bit))
        left.remove(bit)
    return blocks


def bits_between(low, high):
    out = []
    while low < high:
        out.append(low)
        low *= 2
    return out


def matmul(left, right):
    return jnp.dot(left, right, preferred_element_type=jnp.float32)


def matmul_back(left, right):
    return lax.dot_general(
        left, right, (((left.ndim - 1,), (1,)), ((), ())), preferred_element_type=jnp.float32
    )


def weight_outer(left, right):
    axes = tuple(range(left.ndim - 1))
    return lax.dot_general(left, right, ((axes, axes), ((), ())), preferred_element_type=jnp.float32)


def norm_forward(v, gain):
    scale = lax.rsqrt(jnp.mean(v * v, axis=-1, keepdims=True) + epsilon)
    return (v * scale * gain, scale)


def norm_backward(v, scale, gain, upstream):
    weighted = upstream * gain
    d_input = scale * weighted - v * scale * scale * scale * jnp.mean(
        weighted * v, axis=-1, keepdims=True
    )
    d_gain = jnp.sum(upstream * v * scale, axis=(0, 1))
    return (d_input, d_gain)


def silu_slope(v):
    sig = jax.nn.sigmoid(v)
    return sig + v * sig * (1.0 - sig)


def across(small):
    streams, length, n = small.shape
    return jnp.broadcast_to(small.reshape(streams, length * n, 1), (streams, length * n, 128))


def along(wide_sum, n):
    streams, rows, _ = wide_sum.shape
    return jnp.sum(wide_sum, axis=-1).reshape(streams, rows // n, n)


def body(
    tokens, doc_ids, out_grad, norm_mix, w_inner, w_outgate, conv_taps, conv_bias, w_select, select_gain,
    w_step, step_bias, log_decay, skip_gain, w_mixout, norm_ffn, w_gate, w_up, w_down,
):
    streams, length, width = tokens.shape
    channels = w_inner.shape[1]
    taps = conv_taps.shape[0]
    rank = w_step.shape[0]
    states = log_decay.shape[1]
    lead = taps - 1
    count = lax.axis_size("seq")
    stride = count // SIDE
    here = lax.axis_index("seq")
    z, place = here // stride, here % SIDE
    low = jnp.bfloat16

    grad_in = out_grad.astype(jnp.float32)
    source = tokens.astype(jnp.float32)
    rim_ids = jnp.broadcast_to((doc_ids[:, length - lead :] + 1).astype(jnp.float32)[:, :, None], (streams, lead, 128))
    rim = send(jnp.concatenate([source[:, length - lead :], rim_ids], axis=2), links(1))
    mine_grad = own_stream(out_grad).astype(jnp.float32)
    grad_up = send(mine_grad, links(stride))
    grad_down = send(mine_grad, links(-stride))
    normed, scale_mix = norm_forward(source, norm_mix)
    normed_low = normed.astype(low)
    mine_normed = own_stream(normed)
    norm_near, norm_next = send(mine_normed, swaps(1)), send(mine_normed, swaps(2))
    rim_normed, _ = norm_forward(rim[:, :, :width], norm_mix)
    ext_val = matmul(jnp.concatenate([rim_normed.astype(low), normed_low], axis=1), w_inner)
    outgate = matmul(normed_low, w_outgate)
    ext_ids = jnp.concatenate([rim[:, :, width].astype(jnp.int32) - 1, doc_ids], axis=1)
    masks = [
        (ext_ids[:, k : k + length] == doc_ids).astype(jnp.float32)[:, :, None] for k in range(taps)
    ]
    value_pre = conv_bias
    for k in range(taps):
        value_pre = value_pre + conv_taps[k] * ext_val[:, k : k + length] * masks[k]
    value = jax.nn.silu(value_pre)
    value_low = value.astype(low)
    select = head_sum(matmul(value_low, w_select))
    raw_step = select[..., :rank]
    raw_b = select[..., rank : rank + states]
    raw_c = select[..., rank + states :]
    step_n, step_scale = norm_forward(raw_step, select_gain[:rank])
    bsel, b_scale = norm_forward(raw_b, select_gain[rank : rank + states])
    csel, c_scale = norm_forward(raw_c, select_gain[rank + states :])
    step_low = step_n.astype(low)
    step_pre = matmul(step_low, w_step) + step_bias
    step = jax.nn.softplus(step_pre)
    keep = doc_ids == ext_ids[:, lead - 1 : lead - 1 + length]
    fall = jnp.where(keep[:, :, None], step, CUT)
    gain = step * value
    decay_rate = -jnp.exp(log_decay).T
    rate = decay_rate * LOG2E
    b_wide, c_wide = across(bsel), across(csel)
    outs, first, grad_ring, grad_rest, side_far, side_rest = scan_forward(
        fall, gain, b_wide, c_wide, rate, grad_up, grad_down, norm_near, norm_next
    )
    y = outs + skip_gain * value
    gate_z = jax.nn.silu(outgate)
    mixed = y * gate_z
    mixed_low = mixed.astype(low)
    mix = head_sum(matmul(mixed_low, w_mixout))
    resid = source + mix
    hidden, scale_ffn = norm_forward(resid, norm_ffn)
    hidden_low = hidden.astype(low)
    gate = matmul(hidden_low, w_gate)
    up = matmul(hidden_low, w_up)
    act_low = (jax.nn.silu(gate) * up).astype(low)
    ffn = head_sum(matmul(act_low, w_down))
    output = (resid + ffn).astype(low)
    d_act = matmul_back(out_grad, w_down)
    d_gate = (d_act * up * silu_slope(gate)).astype(low)
    d_up = (d_act * jax.nn.silu(gate)).astype(low)
    d_hidden = head_sum(matmul_back(d_gate, w_gate) + matmul_back(d_up, w_up))
    d_resid_norm, grad_norm_ffn = norm_backward(resid, scale_ffn, norm_ffn, d_hidden)
    d_resid = grad_in + d_resid_norm
    d_mix = d_resid.astype(low)
    d_mixed = matmul_back(d_mix, w_mixout)
    d_y = d_mixed * gate_z
    d_outgate = (d_mixed * y * silu_slope(outgate)).astype(low)
    grad_skip_gain = jnp.sum(d_y * value, axis=(0, 1))
    d_step, d_scan, db_wide, dc_wide, decay_sum, hid_ring, hid_rest, mix_side, mix_rest, y_side = scan_backward(
        fall, step, value, d_y, b_wide, c_wide, rate, first, own_stream(hidden), own_stream(d_resid), y
    )

    flat = lambda block: block.reshape(-1, block.shape[-1])
    size = channels // SIDE
    whole_outgate, whole_mixout, turned = mixer_grads(
        flat(normed_low), [norm_near, norm_next, side_far, side_rest], flat(d_mix), [mix_side, mix_rest],
        flat(part_of(y, place, size, 2)), y_side,
        part_of(w_outgate, place, size, 1), part_of(w_mixout, place, size, 0),
    )
    whole_gate, whole_up, whole_down = ffn_grads(
        stride, flat(hidden_low), [hid_ring, hid_rest], flat(out_grad), [grad_ring, grad_rest], w_gate, w_up, w_down,
        flat(d_gate), flat(d_up), flat(act_low),
    )
    side_bits = bits_between(1, stride)
    orders = (side_bits, side_bits[len(side_bits) // 2 :] + side_bits[: len(side_bits) // 2])

    def sum_side(whole):
        whole = whole.reshape(stride, width // count, -1)
        half = whole.shape[2] // 2
        return jnp.concatenate(
            [scatter_bits(whole[..., :half], orders[0]), scatter_bits(whole[..., half:], orders[1])], axis=-1
        )

    grad_w_gate = sum_side(whole_gate)
    grad_w_up = sum_side(whole_up)
    grad_w_down = sum_side(whole_down).T

    groups = [list(range(k, count, SIDE)) for k in range(SIDE)]

    def sum_line(whole):
        own = lax.psum_scatter(whole, "seq", scatter_dimension=0, axis_index_groups=groups, tiled=True)
        own = own.reshape(SIDE, width // count, -1)
        sent = unswap([own[k] for k in range(SIDE)], place)
        got = [sent[0]] + [send(sent[k], swaps(k)) for k in range(1, SIDE)]
        return jnp.concatenate(unswap(got, place), axis=-1)

    grad_w_mixout = sum_line(whole_mixout).T
    grad_w_outgate = sum_line(whole_outgate)

    d_value = d_y * skip_gain + d_scan
    d_step_pre = (d_step * jax.nn.sigmoid(step_pre)).astype(low)
    grad_step_bias = jnp.sum(d_step_pre, axis=(0, 1), dtype=jnp.float32)
    grad_w_step = weight_outer(step_low, d_step_pre)
    d_small = head_sum(
        jnp.concatenate(
            [matmul_back(d_step_pre, w_step), along(db_wide, states), along(dc_wide, states)], axis=-1
        )
    )
    d_raw_step, gain_step = norm_backward(
        raw_step, step_scale, select_gain[:rank], d_small[..., :rank]
    )
    d_raw_b, gain_b = norm_backward(
        raw_b, b_scale, select_gain[rank : rank + states], d_small[..., rank : rank + states]
    )
    d_raw_c, gain_c = norm_backward(
        raw_c, c_scale, select_gain[rank + states :], d_small[..., rank + states :]
    )
    grad_select_gain = jnp.concatenate([gain_step, gain_b, gain_c])
    d_select = jnp.concatenate([d_raw_step, d_raw_b, d_raw_c], axis=-1).astype(low)
    grad_w_select = weight_outer(d_select, value_low)
    d_value = d_value + matmul_back(d_select, w_select)
    d_value_pre = d_value * silu_slope(value_pre)
    grad_conv_bias = jnp.sum(d_value_pre, axis=(0, 1))
    tap_grads = []
    d_ext = jnp.zeros_like(ext_val)
    for k in range(taps):
        masked = d_value_pre * masks[k]
        tap_grads.append(jnp.sum(masked * ext_val[:, k : k + length], axis=(0, 1)))
        d_ext = d_ext + jnp.pad(masked * conv_taps[k], ((0, 0), (k, lead - k), (0, 0)))
    grad_conv_taps = jnp.stack(tap_grads)
    rim_grad = send(d_ext[:, :lead], links(-1))
    d_inner = (d_ext[:, lead:] + jnp.pad(rim_grad, ((0, 0), (length - lead, 0), (0, 0)))).astype(low)
    own_d_inner, side_d_inner = exchange(d_inner, place)
    grad_w_inner = sum_line(inner_grad(turned, own_d_inner, side_d_inner))
    d_normed = head_sum(matmul_back(d_inner, w_inner) + matmul_back(d_outgate, w_outgate))
    d_source, grad_norm_mix = norm_backward(source, scale_mix, norm_mix, d_normed)
    tokens_grad = d_resid + d_source

    pad = lambda v: jnp.pad(v, (0, channels - v.shape[0]))
    selects = grad_select_gain.reshape(count, -1)
    tall = jnp.concatenate(
        [
            grad_w_step,
            decay_sum * decay_rate,
            grad_conv_taps,
            jnp.stack([grad_conv_bias, grad_step_bias, grad_skip_gain, grad_norm_mix, grad_norm_ffn]),
        ]
    )
    tall = jnp.swapaxes(tall.reshape(tall.shape[0], count, -1), 0, 1)
    selects = jnp.pad(selects, ((0, 0), (0, tall.shape[2] - selects.shape[1])))
    tall = jnp.concatenate([tall, selects[:, None]], axis=1)
    broad = grad_w_select.reshape(count, -1, channels)
    every = bits_between(1, count)
    turned = every[1:2] + every[:1] + every[2:]
    tall = scatter_bits(tall, every)
    broad = scatter_bits(broad, turned)
    at = rank + states
    return (
        output,
        tokens_grad,
        tall[at + taps + 3],
        grad_w_inner,
        grad_w_outgate,
        tall[at : at + taps],
        tall[at + taps],
        broad.T,
        tall[at + taps + 5, : grad_select_gain.shape[0] // count],
        tall[:rank],
        tall[at + taps + 1],
        tall[rank:at].T,
        tall[at + taps + 2],
        grad_w_mixout,
        tall[at + taps + 4],
        grad_w_gate,
        grad_w_up,
        grad_w_down,
    )


def solution(mesh):
    in_specs = (
        P(None, "seq", None),
        P(None, "seq"),
        P(None, "seq", None),
        P(),
        P(None, "head"),
        P(None, "head"),
        P(None, "head"),
        P("head"),
        P("head", None),
        P(),
        P(None, "head"),
        P("head"),
        P("head", None),
        P("head"),
        P("head", None),
        P(),
        P(None, "head"),
        P(None, "head"),
        P("head", None),
    )
    out_specs = (
        P(None, "seq", None),
        P(None, "seq", None),
        P("seq"),
        P("seq", "head"),
        P("seq", "head"),
        P(None, ("head", "seq")),
        P(("head", "seq")),
        P("head", "seq"),
        P("seq"),
        P(None, ("head", "seq")),
        P(("head", "seq")),
        P(("head", "seq"), None),
        P(("head", "seq")),
        P("head", "seq"),
        P("seq"),
        P("seq", "head"),
        P("seq", "head"),
        P("head", "seq"),
    )
    return jax.shard_map(body, mesh=mesh, in_specs=in_specs, out_specs=out_specs, check_vma=False)
```

```python
import functools
import math

import jax
import jax.numpy as jnp
from jax import lax
from jax.experimental import pallas as pl
from jax.experimental.pallas import tpu as pltpu
from jax.sharding import PartitionSpec as P

LOG2E = math.log2(math.e)
LN2 = math.log(2.0)
ROWS = 8


def params(limit=48):
    return pltpu.CompilerParams(vmem_limit_bytes=limit * 1024 * 1024)


def wide(tile, lanes):
    return jnp.concatenate([tile] * (lanes // tile.shape[1]), axis=1)


def pieces(lanes):
    return next(w for w in (256, 128) if lanes % w == 0)


def spans(us):
    return pl.CostEstimate(flops=int(us * 1.1e8), bytes_accessed=int(us * 3.0e5), transcendentals=0)


def stack_tokens(target, own_ref, more_refs):
    own = own_ref.shape[0]
    target[:own, :] = own_ref[...].astype(target.dtype)
    at = own
    for ref in more_refs:
        parts = [ref[k] for k in range(ref.shape[0])] if len(ref.shape) == 3 else [ref[...]]
        for part in parts:
            target[at : at + part.shape[0], :] = part.astype(target.dtype)
            at += part.shape[0]


def dot(left, right):
    return jnp.dot(left, right, preferred_element_type=jnp.float32)


def dot_back(left, right):
    return lax.dot_general(left, right, (((1,), (1,)), ((), ())), preferred_element_type=jnp.float32)


def whole(shape):
    return pl.BlockSpec(shape, lambda i: (0,) * len(shape), pipeline_mode=pl.Buffered(1))


def mixer_kernel(more_norm, more_mix, *refs):
    at = iter(range(len(refs)))
    take = lambda count: [refs[next(at)] for _ in range(count)]
    (norm_own,), norm_more = take(1), take(more_norm)
    (mix_own,), mix_more = take(1), take(more_mix)
    y_own, y_side = take(2)
    w_out, w_mix = take(2)
    out, norm_turned = take(2)
    norm, mix, mixed, d_out, wo, wm, local = take(7)
    own = norm_own.shape[0]
    half = own // 2

    @pl.when(pl.program_id(0) == 0)
    def _():
        size = wo.shape[1]
        at = pl.ds(pl.multiple_of(lax.rem(lax.axis_index("seq"), SIDE) * size, 128), size)
        loads = [
            pltpu.make_async_copy(w_out.at[:, at], wo, local.at[0]),
            pltpu.make_async_copy(w_mix.at[at], wm, local.at[1]),
        ]
        for c in loads:
            c.start()
        stack_tokens(norm, norm_own, norm_more)
        stack_tokens(mix, mix_own, mix_more)
        for c in loads:
            c.wait()

        def finish(rows, y):
            outgate = dot(norm[rows, :], wo[...])
            d_mixed = dot_back(mix[rows, :], wm[...])
            sig = 1.0 / (1.0 + jnp.exp(-outgate))
            silu = outgate * sig
            mixed[rows, :] = (y * silu).astype(mixed.dtype)
            d_out[rows, :] = (d_mixed * y * (sig + silu * (1.0 - sig))).astype(d_out.dtype)

        finish(slice(0, own), y_own[...])
        sides = y_side.shape[0]
        head = lax.axis_index("head")
        for k in range(sides):
            for s in range(2):
                start = own + (s * sides + k) * half
                finish(slice(start, start + half), y_side[k, head if s == 0 else 1 - head])

    rows = norm_turned.shape[0]
    span = pl.ds(pl.multiple_of(pl.program_id(0) * rows, rows), rows)
    turned = norm[:, span].T
    norm_turned[...] = turned
    out[0] = dot(turned, d_out[...])
    out[1] = dot(mix[:, span].T, mixed[...])


def mixer_grads(norm_own, norm_more, mix_own, mix_more, y_own, y_side, w_out, w_mix):
    own, width = norm_own.shape
    cut = w_out.shape[1] // SIDE
    block = next(b for b in (256, 128) if width % b == 0)
    tokens = own + sum(math.prod(part.shape[:-1]) for part in norm_more)
    low = jnp.bfloat16
    row = lambda columns: pl.BlockSpec((block, columns), lambda i: (i, 0))
    operands = (norm_own, *norm_more, mix_own, *mix_more, y_own, y_side, w_out, w_mix)
    return pl.pallas_call(
        functools.partial(mixer_kernel, len(norm_more), len(mix_more)),
        grid=(width // block,),
        in_specs=[whole(a.shape) for a in operands[:-2]] + [pl.BlockSpec(memory_space=pl.ANY)] * 2,
        out_specs=[pl.BlockSpec((2, block, cut), lambda i: (0, i, 0)), row(tokens)],
        out_shape=[
            jax.ShapeDtypeStruct((2, width, cut), jnp.float32),
            jax.ShapeDtypeStruct((width, tokens), low),
        ],
        scratch_shapes=[pltpu.VMEM((tokens, width), low)] * 2
        + [pltpu.VMEM((tokens, cut), low)] * 2
        + [pltpu.VMEM((width, cut), low), pltpu.VMEM((cut, width), low), pltpu.SemaphoreType.DMA((2,))],
        compiler_params=params(56),
        cost_estimate=spans(12),
    )(*operands)


SIDE = 4
MESH = pl.DeviceIdType.MESH


def remote(source, target, sends, recvs, at, device):
    return pltpu.make_async_remote_copy(
        src_ref=source, dst_ref=target, send_sem=sends.at[at], recv_sem=recvs.at[at],
        device_id=device, device_id_type=MESH,
    )


class Place:
    def __init__(self, count):
        here = lax.axis_index("seq")
        self.head = lax.axis_index("head")
        self.stride = count // SIDE
        self.groups = count // SIDE
        self.place, self.group = lax.rem(here, SIDE), here // SIDE
        self.z = here // self.stride
        base = here - self.place
        self.member = [(base + (self.place ^ k), self.head) for k in range(SIDE)]
        self.other = [
            (lax.rem(self.group + k, self.groups) * SIDE + self.place, self.head) for k in range(self.groups)
        ]
        self.core = (here, 1 - self.head)
        self.above = (lax.rem(here + self.stride, count), self.head)
        self.below = (lax.rem(here - self.stride + count, count), self.head)

    def greet(self):
        barrier = pltpu.get_barrier_semaphore()
        devices = self.member[1:] + self.other[1:] + [self.core]
        for device in devices:
            pl.semaphore_signal(barrier, inc=1, device_id=device, device_id_type=MESH)
        pl.semaphore_wait(barrier, len(devices))


class Line:
    def __init__(self, where, up_one, down_one, ring, rest, sends, recvs):
        self.where, self.up_one, self.down_one = where, up_one, down_one
        self.ring, self.rest, self.sends, self.recvs = ring, rest, sends, recvs

    def copies(self, step):
        w = self.where
        up = self.up_one if step == 2 else self.ring.at[SIDE - step]
        down = self.down_one if step == 2 else self.ring.at[step - 2]
        return (
            remote(up, self.ring.at[SIDE - 1 - step], self.sends, self.recvs, step - 1, w.above),
            remote(down, self.ring.at[step - 1], self.sends, self.recvs, SIDE - 2 + step, w.below),
        )

    def core(self, slot):
        return remote(self.ring.at[slot], self.rest.at[slot], self.sends, self.recvs, 2 * SIDE - 2 + slot, self.where.core)

    def start(self, step):
        up, down = self.copies(step)
        z = self.where.z
        pl.when((z >= step - 1) & (z < SIDE - 1))(up.start)
        pl.when((z <= SIDE - step) & (z > 0))(down.start)

    def arrive(self, step):
        up, down = self.copies(step)
        z = self.where.z

        @pl.when(z >= step)
        def _():
            up.wait_recv()
            self.core(SIDE - 1 - step).start()

        @pl.when(z <= SIDE - 1 - step)
        def _():
            down.wait_recv()
            self.core(step - 1).start()

    def cores_of_one(self):
        return (
            remote(self.up_one, self.rest.at[SIDE - 2], self.sends, self.recvs, 2 * SIDE - 2 + SIDE - 2, self.where.core),
            remote(self.down_one, self.rest.at[0], self.sends, self.recvs, 2 * SIDE - 2, self.where.core),
        )

    def start_cores_of_one(self):
        up, down = self.cores_of_one()
        pl.when(self.where.z >= 1)(up.start)
        pl.when(self.where.z <= SIDE - 2)(down.start)

    def finish(self):
        z = self.where.z
        for step in range(2, SIDE):
            up, down = self.copies(step)
            pl.when((z >= step - 1) & (z < SIDE - 1))(up.wait_send)
            pl.when((z <= SIDE - step) & (z > 0))(down.wait_send)
        for slot in range(SIDE - 1):
            self.core(slot).wait()


LINE_SEMS = 3 * (SIDE - 1)


class Side:
    def __init__(self, where, mine, side, rest, sends, recvs):
        self.where, self.mine, self.side, self.rest, self.sends, self.recvs = where, mine, side, rest, sends, recvs

    def near(self):
        return [
            remote(self.mine, self.side.at[k - 1], self.sends, self.recvs, k - 1, self.where.member[k]) for k in (1, 2)
        ]

    def far(self):
        half = self.side.shape[1] // 2
        top, low = pl.ds(0, half), pl.ds(half, half)
        return [
            remote(self.side.at[1, top], self.side.at[2, top], self.sends, self.recvs, 2, self.where.member[1]),
            remote(self.side.at[0, low], self.side.at[2, low], self.sends, self.recvs, 3, self.where.member[2]),
        ]

    def core(self, slot):
        return remote(self.side.at[slot], self.rest.at[slot], self.sends, self.recvs, 4 + slot, self.where.core)

    def start(self):
        for c in self.near():
            c.start()

    def turn(self):
        for c in self.near():
            c.wait_recv()
        for c in self.far():
            c.start()
        for slot in (0, 1):
            self.core(slot).start()

    def finish(self):
        for c in self.far():
            c.wait_recv()
        self.core(2).start()
        for c in self.near() + self.far():
            c.wait_send()
        for slot in range(3):
            self.core(slot).wait()


SIDE_SEMS = 7


def chain(where, reverse, ends, total, rate_ref, out_ref, scratch, after_line, after_all):
    own, side, mine, line, back, done, sends, recvs = scratch
    streams, n, channels = ends.shape
    width = channels // SIDE
    rows = streams * n
    place, group, groups = where.place, where.group, where.groups
    for q in range(SIDE):
        cols = slice(q * width, (q + 1) * width)
        own[q, :rows, :] = ends[:, :, cols].reshape(rows, width)
        own[q, rows : rows + streams, :] = total[:, cols]
        own[q, rows + streams :, :] = jnp.zeros((own.shape[1] - rows - streams, width), jnp.float32)
    sides = [remote(own.at[place ^ k], side.at[k], sends, recvs, k, where.member[k]) for k in range(1, SIDE)]
    for c in sides:
        c.start()
    rate = rate_ref[:, pl.ds(pl.multiple_of(place * width, 128), width)]

    def through(steps):
        return jnp.concatenate([jnp.exp2(steps[s : s + 1] * rate) for s in range(streams)], axis=0)

    side[0] = own[place]
    for c in sides:
        c.wait_recv()
    state, steps = jnp.zeros((rows, width), jnp.float32), jnp.zeros((streams, width), jnp.float32)
    before, passed = [None] * SIDE, [None] * SIDE
    for j in reversed(range(SIDE)) if reverse else range(SIDE):
        block = side[place ^ j]
        before[j], passed[j] = state, steps
        step = block[rows : rows + streams]
        state = through(step) * state + block[:rows]
        steps = steps + step
    mine[:rows, :] = state
    mine[rows : rows + streams, :] = steps
    mine[rows + streams :, :] = jnp.zeros((mine.shape[0] - rows - streams, width), jnp.float32)
    lines = [remote(mine, line.at[k], sends, recvs, SIDE + k, where.other[k]) for k in range(1, groups)]
    for c in lines:
        c.start()
    for c in lines:
        c.wait_recv()
    after_line()
    entering = jnp.zeros((rows, width), jnp.float32)
    for k in range(1, groups) if reverse else range(groups - 1, 0, -1):
        counts = (k > group) if reverse else (k <= group)
        block = line[k]
        new = through(block[rows : rows + streams]) * entering + block[:rows]
        entering = jnp.where(counts, new, entering)
    for j in range(SIDE):
        back[j] = through(passed[j]) * entering + before[j]
    backs = [
        remote(back.at[place ^ k], done.at[k], sends, recvs, SIDE + groups + k, where.member[k]) for k in range(1, SIDE)
    ]
    for c in backs:
        c.start()
    after_all()
    done[0] = back[place]
    for c in backs:
        c.wait_recv()
    for q in range(SIDE):
        out_ref[:, :, q * width : (q + 1) * width] = done[place ^ q].reshape(streams, n, width)
    for c in sides + lines + backs:
        c.wait_send()


def chain_scratch(streams, n, channels, groups):
    width = channels // SIDE
    rows = streams * n
    tall = rows + 8 * (-(-streams // 8))
    sems = pltpu.SemaphoreType.DMA((2 * SIDE + groups,))
    return [
        pltpu.VMEM((SIDE, tall, width), jnp.float32),
        pltpu.VMEM((SIDE, tall, width), jnp.float32),
        pltpu.VMEM((tall, width), jnp.float32),
        pltpu.VMEM((groups, tall, width), jnp.float32),
        pltpu.VMEM((SIDE, rows, width), jnp.float32),
        pltpu.VMEM((SIDE, rows, width), jnp.float32),
        sems,
        sems,
    ]


def sums(fall, total):
    for s in range(fall.shape[0]):
        total[s : s + 1, :] = jnp.sum(fall[s], axis=0, keepdims=True)


def blocks_of(channels):
    lanes = pieces(channels)
    return lanes, channels // lanes


def columns(i, lanes):
    return pl.ds(pl.multiple_of(i * lanes, lanes), lanes)


def forward_kernel(
    count, fall, gain, b_ref, c_ref, rate_ref, up_one, down_one, norm_near, norm_next,
    y_ref, first, ring, ring_rest, side_far, side_rest,
    ends, total, line_send, line_recv, side_send, side_recv, *scratch,
):
    where = Place(count)
    streams, length, channels = fall.shape
    n = rate_ref.shape[0]
    lanes, blocks = blocks_of(channels)
    z = where.z
    where.greet()
    line = Line(where, up_one, down_one, ring, ring_rest, line_send, line_recv)

    def summary(i, _):
        cols = columns(i, lanes)
        rate = rate_ref[:, cols]

        def chunk(i, states):
            base = pl.multiple_of(i * ROWS, ROWS)
            out = []
            for s in range(streams):
                state = states[s]
                d = fall[s, pl.ds(base, ROWS), cols]
                x = gain[s, pl.ds(base, ROWS), cols]
                for j in range(ROWS):
                    b = b_ref[s, pl.ds(pl.multiple_of((base + j) * n, n), n), :]
                    fade = jnp.exp2(d[j : j + 1] * rate)
                    state = fade * state + x[j : j + 1] * wide(b, lanes)
                out.append(state)
            return tuple(out)

        start = tuple(jnp.zeros((n, lanes), jnp.float32) for _ in range(streams))
        states = lax.fori_loop(0, length // ROWS, chunk, start)
        for s in range(streams):
            ends[s, :, cols] = states[s]
        return 0

    lax.fori_loop(0, blocks, summary, 0)
    sums(fall, total)

    half = norm_near.shape[0] // 2
    top, low = pl.ds(0, half), pl.ds(half, half)
    far = [
        remote(norm_next.at[top], side_far.at[top], side_send, side_recv, 0, where.member[1]),
        remote(norm_near.at[low], side_far.at[low], side_send, side_recv, 1, where.member[2]),
    ]
    cores = [
        remote(part, side_rest.at[k], side_send, side_recv, 2 + k, where.core)
        for k, part in enumerate((norm_near, norm_next, side_far))
    ]

    def after_line():
        line.start_cores_of_one()
        line.start(2)

    def after_all():
        for c in far + cores[:2]:
            c.start()

    chain(where, False, ends, total, rate_ref, first, scratch, after_line, after_all)

    def run(i, _):
        cols = columns(i, lanes)
        rate = rate_ref[:, cols]

        @pl.when(i == blocks // 2)
        def _():
            line.arrive(2)
            line.start(3)

        def chunk(i, states):
            base = pl.multiple_of(i * ROWS, ROWS)
            out = []
            for s in range(streams):
                state = states[s]
                d = fall[s, pl.ds(base, ROWS), cols]
                x = gain[s, pl.ds(base, ROWS), cols]
                rows = []
                for j in range(ROWS):
                    at = pl.ds(pl.multiple_of((base + j) * n, n), n)
                    fade = jnp.exp2(d[j : j + 1] * rate)
                    state = fade * state + x[j : j + 1] * wide(b_ref[s, at, :], lanes)
                    rows.append(jnp.sum(state * wide(c_ref[s, at, :], lanes), axis=0, keepdims=True))
                y_ref[s, pl.ds(base, ROWS), cols] = jnp.concatenate(rows, axis=0)
                out.append(state)
            return tuple(out)

        lax.fori_loop(0, length // ROWS, chunk, tuple(first[s, :, cols] for s in range(streams)))
        return 0

    lax.fori_loop(0, blocks, run, 0)
    for c in far:
        c.wait_recv()
    cores[2].start()
    line.arrive(3)
    for c in far:
        c.wait_send()
    for c in cores:
        c.wait()
    line.finish()


def backward_kernel(
    count, fall, d_ref, v_ref, g_ref, b_ref, c_ref, rate_ref, first_ref, up_one, down_one, mix, y_ref,
    dstep_ref, dvalue_ref, db_ref, dc_ref, decay_ref, ring, ring_rest, side, side_rest, y_side,
    ends, total, last, path, fades, line_send, line_recv, side_send, side_recv, y_send, y_recv, *scratch,
):
    where = Place(count)
    streams, length, channels = fall.shape
    n = rate_ref.shape[0]
    lanes, blocks = blocks_of(channels)
    chunks = length // ROWS
    width = channels // SIDE
    where.greet()
    line = Line(where, up_one, down_one, ring, ring_rest, line_send, line_recv)
    square = Side(where, mix, side, side_rest, side_send, side_recv)
    quarters = [
        remote(
            y_ref.at[:, :, pl.ds(pl.multiple_of((where.place ^ k) * width, 128), width)],
            y_side.at[k - 1], y_send, y_recv, k - 1, where.member[k],
        )
        for k in range(1, SIDE)
    ]

    def summary(i, _):
        cols = columns(i, lanes)
        rate = rate_ref[:, cols]

        def chunk(i, carry):
            base = pl.multiple_of((chunks - 1 - i) * ROWS, ROWS)
            out = []
            for s in range(streams):
                carried = carry[s]
                d = fall[s, pl.ds(base, ROWS), cols]
                g = g_ref[s, pl.ds(base, ROWS), cols]
                for j in reversed(range(ROWS)):
                    at = pl.ds(pl.multiple_of((base + j) * n, n), n)
                    fade = jnp.exp2(d[j : j + 1] * rate)
                    carried = fade * (g[j : j + 1] * wide(c_ref[s, at, :], lanes) + carried)
                out.append(carried)
            return tuple(out)

        start = tuple(jnp.zeros((n, lanes), jnp.float32) for _ in range(streams))
        states = lax.fori_loop(0, chunks, chunk, start)
        for s in range(streams):
            ends[s, :, cols] = states[s]
        return 0

    lax.fori_loop(0, blocks, summary, 0)
    sums(fall, total)

    def after_line():
        line.start_cores_of_one()
        line.start(2)

    def after_all():
        square.start()
        for c in quarters:
            c.start()

    chain(where, True, ends, total, rate_ref, last, scratch, after_line, after_all)
    db_ref[...] = jnp.zeros_like(db_ref)
    dc_ref[...] = jnp.zeros_like(dc_ref)

    def fold(tile):
        out = tile[:, :128]
        for k in range(1, lanes // 128):
            out = out + tile[:, k * 128 : (k + 1) * 128]
        return out

    def run(i, _):
        cols = columns(i, lanes)
        rate = rate_ref[:, cols]

        @pl.when(i == blocks // 3)
        def _():
            line.arrive(2)
            line.start(3)

        @pl.when(i == blocks // 2)
        def _():
            square.turn()

        def ahead(i, states):
            base = pl.multiple_of(i * ROWS, ROWS)
            out = []
            for s in range(streams):
                state = states[s]
                d = fall[s, pl.ds(base, ROWS), cols]
                x = d_ref[s, pl.ds(base, ROWS), cols] * v_ref[s, pl.ds(base, ROWS), cols]
                for j in range(ROWS):
                    at = pl.ds(pl.multiple_of((base + j) * n, n), n)
                    path[s, at, :] = state
                    fade = jnp.exp2(d[j : j + 1] * rate)
                    fades[s, at, :] = fade
                    state = fade * state + x[j : j + 1] * wide(b_ref[s, at, :], lanes)
                out.append(state)
            return tuple(out)

        tails = lax.fori_loop(0, chunks, ahead, tuple(first_ref[s, :, cols] for s in range(streams)))

        def back(i, carry):
            base = pl.multiple_of((chunks - 1 - i) * ROWS, ROWS)
            out = []
            decay = carry[-1]
            for s in range(streams):
                state, carried = carry[s]
                d = d_ref[s, pl.ds(base, ROWS), cols]
                v = v_ref[s, pl.ds(base, ROWS), cols]
                g = g_ref[s, pl.ds(base, ROWS), cols]
                x = d * v
                weights, touches = [None] * ROWS, [None] * ROWS
                for j in reversed(range(ROWS)):
                    at = pl.ds(pl.multiple_of((base + j) * n, n), n)
                    gj = g[j : j + 1]
                    adjoint = gj * wide(c_ref[s, at, :], lanes) + carried
                    dc_ref[s, at, :] += fold(state * gj)
                    db_ref[s, at, :] += fold(adjoint * x[j : j + 1])
                    weights[j] = jnp.sum(adjoint * wide(b_ref[s, at, :], lanes), axis=0, keepdims=True)
                    carried = adjoint * fades[s, at, :]
                    state = path[s, at, :]
                    touch = carried * state
                    touches[j] = jnp.sum(touch * rate, axis=0, keepdims=True)
                    decay = decay + touch * d[j : j + 1]
                weighted = jnp.concatenate(weights, axis=0)
                at = pl.ds(base, ROWS)
                dstep_ref[s, at, cols] = weighted * v + jnp.concatenate(touches, axis=0) * LN2
                dvalue_ref[s, at, cols] = weighted * d
                out.append((state, carried))
            return tuple(out) + (decay,)

        start = tuple((tails[s], last[s, :, cols]) for s in range(streams))
        done = lax.fori_loop(0, chunks, back, start + (jnp.zeros((n, lanes), jnp.float32),))
        decay_ref[:, cols] = done[-1]
        return 0

    lax.fori_loop(0, blocks, run, 0)
    square.finish()
    line.arrive(3)
    for c in quarters:
        c.wait()
    line.finish()


def in_vmem():
    return pl.BlockSpec(memory_space=pltpu.VMEM)


def in_hbm():
    return pl.BlockSpec(memory_space=pl.ANY)


def shaped(*shape):
    return jax.ShapeDtypeStruct(shape, jnp.float32)


def sems(count):
    return [pltpu.SemaphoreType.DMA((count,))] * 2


def scan_forward(fall, gain, b_wide, c_wide, rate, line, norm_near, norm_next):
    streams, length, channels = fall.shape
    n = rate.shape[0]
    count = lax.axis_size("seq")
    half, width = norm_near.shape
    three = shaped(SIDE - 1, half, width)
    return pl.pallas_call(
        functools.partial(forward_kernel, count),
        out_shape=[shaped(streams, length, channels), shaped(streams, n, channels), three, three, shaped(half, width), three],
        in_specs=[in_vmem()] * 5 + [in_hbm()] * 4,
        out_specs=[in_vmem()] * 2 + [in_hbm()] * 4,
        scratch_shapes=[pltpu.VMEM((streams, n, channels), jnp.float32), pltpu.VMEM((streams, channels), jnp.float32)]
        + sems(LINE_SEMS) + sems(5)
        + chain_scratch(streams, n, channels, count // SIDE),
        compiler_params=pltpu.CompilerParams(
            collective_id=0, has_side_effects=True, vmem_limit_bytes=40 * 1024 * 1024
        ),
        cost_estimate=spans(40),
    )(fall, gain, b_wide, c_wide, rate, *line, norm_near, norm_next)


def scan_backward(fall, step, value, d_y, b_wide, c_wide, rate, first, line, mix, y):
    streams, length, channels = fall.shape
    n = rate.shape[0]
    count = lax.axis_size("seq")
    half, width = mix.shape
    lanes, _ = blocks_of(channels)
    three = shaped(SIDE - 1, half, width)
    tall = shaped(streams, length * n, 128)
    flat = shaped(streams, length, channels)
    kept = pltpu.VMEM((streams, length * n, lanes), jnp.float32)
    return pl.pallas_call(
        functools.partial(backward_kernel, count),
        out_shape=[flat, flat, tall, tall, shaped(n, channels), three, three, three, three,
                   shaped(SIDE - 1, streams, length, channels // SIDE)],
        in_specs=[in_vmem()] * 8 + [in_hbm()] * 4,
        out_specs=[in_vmem()] * 5 + [in_hbm()] * 5,
        scratch_shapes=[
            pltpu.VMEM((streams, n, channels), jnp.float32),
            pltpu.VMEM((streams, channels), jnp.float32),
            pltpu.VMEM((streams, n, channels), jnp.float32),
            kept,
            kept,
        ]
        + sems(LINE_SEMS) + sems(SIDE_SEMS) + sems(SIDE - 1)
        + chain_scratch(streams, n, channels, count // SIDE),
        compiler_params=pltpu.CompilerParams(
            collective_id=1, has_side_effects=True, vmem_limit_bytes=52 * 1024 * 1024
        ),
        cost_estimate=spans(62),
    )(fall, step, value, d_y, b_wide, c_wide, rate, first, *line, mix, y)


CHUNKS = 4


def place_step_one(target, own, z, up, down):
    rows = up.shape[0]

    @pl.when(z >= 1)
    def _():
        target[own + (SIDE - 2) * rows : own + (SIDE - 1) * rows, :] = up[...].astype(target.dtype)

    @pl.when(z <= SIDE - 2)
    def _():
        target[own : own + rows, :] = down[...].astype(target.dtype)


def ffn_kernel(
    count, hid_own, hid_ring, hid_rest, hid_up, hid_down, grad_own, grad_ring, grad_rest, grad_up, grad_down, wg, wu, wd, dg_own, du_own, act_own,
    got, inner, mixer,
    out, passed, d_side, near,
    hid, grad, hid_cut, grad_cut, dg, du, act, sent, stash, sends, recvs, local,
):
    own, cut = hid_own.shape[0], hid_cut.shape[0]
    where = Place(count)
    z, place = where.z, where.place
    width = d_side.shape[-1]
    first = pl.program_id(0) == 0
    last = pl.program_id(0) == pl.num_programs(0) - 1
    quarters = [
        remote(
            inner.at[:, :, pl.ds(pl.multiple_of((place ^ k) * width, 128), width)],
            d_side.at[k - 1], sends, recvs, k - 1, where.member[k],
        )
        for k in range(1, SIDE)
    ]
    rising = z < SIDE // 2
    step = remote(
        sent, passed.at[jnp.where(rising, 0, 1)], sends, recvs, jnp.where(rising, SIDE - 1, SIDE),
        (jnp.where(rising, where.above[0], where.below[0]), where.head),
    )
    from_below = remote(sent, passed.at[0], sends, recvs, SIDE - 1, where.above)
    from_above = remote(sent, passed.at[1], sends, recvs, SIDE, where.below)
    middle = (z > 0) & (z < SIDE - 1)
    odd, far = lax.rem(place, 2), place // 2
    early = [
        remote(stash.at[0, :, :, :, 1 - odd], near.at[0], sends, recvs, SIDE + 1, where.member[1]),
        remote(stash.at[1, :, :, 1 - far], near.at[1], sends, recvs, SIDE + 2, where.member[2]),
    ]
    turns = pl.num_programs(0) // CHUNKS

    @pl.when(first)
    def _():
        where.greet()
        for c in quarters:
            c.start()
        fetch = pltpu.make_async_copy(mixer.at[:, lax.rem(z + 2, SIDE)], sent, local.at[0])
        fetch.start()
        stack_tokens(hid, hid_own, [hid_ring, hid_rest])
        place_step_one(hid, own, z, hid_up, hid_down)
        fetch.wait()

        @pl.when(middle)
        def _():
            sent[...] += got[...]

        step.start()
        stack_tokens(grad, grad_own, [grad_ring, grad_rest])
        place_step_one(grad, own, z, grad_up, grad_down)
        at = pl.ds(pl.multiple_of(z * cut, 128), cut)
        hid_cut[...] = hid[:, at].T
        grad_cut[...] = grad[:, at].T

    dg[:own, :] = dg_own[...]
    du[:own, :] = du_own[...]
    act[:own, :] = act_own[...]

    def turn(i, _):
        rows = pl.ds(pl.multiple_of(i * own, own), own)
        gate = dot(hid[rows, :], wg[...])
        up = dot(hid[rows, :], wu[...])
        d_act = dot_back(grad[rows, :], wd[...])
        sig = 1.0 / (1.0 + jnp.exp(-gate))
        silu = gate * sig
        dg[rows, :] = (d_act * up * (sig + silu * (1.0 - sig))).astype(dg.dtype)
        du[rows, :] = (d_act * silu).astype(du.dtype)
        act[rows, :] = (silu * up).astype(act.dtype)
        return 0

    lax.fori_loop(1, hid.shape[0] // own, turn, 0)
    out[0] = dot(hid_cut[...], dg[...])
    out[1] = dot(hid_cut[...], du[...])
    out[2] = dot(grad_cut[...], act[...])

    @pl.when(pl.program_id(0) < 2 * turns)
    def _():
        block = out.shape[2]
        at = pl.ds(pl.multiple_of(lax.rem(pl.program_id(0), turns) * block, block), block)
        for m in range(3):
            stash[pl.program_id(0) // turns, m, :, :, :, :, at] = out[m].reshape(stash.shape[2:6] + (block,))

    for c in range(2):
        pl.when(pl.program_id(0) == (c + 1) * turns - 1)(early[c].start)

    @pl.when(last)
    def _():
        for c in quarters + early:
            c.wait()
        step.wait_send()

        @pl.when(middle)
        def _():
            from_below.wait_recv()
            from_above.wait_recv()


def ffn_grads(hid_own, hid_ring, hid_rest, hid_one, grad_own, grad_ring, grad_rest, grad_one, w_gate, w_up, w_down, d_gate, d_up, act, got, inner, mixer):
    own, width = hid_own.shape
    units = w_gate.shape[1]
    count = lax.axis_size("seq")
    cut = width // SIDE
    streams, length, channels = inner.shape
    block = next(b for b in (256, 128) if units % (b * CHUNKS) == 0)
    more = count // SIDE // SIDE
    rows = cut // (more * SIDE)
    tokens = own * SIDE
    low = jnp.bfloat16
    column = lambda rows: pl.BlockSpec((rows, block), lambda i: (0, i))
    tokens_in = (hid_own, hid_ring, hid_rest, *hid_one, grad_own, grad_ring, grad_rest, *grad_one)
    return pl.pallas_call(
        functools.partial(ffn_kernel, count),
        grid=(units // block,),
        in_specs=[whole(a.shape) for a in tokens_in]
        + [column(width), column(width), pl.BlockSpec((block, width), lambda i: (i, 0))]
        + [column(own)] * 3
        + [whole(got.shape), in_hbm(), in_hbm()],
        out_specs=[pl.BlockSpec((3, cut, block), lambda i: (0, 0, i))] + [in_hbm()] * 3,
        out_shape=[
            shaped(3, cut, units), shaped(2, *got.shape), shaped(SIDE - 1, streams, length, channels // SIDE),
            shaped(2, 3, more, 2, rows, units // CHUNKS),
        ],
        scratch_shapes=[pltpu.VMEM((tokens, width), low)] * 2
        + [pltpu.VMEM((cut, tokens), low)] * 2
        + [pltpu.VMEM((tokens, block), low)] * 3
        + [pltpu.VMEM(got.shape, jnp.float32), pltpu.VMEM((2, 3, more, 2, 2, rows, units // CHUNKS), jnp.float32)]
        + sems(SIDE + 3) + [pltpu.SemaphoreType.DMA((1,))],
        compiler_params=pltpu.CompilerParams(
            collective_id=2, has_side_effects=True, vmem_limit_bytes=56 * 1024 * 1024
        ),
        cost_estimate=spans(36),
    )(*tokens_in, w_gate, w_up, w_down, d_gate, d_up, act, got, inner, mixer)


class Reduce:
    def __init__(self, where, blocks, got, passed, arrived, sends, recvs):
        self.where, self.blocks, self.got, self.passed, self.arrived = where, blocks, got, passed, arrived
        self.sends, self.recvs = sends, recvs

    def out(self, source, target, at, rising):
        w = self.where
        return remote(source, target, self.sends, self.recvs, at, (jnp.where(rising, w.above[0], w.below[0]), w.head))

    def one(self):
        return self.out(self.blocks.at[:, SIDE - 1 - self.where.z], self.got, 0, self.where.z == 0)

    def start_one(self):
        pl.when((self.where.z == 0) | (self.where.z == SIDE - 1))(self.one().start)

    def middle(self):
        return (self.where.z > 0) & (self.where.z < SIDE - 1)

    def two(self, source):
        rising = self.where.z < SIDE // 2
        return self.out(source, self.passed.at[jnp.where(rising, 0, 1)], jnp.where(rising, 1, 2), rising)

    def start_two(self):
        z = self.where.z

        @pl.when(self.middle())
        def _():
            self.one().wait_recv()
            self.got[...] += self.blocks[:, lax.rem(z + 2, SIDE)]
            self.two(self.got).start()

        @pl.when(jnp.logical_not(self.middle()))
        def _():
            self.two(self.blocks.at[:, lax.rem(z + 2, SIDE)]).start()

    def three(self, source, way):
        return self.out(source, self.arrived.at[way], 3 + way, way == 0)

    def start_three(self, wait):
        z = self.where.z

        @pl.when(self.middle())
        def _():
            for way in (0, 1):
                if wait:
                    self.two_from(way).wait_recv()
                self.passed[way] += self.blocks[:, z + 1 - 2 * way]
                self.three(self.passed.at[way], way).start()

        pl.when(z == 0)(self.three(self.blocks.at[:, 1], 0).start)
        pl.when(z == SIDE - 1)(self.three(self.blocks.at[:, SIDE - 2], 1).start)

    def two_from(self, way):
        return self.out(self.passed.at[way], self.passed.at[way], 1 + way, way == 0)

    def result(self, done):
        z = self.where.z
        done[...] = self.blocks[:, z].reshape(done.shape)
        for way in (0, 1):

            @pl.when((z >= 1) if way == 0 else (z <= SIDE - 2))
            def _():
                self.three(self.passed.at[way], way).wait_recv()
                done[...] += self.arrived[way].reshape(done.shape)

    def finish(self, first):
        z = self.where.z
        if first <= 1:
            pl.when((z == 0) | (z == SIDE - 1))(self.one().wait_send)
        if first <= 2:
            self.two(self.got).wait_send()
        pl.when(z <= SIDE - 2)(self.three(self.passed.at[0], 0).wait_send)
        pl.when(z >= 1)(self.three(self.passed.at[1], 1).wait_send)


REDUCE_SEMS = 5


def sum_kernel(
    count, ffn, mixer_in, passed_in, near_in, turned, d_own, d_side, small,
    ffn_out, mixer_out, inner_out, small_out,
    d_all, kept, near, next_, mixer, m_passed, m_arrived, inner, i_got, i_passed, i_arrived, m_done, m_back, i_done, i_back, s_near, s_next, s_done, s_line,
    ffn_send, ffn_recv, m_send, m_recv, i_send, i_recv, back_send, back_recv, s_send, s_recv, local,
):
    where = Place(count)
    place = where.place
    more = where.stride // SIDE
    span = near.shape[5]
    odd, far = lax.rem(place, 2), place // 2
    cols = [pl.ds(c * span, span) for c in range(CHUNKS)]
    loads = [pltpu.make_async_copy(mixer_in, mixer, local.at[0]), pltpu.make_async_copy(passed_in, m_passed, local.at[1])]
    keeps = [
        pltpu.make_async_copy(
            ffn.at[:, :, :, odd, :, cols[c]] if c % 2 == 0 else ffn.at[:, :, far, :, :, cols[c]], kept.at[c], local.at[2 + c]
        )
        for c in range(CHUNKS)
    ]
    nears = [pltpu.make_async_copy(near_in.at[c], near.at[c], local.at[2 + CHUNKS + c]) for c in range(2)]
    for c in loads + nears + keeps:
        c.start()
    where.greet()
    first = {
        c: remote(
            ffn.at[:, :, :, 1 - odd, :, cols[c]] if c % 2 == 0 else ffn.at[:, :, 1 - far, :, :, cols[c]],
            near.at[c], ffn_send, ffn_recv, c, where.member[1 + c % 2],
        )
        for c in range(2, CHUNKS)
    }
    for c in first.values():
        c.start()
    groups, half = where.groups, s_near.shape[3]
    s_rows = [pl.ds(0, half), pl.ds(half, half)]
    s_first = [
        remote(small.at[:, :, 1 - odd, s_rows[0]], s_near.at[0], s_send, s_recv, 0, where.member[1]),
        remote(small.at[:, 1 - far, :, s_rows[1]], s_near.at[1], s_send, s_recv, 1, where.member[2]),
    ]
    for c in s_first:
        c.start()
    second = {}

    def again(c):
        kept[c] += near[c]
        bit = far if c % 2 == 0 else odd
        second[c] = remote(
            kept.at[c, :, :, 1 - bit], next_.at[c], ffn_send, ffn_recv, CHUNKS + c, where.member[2 - c % 2]
        )
        second[c].start()

    line = Reduce(where, mixer, None, m_passed, m_arrived, m_send, m_recv)
    for c in loads:
        c.wait()
    line.start_three(False)
    for c in range(2):
        nears[c].wait()
        keeps[c].wait()
        again(c)
    own = d_own.shape[0]
    part = own // 2
    d_all[:own, :] = d_own[...]
    for k in range(SIDE - 1):
        for s in range(2):
            start = own + (s * (SIDE - 1) + k) * part
            d_all[start : start + part, :] = d_side[k, where.head if s == 0 else 1 - where.head].astype(d_all.dtype)
    for k in range(SIDE):
        at = slice(k * inner.shape[2], (k + 1) * inner.shape[2])
        inner[0, k] = dot(turned[at, :], d_all[...])
    other = Reduce(where, inner, i_got, i_passed, i_arrived, i_send, i_recv)
    other.start_one()
    other.start_two()
    for c in s_first:
        c.wait_recv()
    s_near[0] += small[:, :, odd, s_rows[0]]
    s_near[1] += small[:, far, :, s_rows[1]]
    s_second = [
        remote(s_near.at[0, :, 1 - far], s_next.at[0], s_send, s_recv, 2, where.member[2]),
        remote(s_near.at[1, :, 1 - odd], s_next.at[1], s_send, s_recv, 3, where.member[1]),
    ]
    for c in s_second:
        c.start()
    for c in range(2, CHUNKS):
        keeps[c].wait()
        first[c].wait_recv()
        again(c)
    for c in s_second:
        c.wait_recv()
    s_done[:, :half] = s_near[0, :, far] + s_next[0]
    s_done[:, half:] = s_near[1, :, odd] + s_next[1]
    s_last = [
        remote(s_done.at[lax.rem(where.group + k, groups)], s_line.at[k], s_send, s_recv, 3 + k, where.other[k])
        for k in range(1, groups)
    ]
    for c in s_last:
        c.start()
    other.start_three(True)

    def spread(reduced, done, back, at):
        reduced.result(done)
        copies = [
            remote(done.at[:, :, place ^ k], back.at[k], back_send, back_recv, at + k, where.member[k])
            for k in range(1, SIDE)
        ]
        for c in copies:
            c.start()
        back[0] = done[:, :, place]
        return copies

    spreads = spread(line, m_done, m_back, 0)
    for c in range(CHUNKS):
        second[c].wait_recv()
        bit = far if c % 2 == 0 else odd
        ffn_out[:, :, :, c * span : (c + 1) * span] = kept[c, :, :, bit] + next_[c]
    spreads += spread(other, i_done, i_back, SIDE)
    for c in spreads:
        c.wait_recv()
    width = inner.shape[3]
    for q in range(SIDE):
        cols = slice(q * width, (q + 1) * width)
        mixer_out[:, :, :, cols] = m_back[place ^ q]
        inner_out[:, :, :, cols] = i_back[place ^ q]
    total = s_done[where.group]
    for k in range(1, groups):
        s_last[k - 1].wait_recv()
        total = total + s_line[k]
    small_out[...] = total
    for c in list(first.values()) + list(second.values()) + spreads + s_first + s_second + s_last:
        c.wait_send()
    line.finish(3)
    other.finish(1)


def sum_grads(ffn, mixer, passed, near, turned, d_own, d_side, small):
    count = lax.axis_size("seq")
    more = count // SIDE // SIDE
    cut, units = ffn.shape[1:]
    rows = cut // (more * SIDE)
    size = mixer.shape[-1]
    f32 = jnp.float32
    v = lambda *shape: pltpu.VMEM(shape, f32)
    groups, tall = count // SIDE, small.shape[1]
    return pl.pallas_call(
        functools.partial(sum_kernel, count),
        out_shape=[shaped(3, more, rows, units), shaped(2, more, rows, size * SIDE), shaped(1, more, rows, size * SIDE),
                   shaped(tall, LANES)],
        in_specs=[in_hbm()] * 4 + [in_vmem()] * 4,
        out_specs=[in_vmem()] * 4,
        scratch_shapes=[
            pltpu.VMEM((turned.shape[1], size), jnp.bfloat16),
            v(CHUNKS, 3, more, 2, rows, units // CHUNKS),
            v(CHUNKS, 3, more, 2, rows, units // CHUNKS),
            v(CHUNKS, 3, more, rows, units // CHUNKS),
            v(2, SIDE, cut, size), v(2, 2, cut, size), v(2, 2, cut, size),
            v(1, SIDE, cut, size), v(1, cut, size), v(2, 1, cut, size), v(2, 1, cut, size),
            v(2, more, SIDE, rows, size), v(SIDE, 2, more, rows, size),
            v(1, more, SIDE, rows, size), v(SIDE, 1, more, rows, size),
            v(2, groups, 2, tall // 2, LANES), v(2, groups, tall // 2, LANES), v(groups, tall, LANES), v(groups, tall, LANES),
        ]
        + sems(2 * CHUNKS) + sems(REDUCE_SEMS) + sems(REDUCE_SEMS) + sems(2 * SIDE) + sems(3 + groups) + [pltpu.SemaphoreType.DMA((4 + CHUNKS,))],
        compiler_params=pltpu.CompilerParams(
            collective_id=3, has_side_effects=True, vmem_limit_bytes=58 * 1024 * 1024
        ),
        cost_estimate=spans(100),
    )(ffn.reshape(3, more, 2, 2, rows, units), mixer, passed, near, turned, d_own, d_side, small.reshape(groups, 2, 2, tall, LANES))


LANES = 128


def gather_kernel(places, w_step, log_decay, taps, rows, select, out):
    ranks, states, taps_n = w_step.shape[0], log_decay.shape[0], taps.shape[0]
    size = w_step.shape[1] // places
    high = select.shape[0] // places
    low = ranks + states + 16
    out[...] = jnp.zeros_like(out)
    for p in range(places):
        cols = slice(p * size, (p + 1) * size)
        out[p, :ranks, :size] = w_step[:, cols]
        out[p, ranks : ranks + states, :size] = log_decay[:, cols]
        at = ranks + states
        out[p, at : at + 8, :size] = jnp.concatenate([taps[:, cols], rows[: 8 - taps_n, cols]], axis=0)
        out[p, at + 8 : at + 16, :size] = rows[8 - taps_n : 16 - taps_n, cols]
        for b in range(select.shape[1] // LANES):
            out[p, low + b * high : low + (b + 1) * high, :] = select[
                p * high : (p + 1) * high, b * LANES : (b + 1) * LANES
            ]


def gather_small(w_step, log_decay, taps, rows, select):
    places = lax.axis_size("seq")
    channels = w_step.shape[1]
    tall = w_step.shape[0] + log_decay.shape[0] + 16 + select.shape[0] // places * (channels // LANES)
    tall = -(-tall // 16) * 16
    return pl.pallas_call(
        functools.partial(gather_kernel, places),
        out_shape=shaped(places, tall, LANES),
        in_specs=[in_vmem()] * 5,
        out_specs=in_vmem(),
        compiler_params=params(24),
        cost_estimate=spans(4),
    )(w_step, log_decay, taps, rows, select)


epsilon = 1e-06
CUT = 1e6


def links(step, wrap=False, axis="seq"):
    n = lax.axis_size(axis)
    return [(i, (i + step) % n) for i in range(n) if wrap or 0 <= i + step < n]


def swaps(bit, axis="seq"):
    return [(i, i ^ bit) for i in range(lax.axis_size(axis))]


def send(block, route, axis="seq"):
    return lax.ppermute(block, axis, route)


def head_sum(part):
    return part + send(part, swaps(1, "head"), "head")


def own_stream(block):
    return lax.dynamic_index_in_dim(block, lax.axis_index("head"), 0, keepdims=False)


def part_of(block, index, size, axis):
    return lax.dynamic_slice_in_dim(block, index * size, size, axis)


def after(block, *earlier):
    return lax.optimization_barrier((block,) + earlier)[0]


def matmul(left, right):
    return jnp.dot(left, right, preferred_element_type=jnp.float32)


def matmul_back(left, right):
    return lax.dot_general(
        left, right, (((left.ndim - 1,), (1,)), ((), ())), preferred_element_type=jnp.float32
    )


def weight_outer(left, right):
    axes = tuple(range(left.ndim - 1))
    return lax.dot_general(left, right, ((axes, axes), ((), ())), preferred_element_type=jnp.float32)


def norm_forward(v, gain):
    scale = lax.rsqrt(jnp.mean(v * v, axis=-1, keepdims=True) + epsilon)
    return (v * scale * gain, scale)


def norm_backward(v, scale, gain, upstream):
    weighted = upstream * gain
    d_input = scale * weighted - v * scale * scale * scale * jnp.mean(
        weighted * v, axis=-1, keepdims=True
    )
    d_gain = jnp.sum(upstream * v * scale, axis=(0, 1))
    return (d_input, d_gain)


def silu_slope(v):
    sig = jax.nn.sigmoid(v)
    return sig + v * sig * (1.0 - sig)


def across(small):
    streams, length, n = small.shape
    return jnp.broadcast_to(small.reshape(streams, length * n, 1), (streams, length * n, 128))


def along(wide_sum, n):
    streams, rows, _ = wide_sum.shape
    return jnp.sum(wide_sum, axis=-1).reshape(streams, rows // n, n)


def body(
    tokens, doc_ids, out_grad, norm_mix, w_inner, w_outgate, conv_taps, conv_bias, w_select, select_gain,
    w_step, step_bias, log_decay, skip_gain, w_mixout, norm_ffn, w_gate, w_up, w_down,
):
    streams, length, width = tokens.shape
    channels = w_inner.shape[1]
    taps = conv_taps.shape[0]
    rank = w_step.shape[0]
    states = log_decay.shape[1]
    lead = taps - 1
    count = lax.axis_size("seq")
    stride = count // SIDE
    here = lax.axis_index("seq")
    z, place = here // stride, here % SIDE
    low = jnp.bfloat16

    grad_in = out_grad.astype(jnp.float32)
    source = tokens.astype(jnp.float32)
    rim_ids = jnp.broadcast_to((doc_ids[:, length - lead :] + 1).astype(jnp.float32)[:, :, None], (streams, lead, 128))
    rim = send(jnp.concatenate([source[:, length - lead :], rim_ids], axis=2), links(1))
    mine_grad, source, rim = lax.optimization_barrier((own_stream(out_grad).astype(jnp.float32), source, rim))
    line_grad = [send(mine_grad, links(stride)), send(mine_grad, links(-stride))]
    normed, scale_mix = norm_forward(source, norm_mix)
    normed_low = normed.astype(low)
    mine_normed = own_stream(normed)
    norm_near, norm_next = send(mine_normed, swaps(1)), send(mine_normed, swaps(2))
    rim_normed, _ = norm_forward(rim[:, :, :width], norm_mix)
    ext_val = matmul(jnp.concatenate([rim_normed.astype(low), normed_low], axis=1), w_inner)
    outgate = matmul(normed_low, w_outgate)
    ext_ids = jnp.concatenate([rim[:, :, width].astype(jnp.int32) - 1, doc_ids], axis=1)
    masks = [
        (ext_ids[:, k : k + length] == doc_ids).astype(jnp.float32)[:, :, None] for k in range(taps)
    ]
    value_pre = conv_bias
    for k in range(taps):
        value_pre = value_pre + conv_taps[k] * ext_val[:, k : k + length] * masks[k]
    value = jax.nn.silu(value_pre)
    value_low = value.astype(low)
    select = head_sum(matmul(value_low, w_select))
    raw_step = select[..., :rank]
    raw_b = select[..., rank : rank + states]
    raw_c = select[..., rank + states :]
    step_n, step_scale = norm_forward(raw_step, select_gain[:rank])
    bsel, b_scale = norm_forward(raw_b, select_gain[rank : rank + states])
    csel, c_scale = norm_forward(raw_c, select_gain[rank + states :])
    step_low = step_n.astype(low)
    step_pre = matmul(step_low, w_step) + step_bias
    step = jax.nn.softplus(step_pre)
    keep = doc_ids == ext_ids[:, lead - 1 : lead - 1 + length]
    fall = jnp.where(keep[:, :, None], step, CUT)
    gain = step * value
    decay_rate = -jnp.exp(log_decay).T
    rate = decay_rate * LOG2E
    b_wide, c_wide = across(bsel), across(csel)
    outs, first, grad_ring, grad_rest, side_far, side_rest = scan_forward(
        fall, gain, b_wide, c_wide, rate, line_grad, norm_near, norm_next
    )
    y = outs + skip_gain * value
    gate_z = jax.nn.silu(outgate)
    mixed = y * gate_z
    mixed_low = mixed.astype(low)
    mix = head_sum(matmul(mixed_low, w_mixout))
    resid = source + mix
    hidden, scale_ffn = norm_forward(resid, norm_ffn)
    hidden_low = hidden.astype(low)
    mine_hidden = own_stream(hidden)
    line_hidden = [send(mine_hidden, links(stride)), send(mine_hidden, links(-stride))]
    gate = matmul(hidden_low, w_gate)
    up = matmul(hidden_low, w_up)
    act_low = (jax.nn.silu(gate) * up).astype(low)
    ffn = head_sum(matmul(act_low, w_down))
    output = (resid + ffn).astype(low)
    d_act = matmul_back(out_grad, w_down)
    d_gate = (d_act * up * silu_slope(gate)).astype(low)
    d_up = (d_act * jax.nn.silu(gate)).astype(low)
    d_hidden = head_sum(matmul_back(d_gate, w_gate) + matmul_back(d_up, w_up))
    d_resid_norm, grad_norm_ffn = norm_backward(resid, scale_ffn, norm_ffn, d_hidden)
    d_resid = grad_in + d_resid_norm
    d_mix = d_resid.astype(low)
    d_mixed = matmul_back(d_mix, w_mixout)
    d_y = d_mixed * gate_z
    d_outgate = (d_mixed * y * silu_slope(outgate)).astype(low)
    grad_skip_gain = jnp.sum(d_y * value, axis=(0, 1))
    d_step, d_scan, db_wide, dc_wide, decay_sum, hid_ring, hid_rest, mix_side, mix_rest, y_side = scan_backward(
        fall, step, value, d_y, b_wide, c_wide, rate, first, line_hidden, own_stream(d_resid), y
    )

    flat = lambda block: block.reshape(-1, block.shape[-1])
    size = channels // SIDE
    mixer, turned = mixer_grads(
        flat(normed_low), [norm_near, norm_next, side_far, side_rest], flat(d_mix), [mix_side, mix_rest],
        flat(part_of(y, place, size, 2)), y_side,
        w_outgate, w_mixout,
    )
    mixer = mixer.reshape(2, SIDE, width // SIDE, size)
    got = send(mixer[:, SIDE - 1], [(i, i + stride) for i in range(stride)]) + send(
        mixer[:, 0], [(i, i - stride) for i in range(count - stride, count)]
    )
    d_step = after(d_step, mixer)

    d_value = d_y * skip_gain + d_scan
    d_step_pre = (d_step * jax.nn.sigmoid(step_pre)).astype(low)
    grad_step_bias = jnp.sum(d_step_pre, axis=(0, 1), dtype=jnp.float32)
    grad_w_step = weight_outer(step_low, d_step_pre)
    d_small = head_sum(
        jnp.concatenate(
            [matmul_back(d_step_pre, w_step), along(db_wide, states), along(dc_wide, states)], axis=-1
        )
    )
    d_raw_step, gain_step = norm_backward(
        raw_step, step_scale, select_gain[:rank], d_small[..., :rank]
    )
    d_raw_b, gain_b = norm_backward(
        raw_b, b_scale, select_gain[rank : rank + states], d_small[..., rank : rank + states]
    )
    d_raw_c, gain_c = norm_backward(
        raw_c, c_scale, select_gain[rank + states :], d_small[..., rank + states :]
    )
    grad_select_gain = jnp.concatenate([gain_step, gain_b, gain_c])
    d_select = jnp.concatenate([d_raw_step, d_raw_b, d_raw_c], axis=-1).astype(low)
    grad_w_select = weight_outer(d_select, value_low)
    d_value = d_value + matmul_back(d_select, w_select)
    d_value_pre = d_value * silu_slope(value_pre)
    grad_conv_bias = jnp.sum(d_value_pre, axis=(0, 1))
    tap_grads = []
    d_ext = jnp.zeros_like(ext_val)
    for k in range(taps):
        masked = d_value_pre * masks[k]
        tap_grads.append(jnp.sum(masked * ext_val[:, k : k + length], axis=(0, 1)))
        d_ext = d_ext + jnp.pad(masked * conv_taps[k], ((0, 0), (k, lead - k), (0, 0)))
    grad_conv_taps = jnp.stack(tap_grads)
    rim_grad = send(d_ext[:, :lead], links(-1))
    d_inner = (d_ext[:, lead:] + jnp.pad(rim_grad, ((0, 0), (length - lead, 0), (0, 0)))).astype(low)
    d_normed = head_sum(matmul_back(d_inner, w_inner) + matmul_back(d_outgate, w_outgate))
    d_source, grad_norm_mix = norm_backward(source, scale_mix, norm_mix, d_normed)
    tokens_grad = d_resid + d_source

    pad = lambda v: jnp.pad(v, (0, channels - v.shape[0]))
    rows = [grad_conv_bias, grad_step_bias, grad_skip_gain, pad(grad_norm_mix), pad(grad_norm_ffn)]
    gains = grad_select_gain.reshape(count, -1)
    rows.append(jnp.pad(gains, ((0, 0), (0, channels // count - gains.shape[1]))).reshape(channels))
    rows = jnp.stack(rows + [jnp.zeros_like(grad_conv_bias)] * (16 - taps - len(rows)))
    small = gather_small(grad_w_step, decay_sum * decay_rate, grad_conv_taps, rows, grad_w_select)
    ffn, passed, d_side, near = ffn_grads(
        flat(hidden_low), hid_ring, hid_rest, line_hidden, flat(out_grad), grad_ring, grad_rest, line_grad, w_gate, w_up, w_down,
        flat(d_gate), flat(d_up), flat(act_low), got, d_inner.astype(jnp.float32), mixer,
    )
    ffn, mixer, inner, tall = sum_grads(
        ffn, mixer, passed, near, turned, flat(part_of(d_inner, place, size, 2)), d_side, small
    )
    if count > SIDE * SIDE:
        groups = [[a * stride + b + SIDE * k for k in range(stride // SIDE)] for a in range(SIDE) for b in range(SIDE)]
        ffn, mixer, inner = (
            lax.psum_scatter(part, "seq", scatter_dimension=1, axis_index_groups=groups) for part in (ffn, mixer, inner)
        )
    else:
        ffn, mixer, inner = (part[:, 0] for part in (ffn, mixer, inner))
    at = rank + states
    high = grad_w_select.shape[0] // count
    broad = tall[at + 16 : at + 16 + high * channels // LANES].reshape(channels // LANES, high, LANES)
    broad = jnp.swapaxes(broad, 0, 1).reshape(high, channels)
    tall = tall[:, : channels // count]
    return (
        output,
        tokens_grad,
        tall[at + taps + 3],
        inner[0],
        mixer[0],
        tall[at : at + taps],
        tall[at + taps],
        broad.T,
        tall[at + taps + 5, : gains.shape[1]],
        tall[:rank],
        tall[at + taps + 1],
        tall[rank:at].T,
        tall[at + taps + 2],
        mixer[1].T,
        tall[at + taps + 4],
        ffn[0],
        ffn[1],
        ffn[2].T,
    )


def solution(mesh):
    in_specs = (
        P(None, "seq", None),
        P(None, "seq"),
        P(None, "seq", None),
        P(),
        P(None, "head"),
        P(None, "head"),
        P(None, "head"),
        P("head"),
        P("head", None),
        P(),
        P(None, "head"),
        P("head"),
        P("head", None),
        P("head"),
        P("head", None),
        P(),
        P(None, "head"),
        P(None, "head"),
        P("head", None),
    )
    out_specs = (
        P(None, "seq", None),
        P(None, "seq", None),
        P("seq"),
        P("seq", "head"),
        P("seq", "head"),
        P(None, ("head", "seq")),
        P(("head", "seq")),
        P("head", "seq"),
        P("seq"),
        P(None, ("head", "seq")),
        P(("head", "seq")),
        P(("head", "seq"), None),
        P(("head", "seq")),
        P("head", "seq"),
        P("seq"),
        P("seq", "head"),
        P("seq", "head"),
        P("head", "seq"),
    )
    return jax.shard_map(body, mesh=mesh, in_specs=in_specs, out_specs=out_specs, check_vma=False)
```

```python
import functools
import math

import jax
import jax.numpy as jnp
from jax import lax
from jax.experimental import pallas as pl
from jax.experimental.pallas import tpu as pltpu
from jax.sharding import PartitionSpec as P

LOG2E = math.log2(math.e)
LN2 = math.log(2.0)
ROWS = 8


def params(limit=48):
    return pltpu.CompilerParams(vmem_limit_bytes=limit * 1024 * 1024)


def wide(tile, lanes):
    return jnp.concatenate([tile] * (lanes // tile.shape[1]), axis=1)


def pieces(lanes):
    return next(w for w in (256, 128) if lanes % w == 0)


def spans(us):
    return pl.CostEstimate(flops=int(us * 1.1e8), bytes_accessed=int(us * 3.0e5), transcendentals=0)


def stack_tokens(target, own_ref, more_refs):
    own = own_ref.shape[0]
    target[:own, :] = own_ref[...].astype(target.dtype)
    at = own
    for ref in more_refs:
        parts = [ref[k] for k in range(ref.shape[0])] if len(ref.shape) == 3 else [ref[...]]
        for part in parts:
            target[at : at + part.shape[0], :] = part.astype(target.dtype)
            at += part.shape[0]


def dot(left, right):
    return jnp.dot(left, right, preferred_element_type=jnp.float32)


def dot_back(left, right):
    return lax.dot_general(left, right, (((1,), (1,)), ((), ())), preferred_element_type=jnp.float32)


def whole(shape):
    return pl.BlockSpec(shape, lambda i: (0,) * len(shape), pipeline_mode=pl.Buffered(1))


def mixer_kernel(more_norm, more_mix, *refs):
    at = iter(range(len(refs)))
    take = lambda count: [refs[next(at)] for _ in range(count)]
    (norm_own,), norm_more = take(1), take(more_norm)
    (mix_own,), mix_more = take(1), take(more_mix)
    y_own, y_side = take(2)
    w_out, w_mix = take(2)
    out, norm_turned = take(2)
    norm, mix, mixed, d_out, wo, wm, local = take(7)
    own = norm_own.shape[0]
    half = own // 2

    @pl.when(pl.program_id(0) == 0)
    def _():
        size = wo.shape[1]
        at = pl.ds(pl.multiple_of(lax.rem(lax.axis_index("seq"), SIDE) * size, 128), size)
        loads = [
            pltpu.make_async_copy(w_out.at[:, at], wo, local.at[0]),
            pltpu.make_async_copy(w_mix.at[at], wm, local.at[1]),
        ]
        for c in loads:
            c.start()
        stack_tokens(norm, norm_own, norm_more)
        stack_tokens(mix, mix_own, mix_more)
        for c in loads:
            c.wait()

        def finish(rows, y):
            outgate = dot(norm[rows, :], wo[...])
            d_mixed = dot_back(mix[rows, :], wm[...])
            sig = 1.0 / (1.0 + jnp.exp(-outgate))
            silu = outgate * sig
            mixed[rows, :] = (y * silu).astype(mixed.dtype)
            d_out[rows, :] = (d_mixed * y * (sig + silu * (1.0 - sig))).astype(d_out.dtype)

        finish(slice(0, own), y_own[...])
        sides = y_side.shape[0]
        head = lax.axis_index("head")
        for k in range(sides):
            for s in range(2):
                start = own + (s * sides + k) * half
                finish(slice(start, start + half), y_side[k, head if s == 0 else 1 - head])

    rows = norm_turned.shape[0]
    span = pl.ds(pl.multiple_of(pl.program_id(0) * rows, rows), rows)
    turned = norm[:, span].T
    norm_turned[...] = turned
    out[0] = dot(turned, d_out[...])
    out[1] = dot(mix[:, span].T, mixed[...])


def mixer_grads(norm_own, norm_more, mix_own, mix_more, y_own, y_side, w_out, w_mix):
    own, width = norm_own.shape
    cut = w_out.shape[1] // SIDE
    block = next(b for b in (256, 128) if width % b == 0)
    tokens = own + sum(math.prod(part.shape[:-1]) for part in norm_more)
    low = jnp.bfloat16
    row = lambda columns: pl.BlockSpec((block, columns), lambda i: (i, 0))
    operands = (norm_own, *norm_more, mix_own, *mix_more, y_own, y_side, w_out, w_mix)
    return pl.pallas_call(
        functools.partial(mixer_kernel, len(norm_more), len(mix_more)),
        grid=(width // block,),
        in_specs=[whole(a.shape) for a in operands[:-2]] + [in_hbm()] * 2,
        out_specs=[pl.BlockSpec((2, block, cut), lambda i: (0, i, 0)), row(tokens)],
        out_shape=[
            jax.ShapeDtypeStruct((2, width, cut), jnp.float32),
            jax.ShapeDtypeStruct((width, tokens), low),
        ],
        scratch_shapes=[pltpu.VMEM((tokens, width), low)] * 2
        + [pltpu.VMEM((tokens, cut), low)] * 2
        + [pltpu.VMEM((width, cut), low), pltpu.VMEM((cut, width), low), pltpu.SemaphoreType.DMA((2,))],
        compiler_params=params(40),
        cost_estimate=spans(12),
    )(*operands)


SIDE = 4
MESH = pl.DeviceIdType.MESH


def remote(source, target, sends, recvs, at, device):
    return pltpu.make_async_remote_copy(
        src_ref=source, dst_ref=target, send_sem=sends.at[at], recv_sem=recvs.at[at],
        device_id=device, device_id_type=MESH,
    )


class Place:
    def __init__(self, count):
        here = lax.axis_index("seq")
        self.head = lax.axis_index("head")
        self.stride = count // SIDE
        self.groups = count // SIDE
        self.place, self.group = lax.rem(here, SIDE), here // SIDE
        self.z = here // self.stride
        base = here - self.place
        self.member = [(base + (self.place ^ k), self.head) for k in range(SIDE)]
        self.other = [
            (lax.rem(self.group + k, self.groups) * SIDE + self.place, self.head) for k in range(self.groups)
        ]
        self.core = (here, 1 - self.head)
        self.above = (lax.rem(here + self.stride, count), self.head)
        self.below = (lax.rem(here - self.stride + count, count), self.head)

    def greet(self):
        barrier = pltpu.get_barrier_semaphore()
        devices = self.member[1:] + self.other[1:] + [self.core]
        for device in devices:
            pl.semaphore_signal(barrier, inc=1, device_id=device, device_id_type=MESH)
        pl.semaphore_wait(barrier, len(devices))


class Line:
    def __init__(self, where, up_one, down_one, ring, rest, sends, recvs):
        self.where, self.up_one, self.down_one = where, up_one, down_one
        self.ring, self.rest, self.sends, self.recvs = ring, rest, sends, recvs

    def copies(self, step):
        w = self.where
        up = self.up_one if step == 2 else self.ring.at[SIDE - step]
        down = self.down_one if step == 2 else self.ring.at[step - 2]
        return (
            remote(up, self.ring.at[SIDE - 1 - step], self.sends, self.recvs, step - 1, w.above),
            remote(down, self.ring.at[step - 1], self.sends, self.recvs, SIDE - 2 + step, w.below),
        )

    def core(self, slot):
        return remote(self.ring.at[slot], self.rest.at[slot], self.sends, self.recvs, 2 * SIDE - 2 + slot, self.where.core)

    def start(self, step):
        up, down = self.copies(step)
        z = self.where.z
        pl.when((z >= step - 1) & (z < SIDE - 1))(up.start)
        pl.when((z <= SIDE - step) & (z > 0))(down.start)

    def arrive(self, step):
        up, down = self.copies(step)
        z = self.where.z

        @pl.when(z >= step)
        def _():
            up.wait_recv()
            self.core(SIDE - 1 - step).start()

        @pl.when(z <= SIDE - 1 - step)
        def _():
            down.wait_recv()
            self.core(step - 1).start()

    def cores_of_one(self):
        return (
            remote(self.up_one, self.rest.at[SIDE - 2], self.sends, self.recvs, 2 * SIDE - 2 + SIDE - 2, self.where.core),
            remote(self.down_one, self.rest.at[0], self.sends, self.recvs, 2 * SIDE - 2, self.where.core),
        )

    def start_cores_of_one(self):
        up, down = self.cores_of_one()
        pl.when(self.where.z >= 1)(up.start)
        pl.when(self.where.z <= SIDE - 2)(down.start)

    def finish_two(self):
        z = self.where.z
        up, down = self.copies(2)
        pl.when((z >= 1) & (z < SIDE - 1))(up.wait_send)
        pl.when((z <= SIDE - 2) & (z > 0))(down.wait_send)
        self.core(1).wait()
        pl.when(z >= 1)(self.core(SIDE - 2).wait)
        pl.when(z <= SIDE - 2)(self.core(0).wait)

    def finish(self):
        z = self.where.z
        for step in range(2, SIDE):
            up, down = self.copies(step)
            pl.when((z >= step - 1) & (z < SIDE - 1))(up.wait_send)
            pl.when((z <= SIDE - step) & (z > 0))(down.wait_send)
        for slot in range(SIDE - 1):
            self.core(slot).wait()


LINE_SEMS = 3 * (SIDE - 1)


class Side:
    def __init__(self, where, mine, side, rest, sends, recvs):
        self.where, self.mine, self.side, self.rest, self.sends, self.recvs = where, mine, side, rest, sends, recvs

    def near(self):
        return [
            remote(self.mine, self.side.at[k - 1], self.sends, self.recvs, k - 1, self.where.member[k]) for k in (1, 2)
        ]

    def far(self):
        half = self.side.shape[1] // 2
        top, low = pl.ds(0, half), pl.ds(half, half)
        return [
            remote(self.side.at[1, top], self.side.at[2, top], self.sends, self.recvs, 2, self.where.member[1]),
            remote(self.side.at[0, low], self.side.at[2, low], self.sends, self.recvs, 3, self.where.member[2]),
        ]

    def core(self, slot):
        return remote(self.side.at[slot], self.rest.at[slot], self.sends, self.recvs, 4 + slot, self.where.core)

    def start(self):
        for c in self.near():
            c.start()

    def turn(self):
        for c in self.near():
            c.wait_recv()
        for c in self.far():
            c.start()
        for slot in (0, 1):
            self.core(slot).start()

    def finish(self):
        for c in self.far():
            c.wait_recv()
        self.core(2).start()
        for c in self.near() + self.far():
            c.wait_send()
        for slot in range(3):
            self.core(slot).wait()


SIDE_SEMS = 7


def chain(where, reverse, ends, total, rate_ref, out_ref, scratch, after_line, after_all):
    own, side, mine, line, back, done, sends, recvs = scratch
    streams, n, channels = ends.shape
    width = channels // SIDE
    rows = streams * n
    place, group, groups = where.place, where.group, where.groups
    for q in range(SIDE):
        cols = slice(q * width, (q + 1) * width)
        own[q, :rows, :] = ends[:, :, cols].reshape(rows, width)
        own[q, rows : rows + streams, :] = total[:, cols]
        own[q, rows + streams :, :] = jnp.zeros((own.shape[1] - rows - streams, width), jnp.float32)
    sides = [remote(own.at[place ^ k], side.at[k], sends, recvs, k, where.member[k]) for k in range(1, SIDE)]
    for c in sides:
        c.start()
    rate = rate_ref[:, pl.ds(pl.multiple_of(place * width, 128), width)]

    def through(steps):
        return jnp.concatenate([jnp.exp2(steps[s : s + 1] * rate) for s in range(streams)], axis=0)

    side[0] = own[place]
    for c in sides:
        c.wait_recv()
    state, steps = jnp.zeros((rows, width), jnp.float32), jnp.zeros((streams, width), jnp.float32)
    before, passed = [None] * SIDE, [None] * SIDE
    for j in reversed(range(SIDE)) if reverse else range(SIDE):
        block = side[place ^ j]
        before[j], passed[j] = state, steps
        step = block[rows : rows + streams]
        state = through(step) * state + block[:rows]
        steps = steps + step
    mine[:rows, :] = state
    mine[rows : rows + streams, :] = steps
    mine[rows + streams :, :] = jnp.zeros((mine.shape[0] - rows - streams, width), jnp.float32)
    lines = [remote(mine, line.at[k], sends, recvs, SIDE + k, where.other[k]) for k in range(1, groups)]
    for c in lines:
        c.start()
    for c in lines:
        c.wait_recv()
    after_line()
    entering = jnp.zeros((rows, width), jnp.float32)
    for k in range(1, groups) if reverse else range(groups - 1, 0, -1):
        counts = (k > group) if reverse else (k <= group)
        block = line[k]
        new = through(block[rows : rows + streams]) * entering + block[:rows]
        entering = jnp.where(counts, new, entering)
    for j in range(SIDE):
        back[j] = through(passed[j]) * entering + before[j]
    backs = [
        remote(back.at[place ^ k], done.at[k], sends, recvs, SIDE + groups + k, where.member[k]) for k in range(1, SIDE)
    ]
    for c in backs:
        c.start()
    after_all()
    done[0] = back[place]
    for c in backs:
        c.wait_recv()
    for q in range(SIDE):
        out_ref[:, :, q * width : (q + 1) * width] = done[place ^ q].reshape(streams, n, width)
    for c in sides + lines + backs:
        c.wait_send()


def chain_scratch(streams, n, channels, groups):
    width = channels // SIDE
    rows = streams * n
    tall = rows + 8 * (-(-streams // 8))
    sems = pltpu.SemaphoreType.DMA((2 * SIDE + groups,))
    return [
        pltpu.VMEM((SIDE, tall, width), jnp.float32),
        pltpu.VMEM((SIDE, tall, width), jnp.float32),
        pltpu.VMEM((tall, width), jnp.float32),
        pltpu.VMEM((groups, tall, width), jnp.float32),
        pltpu.VMEM((SIDE, rows, width), jnp.float32),
        pltpu.VMEM((SIDE, rows, width), jnp.float32),
        sems,
        sems,
    ]


def sums(fall, total):
    for s in range(fall.shape[0]):
        total[s : s + 1, :] = jnp.sum(fall[s], axis=0, keepdims=True)


def blocks_of(channels):
    lanes = pieces(channels)
    return lanes, channels // lanes


def columns(i, lanes):
    return pl.ds(pl.multiple_of(i * lanes, lanes), lanes)


def forward_kernel(
    count, fall, gain, b_ref, c_ref, rate_ref, up_one, down_one, norm_near, norm_next,
    y_ref, first, ring, ring_rest, side_far, side_rest,
    ends, total, line_send, line_recv, side_send, side_recv, *scratch,
):
    where = Place(count)
    streams, length, channels = fall.shape
    n = rate_ref.shape[0]
    lanes, blocks = blocks_of(channels)
    z = where.z
    where.greet()
    line = Line(where, up_one, down_one, ring, ring_rest, line_send, line_recv)

    def summary(i, _):
        cols = columns(i, lanes)
        rate = rate_ref[:, cols]

        def chunk(i, states):
            base = pl.multiple_of(i * ROWS, ROWS)
            out = []
            for s in range(streams):
                state = states[s]
                d = fall[s, pl.ds(base, ROWS), cols]
                x = gain[s, pl.ds(base, ROWS), cols]
                for j in range(ROWS):
                    b = b_ref[s, pl.ds(pl.multiple_of((base + j) * n, n), n), :]
                    fade = jnp.exp2(d[j : j + 1] * rate)
                    state = fade * state + x[j : j + 1] * wide(b, lanes)
                out.append(state)
            return tuple(out)

        start = tuple(jnp.zeros((n, lanes), jnp.float32) for _ in range(streams))
        states = lax.fori_loop(0, length // ROWS, chunk, start)
        for s in range(streams):
            ends[s, :, cols] = states[s]
        return 0

    lax.fori_loop(0, blocks, summary, 0)
    sums(fall, total)

    half = norm_near.shape[0] // 2
    top, low = pl.ds(0, half), pl.ds(half, half)
    far = [
        remote(norm_next.at[top], side_far.at[top], side_send, side_recv, 0, where.member[1]),
        remote(norm_near.at[low], side_far.at[low], side_send, side_recv, 1, where.member[2]),
    ]
    cores = [
        remote(part, side_rest.at[k], side_send, side_recv, 2 + k, where.core)
        for k, part in enumerate((norm_near, norm_next, side_far))
    ]

    def after_line():
        line.start_cores_of_one()
        line.start(2)

    def after_all():
        for c in far + cores[:2]:
            c.start()

    chain(where, False, ends, total, rate_ref, first, scratch, after_line, after_all)

    def run(i, _):
        cols = columns(i, lanes)
        rate = rate_ref[:, cols]

        def chunk(i, states):
            base = pl.multiple_of(i * ROWS, ROWS)
            out = []
            for s in range(streams):
                state = states[s]
                d = fall[s, pl.ds(base, ROWS), cols]
                x = gain[s, pl.ds(base, ROWS), cols]
                rows = []
                for j in range(ROWS):
                    at = pl.ds(pl.multiple_of((base + j) * n, n), n)
                    fade = jnp.exp2(d[j : j + 1] * rate)
                    state = fade * state + x[j : j + 1] * wide(b_ref[s, at, :], lanes)
                    rows.append(jnp.sum(state * wide(c_ref[s, at, :], lanes), axis=0, keepdims=True))
                y_ref[s, pl.ds(base, ROWS), cols] = jnp.concatenate(rows, axis=0)
                out.append(state)
            return tuple(out)

        lax.fori_loop(0, length // ROWS, chunk, tuple(first[s, :, cols] for s in range(streams)))
        return 0

    lax.fori_loop(0, blocks, run, 0)
    for c in far:
        c.wait_recv()
    cores[2].start()
    line.arrive(2)
    for c in far:
        c.wait_send()
    for c in cores:
        c.wait()
    line.finish_two()


def backward_kernel(
    count, fall, d_ref, v_ref, g_ref, b_ref, c_ref, rate_ref, first_ref, up_one, down_one, mix, grad_middle,
    dstep_ref, dvalue_ref, db_ref, dc_ref, decay_ref, ring, ring_rest, side, side_rest, grad_end, grad_rest,
    ends, total, last, path, fades, line_send, line_recv, side_send, side_recv, *scratch,
):
    where = Place(count)
    streams, length, channels = fall.shape
    n = rate_ref.shape[0]
    lanes, blocks = blocks_of(channels)
    chunks = length // ROWS
    width = channels // SIDE
    where.greet()
    line = Line(where, up_one, down_one, ring, ring_rest, line_send, line_recv)
    z = where.z
    rise = remote(grad_middle, grad_end, line_send, line_recv, LINE_SEMS, where.above)
    sink = remote(grad_middle, grad_end, line_send, line_recv, LINE_SEMS + 1, where.below)
    core = remote(grad_end, grad_rest, line_send, line_recv, LINE_SEMS + 2, where.core)
    square = Side(where, mix, side, side_rest, side_send, side_recv)
    line.start(2)
    line.start_cores_of_one()

    def summary(i, _):
        cols = columns(i, lanes)
        rate = rate_ref[:, cols]

        def chunk(i, carry):
            base = pl.multiple_of((chunks - 1 - i) * ROWS, ROWS)
            out = []
            for s in range(streams):
                carried = carry[s]
                d = fall[s, pl.ds(base, ROWS), cols]
                g = g_ref[s, pl.ds(base, ROWS), cols]
                for j in reversed(range(ROWS)):
                    at = pl.ds(pl.multiple_of((base + j) * n, n), n)
                    fade = jnp.exp2(d[j : j + 1] * rate)
                    carried = fade * (g[j : j + 1] * wide(c_ref[s, at, :], lanes) + carried)
                out.append(carried)
            return tuple(out)

        start = tuple(jnp.zeros((n, lanes), jnp.float32) for _ in range(streams))
        states = lax.fori_loop(0, chunks, chunk, start)
        for s in range(streams):
            ends[s, :, cols] = states[s]
        return 0

    lax.fori_loop(0, blocks, summary, 0)
    sums(fall, total)

    def after_line():
        line.arrive(2)
        line.start(3)

    def after_all():
        square.start()

    chain(where, True, ends, total, rate_ref, last, scratch, after_line, after_all)
    db_ref[...] = jnp.zeros_like(db_ref)
    dc_ref[...] = jnp.zeros_like(dc_ref)

    def fold(tile):
        out = tile[:, :128]
        for k in range(1, lanes // 128):
            out = out + tile[:, k * 128 : (k + 1) * 128]
        return out

    def run(i, _):
        cols = columns(i, lanes)
        rate = rate_ref[:, cols]

        @pl.when(i == blocks // 3)
        def _():
            pl.when(z == SIDE - 2)(rise.start)
            pl.when(z == 1)(sink.start)

        @pl.when(i == blocks // 2)
        def _():
            square.turn()

        def ahead(i, states):
            base = pl.multiple_of(i * ROWS, ROWS)
            out = []
            for s in range(streams):
                state = states[s]
                d = fall[s, pl.ds(base, ROWS), cols]
                x = d_ref[s, pl.ds(base, ROWS), cols] * v_ref[s, pl.ds(base, ROWS), cols]
                for j in range(ROWS):
                    at = pl.ds(pl.multiple_of((base + j) * n, n), n)
                    path[s, at, :] = state
                    fade = jnp.exp2(d[j : j + 1] * rate)
                    fades[s, at, :] = fade
                    state = fade * state + x[j : j + 1] * wide(b_ref[s, at, :], lanes)
                out.append(state)
            return tuple(out)

        tails = lax.fori_loop(0, chunks, ahead, tuple(first_ref[s, :, cols] for s in range(streams)))

        def back(i, carry):
            base = pl.multiple_of((chunks - 1 - i) * ROWS, ROWS)
            out = []
            decay = carry[-1]
            for s in range(streams):
                state, carried = carry[s]
                d = d_ref[s, pl.ds(base, ROWS), cols]
                v = v_ref[s, pl.ds(base, ROWS), cols]
                g = g_ref[s, pl.ds(base, ROWS), cols]
                x = d * v
                weights, touches = [None] * ROWS, [None] * ROWS
                for j in reversed(range(ROWS)):
                    at = pl.ds(pl.multiple_of((base + j) * n, n), n)
                    gj = g[j : j + 1]
                    adjoint = gj * wide(c_ref[s, at, :], lanes) + carried
                    dc_ref[s, at, :] += fold(state * gj)
                    db_ref[s, at, :] += fold(adjoint * x[j : j + 1])
                    weights[j] = jnp.sum(adjoint * wide(b_ref[s, at, :], lanes), axis=0, keepdims=True)
                    carried = adjoint * fades[s, at, :]
                    state = path[s, at, :]
                    touch = carried * state
                    touches[j] = jnp.sum(touch * rate, axis=0, keepdims=True)
                    decay = decay + touch * d[j : j + 1]
                weighted = jnp.concatenate(weights, axis=0)
                at = pl.ds(base, ROWS)
                dstep_ref[s, at, cols] = weighted * v + jnp.concatenate(touches, axis=0) * LN2
                dvalue_ref[s, at, cols] = weighted * d
                out.append((state, carried))
            return tuple(out) + (decay,)

        start = tuple((tails[s], last[s, :, cols]) for s in range(streams))
        done = lax.fori_loop(0, chunks, back, start + (jnp.zeros((n, lanes), jnp.float32),))
        decay_ref[:, cols] = done[-1]
        return 0

    lax.fori_loop(0, blocks, run, 0)
    square.finish()
    line.arrive(3)
    pl.when(z == SIDE - 1)(rise.wait_recv)
    pl.when(z == 0)(sink.wait_recv)
    pl.when((z == 0) | (z == SIDE - 1))(core.start)
    line.finish()
    pl.when(z == SIDE - 2)(rise.wait_send)
    pl.when(z == 1)(sink.wait_send)
    pl.when((z == 0) | (z == SIDE - 1))(core.wait)


def in_vmem():
    return pl.BlockSpec(memory_space=pltpu.VMEM)


def in_hbm():
    return pl.BlockSpec(memory_space=pl.ANY)


def shaped(*shape):
    return jax.ShapeDtypeStruct(shape, jnp.float32)


def sems(count):
    return [pltpu.SemaphoreType.DMA((count,))] * 2


def scan_forward(fall, gain, b_wide, c_wide, rate, line, norm_near, norm_next):
    streams, length, channels = fall.shape
    n = rate.shape[0]
    count = lax.axis_size("seq")
    half, width = norm_near.shape
    three = shaped(SIDE - 1, half, width)
    return pl.pallas_call(
        functools.partial(forward_kernel, count),
        out_shape=[shaped(streams, length, channels), shaped(streams, n, channels), three, three, shaped(half, width), three],
        in_specs=[in_vmem()] * 5 + [in_hbm()] * 4,
        out_specs=[in_vmem()] * 2 + [in_hbm()] * 4,
        scratch_shapes=[pltpu.VMEM((streams, n, channels), jnp.float32), pltpu.VMEM((streams, channels), jnp.float32)]
        + sems(LINE_SEMS) + sems(5)
        + chain_scratch(streams, n, channels, count // SIDE),
        compiler_params=pltpu.CompilerParams(
            collective_id=0, has_side_effects=True, vmem_limit_bytes=24 * 1024 * 1024
        ),
        cost_estimate=spans(40),
    )(fall, gain, b_wide, c_wide, rate, *line, norm_near, norm_next)


def scan_backward(fall, step, value, d_y, b_wide, c_wide, rate, first, line, mix, grad_middle):
    streams, length, channels = fall.shape
    n = rate.shape[0]
    count = lax.axis_size("seq")
    half, width = mix.shape
    lanes, _ = blocks_of(channels)
    three = shaped(SIDE - 1, half, width)
    tall = shaped(streams, length * n, 128)
    flat = shaped(streams, length, channels)
    kept = pltpu.VMEM((streams, length * n, lanes), jnp.float32)
    return pl.pallas_call(
        functools.partial(backward_kernel, count),
        out_shape=[flat, flat, tall, tall, shaped(n, channels), three, three, three, three, shaped(half, width), shaped(half, width)],
        in_specs=[in_vmem()] * 8 + [in_hbm()] * 4,
        out_specs=[in_vmem()] * 5 + [in_hbm()] * 6,
        scratch_shapes=[
            pltpu.VMEM((streams, n, channels), jnp.float32),
            pltpu.VMEM((streams, channels), jnp.float32),
            pltpu.VMEM((streams, n, channels), jnp.float32),
            kept,
            kept,
        ]
        + sems(LINE_SEMS + 3) + sems(SIDE_SEMS)
        + chain_scratch(streams, n, channels, count // SIDE),
        compiler_params=pltpu.CompilerParams(
            collective_id=1, has_side_effects=True, vmem_limit_bytes=40 * 1024 * 1024
        ),
        cost_estimate=spans(62),
    )(fall, step, value, d_y, b_wide, c_wide, rate, first, *line, mix, grad_middle)


CHUNKS = 8
EARLY = 6


def stack_line(target, own, z, up, down, middle, first, last, rest, rest_first, rest_last):
    rows = own.shape[0]
    size = up.shape[0]
    target[:rows, :] = own[...].astype(target.dtype)

    def put(slot, block):
        target[rows + slot * size : rows + (slot + 1) * size, :] = block[...].astype(target.dtype)

    put(1, middle)
    put(4, rest.at[1])

    @pl.when(z >= 1)
    def _():
        put(2, up)
        put(5, rest.at[2])

    @pl.when(z < 1)
    def _():
        put(2, last)
        put(5, rest_last)

    @pl.when(z <= SIDE - 2)
    def _():
        put(0, down)
        put(3, rest.at[0])

    @pl.when(z > SIDE - 2)
    def _():
        put(0, first)
        put(3, rest_first)


def ffn_kernel(
    count, hid_own, hid_up, hid_down, hid_ring, hid_rest, grad_own, grad_up, grad_down, grad_middle, grad_rest, grad_end, grad_rest_end, wg, wu, wd, dg_own, du_own, act_own,
    mixer, out, near, passed,
    hid, grad, hid_cut, grad_cut, dg, du, act, stash, got, sent, sends, recvs, local,
):
    own, cut = hid_own.shape[0], hid_cut.shape[0]
    where = Place(count)
    z, place = where.z, where.place
    first = pl.program_id(0) == 0
    last = pl.program_id(0) == pl.num_programs(0) - 1
    odd, far = lax.rem(place, 2), place // 2
    early = [
        remote(
            stash.at[c, :, :, :, 1 - odd] if c % 2 == 0 else stash.at[c, :, :, 1 - far],
            near.at[c], sends, recvs, c, where.member[1 + c % 2],
        )
        for c in range(EARLY)
    ]
    tips, rising = (z == 0) | (z == SIDE - 1), z < SIDE // 2

    def along(source, target, at, up):
        return remote(source, target, sends, recvs, at, (jnp.where(up, where.above[0], where.below[0]), where.head))

    one = along(mixer.at[:, SIDE - 1 - z], got, EARLY, z == 0)
    fetch = pltpu.make_async_copy(mixer.at[:, lax.rem(z + 2, SIDE)], sent, local.at[0])
    way = jnp.where(rising, 0, 1)
    two = along(sent, passed.at[way], EARLY + 1 + way, rising)
    from_below = along(sent, passed.at[0], EARLY + 1, True)
    from_above = along(sent, passed.at[1], EARLY + 2, False)

    @pl.when(first)
    def _():
        where.greet()
        fetch.start()
        pl.when(tips)(one.start)
        fetch.wait()
        pl.when(tips)(two.start)
        ring, rest = hid_ring, hid_rest
        stack_line(hid, hid_own, z, hid_up, hid_down, ring.at[1], ring.at[0], ring.at[2], rest, rest.at[0], rest.at[2])
        ends = (grad_middle, grad_end, grad_end, grad_rest, grad_rest_end, grad_rest_end)
        stack_line(grad, grad_own, z, grad_up, grad_down, *ends)
        at = pl.ds(pl.multiple_of(z * cut, 128), cut)
        hid_cut[...] = hid[:, at].T
        grad_cut[...] = grad[:, at].T

    dg[:own, :] = dg_own[...]
    du[:own, :] = du_own[...]
    act[:own, :] = act_own[...]

    def turn(i, _):
        rows = pl.ds(pl.multiple_of(i * own, own), own)
        gate = dot(hid[rows, :], wg[...])
        up = dot(hid[rows, :], wu[...])
        d_act = dot_back(grad[rows, :], wd[...])
        sig = 1.0 / (1.0 + jnp.exp(-gate))
        silu = gate * sig
        dg[rows, :] = (d_act * up * (sig + silu * (1.0 - sig))).astype(dg.dtype)
        du[rows, :] = (d_act * silu).astype(du.dtype)
        act[rows, :] = (silu * up).astype(act.dtype)
        return 0

    lax.fori_loop(1, hid.shape[0] // own, turn, 0)
    out[0] = dot(hid_cut[...], dg[...])
    out[1] = dot(hid_cut[...], du[...])
    out[2] = dot(grad_cut[...], act[...])

    for c in range(EARLY):

        @pl.when(pl.program_id(0) == c)
        def _():
            for m in range(3):
                stash[c, m] = out[m].reshape(stash.shape[2:])
            early[c].start()

    @pl.when((pl.program_id(0) == pl.num_programs(0) // 2 + 1) & jnp.logical_not(tips))
    def _():
        one.wait_recv()
        sent[...] += got[...]
        two.start()

    @pl.when(last)
    def _():
        for c in early:
            c.wait()
        pl.when(tips)(one.wait_send)
        two.wait_send()

        @pl.when(jnp.logical_not(tips))
        def _():
            from_below.wait_recv()
            from_above.wait_recv()


def ffn_grads(hidden, out_grad, w_gate, w_up, w_down, d_gate, d_up, act, mixer):
    hid_own = hidden[0]
    own, width = hid_own.shape
    units = w_gate.shape[1]
    count = lax.axis_size("seq")
    cut = width // SIDE
    block = units // CHUNKS
    more = count // SIDE // SIDE
    rows = cut // (more * SIDE)
    tokens = own * SIDE
    low = jnp.bfloat16
    column = lambda rows: pl.BlockSpec((rows, block), lambda i: (0, i))
    tokens_in = (*hidden, *out_grad)
    return pl.pallas_call(
        functools.partial(ffn_kernel, count),
        grid=(units // block,),
        in_specs=[whole(a.shape) for a in tokens_in]
        + [column(width), column(width), pl.BlockSpec((block, width), lambda i: (i, 0))]
        + [column(own)] * 3
        + [in_hbm()],
        out_specs=[pl.BlockSpec((3, cut, block), lambda i: (0, 0, i))] + [in_hbm()] * 2,
        out_shape=[shaped(3, cut, units), shaped(EARLY, 3, more, 2, rows, block), shaped(2, 2, *mixer.shape[2:])],
        scratch_shapes=[pltpu.VMEM((tokens, width), low)] * 2
        + [pltpu.VMEM((cut, tokens), low)] * 2
        + [pltpu.VMEM((tokens, block), low)] * 3
        + [pltpu.VMEM((EARLY, 3, more, 2, 2, rows, block), jnp.float32)]
        + [pltpu.VMEM((2, *mixer.shape[2:]), jnp.float32)] * 2
        + sems(EARLY + 3) + [pltpu.SemaphoreType.DMA((1,))],
        compiler_params=pltpu.CompilerParams(
            collective_id=2, has_side_effects=True, vmem_limit_bytes=56 * 1024 * 1024
        ),
        cost_estimate=spans(36),
    )(*tokens_in, w_gate, w_up, w_down, d_gate, d_up, act, mixer)


class Reduce:
    def __init__(self, where, blocks, got, passed, arrived, sends, recvs):
        self.where, self.blocks, self.got, self.passed, self.arrived = where, blocks, got, passed, arrived
        self.sends, self.recvs = sends, recvs

    def out(self, source, target, at, rising):
        w = self.where
        return remote(source, target, self.sends, self.recvs, at, (jnp.where(rising, w.above[0], w.below[0]), w.head))

    def one(self):
        return self.out(self.blocks.at[:, SIDE - 1 - self.where.z], self.got, 0, self.where.z == 0)

    def start_one(self):
        pl.when((self.where.z == 0) | (self.where.z == SIDE - 1))(self.one().start)

    def middle(self):
        return (self.where.z > 0) & (self.where.z < SIDE - 1)

    def two(self, source):
        rising = self.where.z < SIDE // 2
        return self.out(source, self.passed.at[jnp.where(rising, 0, 1)], jnp.where(rising, 1, 2), rising)

    def start_two(self):
        z = self.where.z

        @pl.when(self.middle())
        def _():
            self.one().wait_recv()
            self.got[...] += self.blocks[:, lax.rem(z + 2, SIDE)]
            self.two(self.got).start()

        @pl.when(jnp.logical_not(self.middle()))
        def _():
            self.two(self.blocks.at[:, lax.rem(z + 2, SIDE)]).start()

    def three(self, source, way):
        return self.out(source, self.arrived.at[way], 3 + way, way == 0)

    def start_three(self, wait):
        z = self.where.z

        @pl.when(self.middle())
        def _():
            for way in (0, 1):
                if wait:
                    self.two_from(way).wait_recv()
                self.passed[way] += self.blocks[:, z + 1 - 2 * way]
                self.three(self.passed.at[way], way).start()

        pl.when(z == 0)(self.three(self.blocks.at[:, 1], 0).start)
        pl.when(z == SIDE - 1)(self.three(self.blocks.at[:, SIDE - 2], 1).start)

    def two_from(self, way):
        return self.out(self.passed.at[way], self.passed.at[way], 1 + way, way == 0)

    def result(self, done):
        z = self.where.z
        done[...] = self.blocks[:, z].reshape(done.shape)
        for way in (0, 1):

            @pl.when((z >= 1) if way == 0 else (z <= SIDE - 2))
            def _():
                self.three(self.passed.at[way], way).wait_recv()
                done[...] += self.arrived[way].reshape(done.shape)

    def finish(self, first):
        z = self.where.z
        if first <= 1:
            pl.when((z == 0) | (z == SIDE - 1))(self.one().wait_send)
        if first <= 2:
            self.two(self.got).wait_send()
        pl.when(z <= SIDE - 2)(self.three(self.passed.at[0], 0).wait_send)
        pl.when(z >= 1)(self.three(self.passed.at[1], 1).wait_send)


REDUCE_SEMS = 5


def sum_kernel(
    count, ffn, mixer_in, passed_in, d_inner, near_in, turned, d_own, small,
    ffn_out, mixer_out, inner_out, small_out,
    d_all, kept, near, next_, mixer, m_passed, m_arrived, d_side, inner, i_got, i_passed, i_arrived, m_done, m_back, i_done, i_back, s_near, s_next, s_done, s_line,
    ffn_send, ffn_recv, m_send, m_recv, i_send, i_recv, back_send, back_recv, s_send, s_recv, d_send, d_recv, local,
):
    where = Place(count)
    place = where.place
    more = where.stride // SIDE
    span = near.shape[5]
    odd, far = lax.rem(place, 2), place // 2
    cols = [pl.ds(c * span, span) for c in range(CHUNKS)]
    loads = [pltpu.make_async_copy(mixer_in, mixer, local.at[0]), pltpu.make_async_copy(passed_in, m_passed, local.at[1])]
    keeps = [
        pltpu.make_async_copy(
            ffn.at[:, :, :, odd, :, cols[c]] if c % 2 == 0 else ffn.at[:, :, far, :, :, cols[c]], kept.at[c], local.at[3 + c]
        )
        for c in range(CHUNKS)
    ]
    nears = [pltpu.make_async_copy(near_in.at[c], near.at[c], local.at[3 + CHUNKS + c]) for c in range(EARLY)]
    for c in loads + nears + keeps:
        c.start()
    where.greet()
    first = {
        c: remote(
            ffn.at[:, :, :, 1 - odd, :, cols[c]] if c % 2 == 0 else ffn.at[:, :, 1 - far, :, :, cols[c]],
            near.at[c], ffn_send, ffn_recv, c, where.member[1 + c % 2],
        )
        for c in range(EARLY, CHUNKS)
    }
    size = inner.shape[3]
    quarters = [
        remote(
            d_inner.at[:, :, pl.ds(pl.multiple_of((place ^ k) * size, 128), size)], d_side.at[k - 1],
            d_send, d_recv, k - 1, where.member[k],
        )
        for k in range(1, SIDE)
    ]
    for c in quarters:
        c.start()
    for c in first.values():
        c.start()
    groups, half = where.groups, s_near.shape[3]
    s_rows = [pl.ds(0, half), pl.ds(half, half)]
    s_first = [
        remote(small.at[:, :, 1 - odd, s_rows[0]], s_near.at[0], s_send, s_recv, 0, where.member[1]),
        remote(small.at[:, 1 - far, :, s_rows[1]], s_near.at[1], s_send, s_recv, 1, where.member[2]),
    ]
    for c in s_first:
        c.start()
    second = {}

    def again(c):
        kept[c] += near[c]
        bit = far if c % 2 == 0 else odd
        second[c] = remote(
            kept.at[c, :, :, 1 - bit], next_.at[c], ffn_send, ffn_recv, CHUNKS + c, where.member[2 - c % 2]
        )
        second[c].start()

    line = Reduce(where, mixer, None, m_passed, m_arrived, m_send, m_recv)
    for c in loads:
        c.wait()
    line.start_three(False)
    for c in range(EARLY):
        nears[c].wait()
        keeps[c].wait()
        again(c)
    for c in quarters:
        c.wait_recv()
    own = d_own.shape[0]
    part = own // 2
    d_all[:own, :] = d_own[...]
    for k in range(SIDE - 1):
        for s in range(2):
            start = own + (s * (SIDE - 1) + k) * part
            d_all[start : start + part, :] = d_side[k, where.head if s == 0 else 1 - where.head].astype(d_all.dtype)
    for k in range(SIDE):
        at = slice(k * inner.shape[2], (k + 1) * inner.shape[2])
        inner[0, k] = dot(turned[at, :], d_all[...])
    other = Reduce(where, inner, i_got, i_passed, i_arrived, i_send, i_recv)
    other.start_one()
    other.start_two()
    for c in s_first:
        c.wait_recv()
    s_near[0] += small[:, :, odd, s_rows[0]]
    s_near[1] += small[:, far, :, s_rows[1]]
    s_second = [
        remote(s_near.at[0, :, 1 - far], s_next.at[0], s_send, s_recv, 2, where.member[2]),
        remote(s_near.at[1, :, 1 - odd], s_next.at[1], s_send, s_recv, 3, where.member[1]),
    ]
    for c in s_second:
        c.start()
    for c in range(EARLY, CHUNKS):
        keeps[c].wait()
        first[c].wait_recv()
        again(c)
    for c in s_second:
        c.wait_recv()
    s_done[:, :half] = s_near[0, :, far] + s_next[0]
    s_done[:, half:] = s_near[1, :, odd] + s_next[1]
    s_last = [
        remote(s_done.at[lax.rem(where.group + k, groups)], s_line.at[k], s_send, s_recv, 3 + k, where.other[k])
        for k in range(1, groups)
    ]
    for c in s_last:
        c.start()
    other.start_three(True)

    def spread(reduced, done, back, at):
        reduced.result(done)
        copies = [
            remote(done.at[:, :, place ^ k], back.at[k], back_send, back_recv, at + k, where.member[k])
            for k in range(1, SIDE)
        ]
        for c in copies:
            c.start()
        back[0] = done[:, :, place]
        return copies

    spreads = spread(line, m_done, m_back, 0)
    for c in range(CHUNKS):
        second[c].wait_recv()
        bit = far if c % 2 == 0 else odd
        ffn_out[:, :, :, c * span : (c + 1) * span] = kept[c, :, :, bit] + next_[c]
    spreads += spread(other, i_done, i_back, SIDE)
    for c in spreads:
        c.wait_recv()
    width = inner.shape[3]
    for q in range(SIDE):
        cols = slice(q * width, (q + 1) * width)
        mixer_out[:, :, :, cols] = m_back[place ^ q]
        inner_out[:, :, :, cols] = i_back[place ^ q]
    total = s_done[where.group]
    for k in range(1, groups):
        s_last[k - 1].wait_recv()
        total = total + s_line[k]
    small_out[...] = total
    for c in list(first.values()) + list(second.values()) + spreads + s_first + s_second + s_last:
        c.wait_send()
    for c in quarters:
        c.wait_send()
    line.finish(3)
    other.finish(1)


def sum_grads(ffn, mixer, passed, d_inner, near, turned, d_own, small):
    count = lax.axis_size("seq")
    more = count // SIDE // SIDE
    cut, units = ffn.shape[1:]
    rows = cut // (more * SIDE)
    size = mixer.shape[-1]
    f32 = jnp.float32
    v = lambda *shape: pltpu.VMEM(shape, f32)
    groups, tall = count // SIDE, small.shape[1]
    return pl.pallas_call(
        functools.partial(sum_kernel, count),
        out_shape=[shaped(3, more, rows, units), shaped(2, more, rows, size * SIDE), shaped(1, more, rows, size * SIDE),
                   shaped(tall, LANES)],
        in_specs=[in_hbm()] * 5 + [in_vmem()] * 3,
        out_specs=[in_vmem()] * 4,
        scratch_shapes=[
            pltpu.VMEM((turned.shape[1], size), jnp.bfloat16),
            v(CHUNKS, 3, more, 2, rows, units // CHUNKS),
            v(CHUNKS, 3, more, 2, rows, units // CHUNKS),
            v(CHUNKS, 3, more, rows, units // CHUNKS),
            v(2, SIDE, cut, size), v(2, 2, cut, size), v(2, 2, cut, size),
            v(SIDE - 1, *d_inner.shape[:2], size),
            v(1, SIDE, cut, size), v(1, cut, size), v(2, 1, cut, size), v(2, 1, cut, size),
            v(2, more, SIDE, rows, size), v(SIDE, 2, more, rows, size),
            v(1, more, SIDE, rows, size), v(SIDE, 1, more, rows, size),
            v(2, groups, 2, tall // 2, LANES), v(2, groups, tall // 2, LANES), v(groups, tall, LANES), v(groups, tall, LANES),
        ]
        + sems(2 * CHUNKS) + sems(REDUCE_SEMS) + sems(REDUCE_SEMS) + sems(2 * SIDE) + sems(3 + groups) + sems(SIDE) + [pltpu.SemaphoreType.DMA((3 + CHUNKS + EARLY,))],
        compiler_params=pltpu.CompilerParams(
            collective_id=3, has_side_effects=True, vmem_limit_bytes=58 * 1024 * 1024
        ),
        cost_estimate=spans(100),
    )(ffn.reshape(3, more, 2, 2, rows, units), mixer, passed, d_inner, near, turned, d_own, small.reshape(groups, 2, 2, tall, LANES))


def middle_kernel(
    count, hid, grad, wg, wu, wd, hidden, y,
    dg, du, act, ffn, d_hid, up_one, down_one, y_side, sends, recvs,
):
    where = Place(count)
    z, place = where.z, where.place
    width = y_side.shape[-1]
    quarters = [
        remote(
            y.at[:, :, pl.ds(pl.multiple_of((place ^ k) * width, 128), width)], y_side.at[k - 1],
            sends, recvs, k - 1, where.member[k],
        )
        for k in range(1, SIDE)
    ]
    mine = hidden.at[where.head]
    up = remote(mine, up_one, sends, recvs, SIDE - 1, where.above)
    down = remote(mine, down_one, sends, recvs, SIDE, where.below)

    @pl.when(pl.program_id(0) == 0)
    def _():
        where.greet()
        pl.when(z < SIDE - 1)(up.start)
        pl.when(z > 0)(down.start)
        for c in quarters:
            c.start()
        ffn[...] = jnp.zeros_like(ffn)
        d_hid[...] = jnp.zeros_like(d_hid)

    gate = dot(hid[...], wg[...])
    raised = dot(hid[...], wu[...])
    d_act = dot_back(grad[...], wd[...])
    sig = 1.0 / (1.0 + jnp.exp(-gate))
    silu = gate * sig
    dg[...] = (d_act * raised * (sig + silu * (1.0 - sig))).astype(dg.dtype)
    du[...] = (d_act * silu).astype(du.dtype)
    act[...] = (silu * raised).astype(act.dtype)
    ffn[...] += dot(act[...], wd[...])
    d_hid[...] += dot_back(dg[...], wg[...]) + dot_back(du[...], wu[...])

    @pl.when(pl.program_id(0) == pl.num_programs(0) - 1)
    def _():
        for c in quarters:
            c.wait()
        pl.when(z < SIDE - 1)(up.wait_send)
        pl.when(z > 0)(down.wait_send)
        pl.when(z > 0)(up.wait_recv)
        pl.when(z < SIDE - 1)(down.wait_recv)


def feed_forward(hid, grad, w_gate, w_up, w_down, hidden, y):
    own, width = hid.shape
    units = w_gate.shape[1]
    count = lax.axis_size("seq")
    streams, length, channels = y.shape
    block = next(b for b in (256, 128) if units % b == 0)
    column = lambda rows: pl.BlockSpec((rows, block), lambda i: (0, i))
    low = jax.ShapeDtypeStruct((own, units), jnp.bfloat16)
    flat = shaped(own, width)
    one = shaped(length, width)
    return pl.pallas_call(
        functools.partial(middle_kernel, count),
        grid=(units // block,),
        in_specs=[whole(hid.shape), whole(grad.shape), column(width), column(width),
                  pl.BlockSpec((block, width), lambda i: (i, 0)), in_hbm(), in_hbm()],
        out_specs=[column(own)] * 3 + [whole(flat.shape)] * 2 + [in_hbm()] * 3,
        out_shape=[low, low, low, flat, flat, one, one, shaped(SIDE - 1, streams, length, channels // SIDE)],
        scratch_shapes=sems(SIDE + 1),
        compiler_params=pltpu.CompilerParams(
            collective_id=4, has_side_effects=True, vmem_limit_bytes=24 * 1024 * 1024
        ),
        cost_estimate=spans(20),
    )(hid, grad, w_gate, w_up, w_down, hidden, y)


LANES = 128


def gather_kernel(places, w_step, log_decay, select, *refs):
    rows, out = refs[:-1], refs[-1]
    ranks, states = w_step.shape[0], log_decay.shape[0]
    size = w_step.shape[1] // places
    high = select.shape[0] // places
    low = ranks + states + 16
    out[...] = jnp.zeros_like(out)
    for p in range(places):
        cols = slice(p * size, (p + 1) * size)
        out[p, :ranks, :size] = w_step[:, cols]
        out[p, ranks : ranks + states, :size] = log_decay[:, cols]
        for k, row in enumerate(rows):
            out[p, ranks + states + k : ranks + states + k + 1, :size] = row[:, cols]
        for b in range(select.shape[1] // LANES):
            out[p, low + b * high : low + (b + 1) * high, :] = select[
                p * high : (p + 1) * high, b * LANES : (b + 1) * LANES
            ]


def gather_small(w_step, log_decay, select, rows):
    places = lax.axis_size("seq")
    channels = w_step.shape[1]
    tall = w_step.shape[0] + log_decay.shape[0] + 16 + select.shape[0] // places * (channels // LANES)
    tall = -(-tall // 16) * 16
    return pl.pallas_call(
        functools.partial(gather_kernel, places),
        out_shape=shaped(places, tall, LANES),
        in_specs=[in_vmem()] * (3 + len(rows)),
        out_specs=in_vmem(),
        compiler_params=params(12),
        cost_estimate=spans(4),
    )(w_step, log_decay, select, *[row.reshape(1, -1) for row in rows])


def place_kernel(rank, states, taps, high, size, gains, ffn, mixer, inner, small, *outs):
    gate, up, down, mixout, outgate, w_in, w_step, log_decay, conv_taps, w_select = outs[:10]
    gate[...] = ffn[0]
    up[...] = ffn[1]
    down[...] = ffn[2]
    outgate[...] = mixer[0]
    mixout[...] = mixer[1]
    w_in[...] = inner[0]
    w_step[...] = small[:rank, :size]
    at = rank + states
    log_decay[...] = small[rank:at, :size]
    conv_taps[...] = small[at : at + taps, :size]
    at += taps
    for k, row in enumerate(outs[10:15]):
        row[...] = small[at + k : at + k + 1, :size]
    outs[15][...] = small[at + 5 : at + 6, :gains]
    at = rank + states + 16
    for b in range(w_select.shape[1] // LANES):
        w_select[:, b * LANES : (b + 1) * LANES] = small[at + b * high : at + (b + 1) * high, :]


def place_all(rank, states, taps, high, gains, channels, ffn, mixer, inner, small):
    rows, units = ffn.shape[1:]
    size = channels // lax.axis_size("seq")
    width = mixer.shape[2]
    shapes = [(rows, units), (rows, units), (rows, units), (rows, width), (rows, width), (rows, width), (rank, size),
              (states, size), (taps, size), (high, channels)] + [(1, size)] * 5 + [(1, gains)]
    return pl.pallas_call(
        functools.partial(place_kernel, rank, states, taps, high, size, gains),
        out_shape=[shaped(*shape) for shape in shapes],
        in_specs=[in_vmem()] * 4,
        out_specs=[in_vmem()] * len(shapes),
        compiler_params=params(40),
        cost_estimate=spans(6),
    )(ffn, mixer, inner, small)


epsilon = 1e-06
CUT = 1e6


def links(step, wrap=False, axis="seq"):
    n = lax.axis_size(axis)
    return [(i, (i + step) % n) for i in range(n) if wrap or 0 <= i + step < n]


def swaps(bit, axis="seq"):
    return [(i, i ^ bit) for i in range(lax.axis_size(axis))]


def send(block, route, axis="seq"):
    return lax.ppermute(block, axis, route)


def head_sum(part):
    return part + send(part, swaps(1, "head"), "head")


def own_stream(block):
    return lax.dynamic_index_in_dim(block, lax.axis_index("head"), 0, keepdims=False)


def part_of(block, index, size, axis):
    return lax.dynamic_slice_in_dim(block, index * size, size, axis)


def after(block, *earlier):
    return lax.optimization_barrier((block,) + earlier)[0]


def matmul(left, right):
    return jnp.dot(left, right, preferred_element_type=jnp.float32)


def matmul_back(left, right):
    return lax.dot_general(
        left, right, (((left.ndim - 1,), (1,)), ((), ())), preferred_element_type=jnp.float32
    )


def weight_outer(left, right):
    axes = tuple(range(left.ndim - 1))
    return lax.dot_general(left, right, ((axes, axes), ((), ())), preferred_element_type=jnp.float32)


def norm_forward(v, gain):
    scale = lax.rsqrt(jnp.mean(v * v, axis=-1, keepdims=True) + epsilon)
    return (v * scale * gain, scale)


def norm_backward(v, scale, gain, upstream):
    weighted = upstream * gain
    d_input = scale * weighted - v * scale * scale * scale * jnp.mean(
        weighted * v, axis=-1, keepdims=True
    )
    d_gain = jnp.sum(upstream * v * scale, axis=(0, 1))
    return (d_input, d_gain)


def silu_slope(v):
    sig = jax.nn.sigmoid(v)
    return sig + v * sig * (1.0 - sig)


def across(small):
    streams, length, n = small.shape
    return jnp.broadcast_to(small.reshape(streams, length * n, 1), (streams, length * n, 128))


def along(wide_sum, n):
    streams, rows, _ = wide_sum.shape
    return jnp.sum(wide_sum, axis=-1).reshape(streams, rows // n, n)


def body(
    tokens, doc_ids, out_grad, norm_mix, w_inner, w_outgate, conv_taps, conv_bias, w_select, select_gain,
    w_step, step_bias, log_decay, skip_gain, w_mixout, norm_ffn, w_gate, w_up, w_down,
):
    streams, length, width = tokens.shape
    channels = w_inner.shape[1]
    taps = conv_taps.shape[0]
    rank = w_step.shape[0]
    states = log_decay.shape[1]
    lead = taps - 1
    count = lax.axis_size("seq")
    stride = count // SIDE
    here = lax.axis_index("seq")
    z, place = here // stride, here % SIDE
    size = channels // SIDE
    low = jnp.bfloat16

    grad_in = out_grad.astype(jnp.float32)
    source = tokens.astype(jnp.float32)
    rim_ids = jnp.broadcast_to((doc_ids[:, length - lead :] + 1).astype(jnp.float32)[:, :, None], (streams, lead, 128))
    rim = send(jnp.concatenate([source[:, length - lead :], rim_ids], axis=2), links(1))
    mine_grad, source, rim = lax.optimization_barrier((own_stream(out_grad).astype(jnp.float32), source, rim))
    line_grad = [send(mine_grad, links(stride)), send(mine_grad, links(-stride))]
    normed, scale_mix = norm_forward(source, norm_mix)
    normed_low = normed.astype(low)
    mine_normed = own_stream(normed)
    norm_near, norm_next = send(mine_normed, swaps(1)), send(mine_normed, swaps(2))
    rim_normed, _ = norm_forward(rim[:, :, :width], norm_mix)
    ext_val = matmul(jnp.concatenate([rim_normed.astype(low), normed_low], axis=1), w_inner)
    outgate = matmul(normed_low, w_outgate)
    ext_ids = jnp.concatenate([rim[:, :, width].astype(jnp.int32) - 1, doc_ids], axis=1)
    masks = [
        (ext_ids[:, k : k + length] == doc_ids).astype(jnp.float32)[:, :, None] for k in range(taps)
    ]
    value_pre = conv_bias
    for k in range(taps):
        value_pre = value_pre + conv_taps[k] * ext_val[:, k : k + length] * masks[k]
    value = jax.nn.silu(value_pre)
    value_low = value.astype(low)
    select = head_sum(matmul(value_low, w_select))
    raw_step = select[..., :rank]
    raw_b = select[..., rank : rank + states]
    raw_c = select[..., rank + states :]
    step_n, step_scale = norm_forward(raw_step, select_gain[:rank])
    bsel, b_scale = norm_forward(raw_b, select_gain[rank : rank + states])
    csel, c_scale = norm_forward(raw_c, select_gain[rank + states :])
    step_low = step_n.astype(low)
    step_pre = matmul(step_low, w_step) + step_bias
    step = jax.nn.softplus(step_pre)
    keep = doc_ids == ext_ids[:, lead - 1 : lead - 1 + length]
    fall = jnp.where(keep[:, :, None], step, CUT)
    gain = step * value
    decay_rate = -jnp.exp(log_decay).T
    rate = decay_rate * LOG2E
    b_wide, c_wide = across(bsel), across(csel)
    outs, first, grad_ring, grad_rest, side_far, side_rest = scan_forward(
        fall, gain, b_wide, c_wide, rate, line_grad, norm_near, norm_next
    )
    y = outs + skip_gain * value
    gate_z = jax.nn.silu(outgate)
    mixed = y * gate_z
    mixed_low = mixed.astype(low)
    mix = head_sum(matmul(mixed_low, w_mixout))
    resid = source + mix
    hidden, scale_ffn = norm_forward(resid, norm_ffn)
    hidden_low = hidden.astype(low)
    flat = lambda block: block.reshape(-1, block.shape[-1])
    like = lambda block: block.reshape(streams, length, -1)
    d_gate, d_up, act_low, ffn, d_hidden, *line_hidden, y_side = feed_forward(
        flat(hidden_low), flat(out_grad), w_gate, w_up, w_down, hidden, y
    )
    output = (resid + head_sum(like(ffn))).astype(low)
    d_hidden = head_sum(like(d_hidden))
    d_resid_norm, grad_norm_ffn = norm_backward(resid, scale_ffn, norm_ffn, d_hidden)
    d_resid = grad_in + d_resid_norm
    d_mix = d_resid.astype(low)
    d_mixed = matmul_back(d_mix, w_mixout)
    d_y = d_mixed * gate_z
    d_outgate = (d_mixed * y * silu_slope(outgate)).astype(low)
    grad_skip_gain = jnp.sum(d_y * value, axis=(0, 1))
    (
        d_step, d_scan, db_wide, dc_wide, decay_sum, hid_ring, hid_rest, mix_side, mix_rest, grad_end, grad_rest_end,
    ) = scan_backward(
        fall, step, value, d_y, b_wide, c_wide, rate, first, line_hidden, own_stream(d_resid), grad_ring[1]
    )

    mixer, turned = mixer_grads(
        flat(normed_low), [norm_near, norm_next, side_far, side_rest], flat(d_mix), [mix_side, mix_rest],
        flat(part_of(y, place, size, 2)), y_side,
        w_outgate, w_mixout,
    )
    mixer = mixer.reshape(2, SIDE, width // SIDE, size)
    ffn, near, passed = ffn_grads(
        (flat(hidden_low), *line_hidden, hid_ring, hid_rest),
        (flat(out_grad), *line_grad, grad_ring[1], grad_rest, grad_end, grad_rest_end),
        w_gate, w_up, w_down, d_gate, d_up, act_low, mixer,
    )
    d_step = after(d_step, ffn)

    d_value = d_y * skip_gain + d_scan
    d_step_pre = (d_step * jax.nn.sigmoid(step_pre)).astype(low)
    grad_step_bias = jnp.sum(d_step_pre, axis=(0, 1), dtype=jnp.float32)
    grad_w_step = weight_outer(step_low, d_step_pre)
    d_small = head_sum(
        jnp.concatenate(
            [matmul_back(d_step_pre, w_step), along(db_wide, states), along(dc_wide, states)], axis=-1
        )
    )
    d_raw_step, gain_step = norm_backward(
        raw_step, step_scale, select_gain[:rank], d_small[..., :rank]
    )
    d_raw_b, gain_b = norm_backward(
        raw_b, b_scale, select_gain[rank : rank + states], d_small[..., rank : rank + states]
    )
    d_raw_c, gain_c = norm_backward(
        raw_c, c_scale, select_gain[rank + states :], d_small[..., rank + states :]
    )
    grad_select_gain = jnp.concatenate([gain_step, gain_b, gain_c])
    d_select = jnp.concatenate([d_raw_step, d_raw_b, d_raw_c], axis=-1).astype(low)
    grad_w_select = weight_outer(d_select, value_low)
    d_value = d_value + matmul_back(d_select, w_select)
    d_value_pre = d_value * silu_slope(value_pre)
    grad_conv_bias = jnp.sum(d_value_pre, axis=(0, 1))
    tap_grads = []
    d_ext = jnp.zeros_like(ext_val)
    for k in range(taps):
        masked = d_value_pre * masks[k]
        tap_grads.append(jnp.sum(masked * ext_val[:, k : k + length], axis=(0, 1)))
        d_ext = d_ext + jnp.pad(masked * conv_taps[k], ((0, 0), (k, lead - k), (0, 0)))
    rim_grad = send(d_ext[:, :lead], links(-1))
    d_inner = (d_ext[:, lead:] + jnp.pad(rim_grad, ((0, 0), (length - lead, 0), (0, 0)))).astype(low)
    d_normed = head_sum(matmul_back(d_inner, w_inner) + matmul_back(d_outgate, w_outgate))
    d_source, grad_norm_mix = norm_backward(source, scale_mix, norm_mix, d_normed)
    tokens_grad = d_resid + d_source

    gains = grad_select_gain.reshape(count, -1)
    spread = jnp.pad(gains, ((0, 0), (0, channels // count - gains.shape[1]))).reshape(channels)
    pad = lambda v: jnp.pad(v, (0, channels - v.shape[0]))
    rows = tap_grads + [
        grad_conv_bias, grad_step_bias, grad_skip_gain, pad(grad_norm_mix), pad(grad_norm_ffn), spread
    ]
    grad_w_step = after(grad_w_step, tokens_grad)
    small = gather_small(grad_w_step, decay_sum * decay_rate, grad_w_select, rows)
    ffn, mixer, inner, tall = sum_grads(
        ffn, mixer, passed, d_inner.astype(jnp.float32), near, turned, flat(part_of(d_inner, place, size, 2)), small
    )
    if count > SIDE * SIDE:
        groups = [[a * stride + b + SIDE * k for k in range(stride // SIDE)] for a in range(SIDE) for b in range(SIDE)]
        ffn, mixer, inner = (
            lax.psum_scatter(part, "seq", scatter_dimension=1, axis_index_groups=groups) for part in (ffn, mixer, inner)
        )
    else:
        ffn, mixer, inner = (part[:, 0] for part in (ffn, mixer, inner))
    outs = place_all(
        rank, states, taps, grad_w_select.shape[0] // count, gains.shape[1], channels, ffn, mixer, inner, tall
    )
    gate, up, down, mixout, outgate, w_in, d_w_step, d_log_decay, d_taps, d_select = outs[:10]
    conv, bias, skip, mix_gain, ffn_gain, select_gains = (row[0] for row in outs[10:])
    return (
        output,
        tokens_grad,
        mix_gain,
        w_in,
        outgate,
        d_taps,
        conv,
        d_select.T,
        select_gains,
        d_w_step,
        bias,
        d_log_decay.T,
        skip,
        mixout.T,
        ffn_gain,
        gate,
        up,
        down.T,
    )


def solution(mesh):
    in_specs = (
        P(None, "seq", None),
        P(None, "seq"),
        P(None, "seq", None),
        P(),
        P(None, "head"),
        P(None, "head"),
        P(None, "head"),
        P("head"),
        P("head", None),
        P(),
        P(None, "head"),
        P("head"),
        P("head", None),
        P("head"),
        P("head", None),
        P(),
        P(None, "head"),
        P(None, "head"),
        P("head", None),
    )
    out_specs = (
        P(None, "seq", None),
        P(None, "seq", None),
        P("seq"),
        P("seq", "head"),
        P("seq", "head"),
        P(None, ("head", "seq")),
        P(("head", "seq")),
        P("head", "seq"),
        P("seq"),
        P(None, ("head", "seq")),
        P(("head", "seq")),
        P(("head", "seq"), None),
        P(("head", "seq")),
        P("head", "seq"),
        P("seq"),
        P("seq", "head"),
        P("seq", "head"),
        P("head", "seq"),
    )
    return jax.shard_map(body, mesh=mesh, in_specs=in_specs, out_specs=out_specs, check_vma=False)
```

```python
import functools
import math

import jax
import jax.numpy as jnp
from jax import lax
from jax.experimental import pallas as pl
from jax.experimental.pallas import tpu as pltpu
from jax.sharding import PartitionSpec as P

LOG2E = math.log2(math.e)
LN2 = math.log(2.0)
ROWS = 8


def params(limit=48):
    return pltpu.CompilerParams(vmem_limit_bytes=limit * 1024 * 1024)


def wide(tile, lanes):
    return jnp.concatenate([tile] * (lanes // tile.shape[1]), axis=1)


def pieces(lanes):
    return next(w for w in (256, 128) if lanes % w == 0)


def spans(us):
    return pl.CostEstimate(flops=int(us * 1.1e8), bytes_accessed=int(us * 3.0e5), transcendentals=0)


def fetch_tokens(blocks, stage, arrived):
    copies = [pltpu.make_async_copy(block, stage.at[k], arrived.at[k]) for k, block in enumerate(blocks)]
    for c in copies:
        c.start()

    def put(target, own):
        rows, size = own.shape[0], stage.shape[1]
        target[:rows, :] = own[...].astype(target.dtype)
        for k, c in enumerate(copies):
            c.wait()
            target[rows + k * size : rows + (k + 1) * size, :] = stage[k].astype(target.dtype)

    return put


def parts_of(refs):
    return [part for ref in refs for part in ([ref.at[k] for k in range(ref.shape[0])] if len(ref.shape) == 3 else [ref])]


def dot(left, right):
    return jnp.dot(left, right, preferred_element_type=jnp.float32)


def dot_back(left, right):
    return lax.dot_general(left, right, (((1,), (1,)), ((), ())), preferred_element_type=jnp.float32)


def whole(shape):
    return pl.BlockSpec(shape, lambda i: (0,) * len(shape), pipeline_mode=pl.Buffered(1))


def mixer_kernel(more_norm, more_mix, *refs):
    at = iter(range(len(refs)))
    take = lambda count: [refs[next(at)] for _ in range(count)]
    (norm_own,), norm_more = take(1), take(more_norm)
    (mix_own,), mix_more = take(1), take(more_mix)
    y_own, y_side = take(2)
    w_out, w_mix = take(2)
    out, norm_turned = take(2)
    norm, mix, mixed, d_out, wo, wm, local, norm_stage, mix_stage, norm_got, mix_got = take(11)
    own = norm_own.shape[0]
    half = own // 2

    @pl.when(pl.program_id(0) == 0)
    def _():
        size = wo.shape[1]
        at = pl.ds(pl.multiple_of(lax.rem(lax.axis_index("seq"), SIDE) * size, 128), size)
        loads = [
            pltpu.make_async_copy(w_out.at[:, at], wo, local.at[0]),
            pltpu.make_async_copy(w_mix.at[at], wm, local.at[1]),
        ]
        for c in loads:
            c.start()
        put_norm = fetch_tokens(parts_of(norm_more), norm_stage, norm_got)
        put_mix = fetch_tokens(parts_of(mix_more), mix_stage, mix_got)
        put_norm(norm, norm_own)
        put_mix(mix, mix_own)
        for c in loads:
            c.wait()

        def finish(rows, y):
            outgate = dot(norm[rows, :], wo[...])
            d_mixed = dot_back(mix[rows, :], wm[...])
            sig = 1.0 / (1.0 + jnp.exp(-outgate))
            silu = outgate * sig
            mixed[rows, :] = (y * silu).astype(mixed.dtype)
            d_out[rows, :] = (d_mixed * y * (sig + silu * (1.0 - sig))).astype(d_out.dtype)

        finish(slice(0, own), y_own[...])
        sides = y_side.shape[0]
        head = lax.axis_index("head")
        for k in range(sides):
            for s in range(2):
                start = own + (s * sides + k) * half
                finish(slice(start, start + half), y_side[k, head if s == 0 else 1 - head])

    rows = norm_turned.shape[0]
    span = pl.ds(pl.multiple_of(pl.program_id(0) * rows, rows), rows)
    turned = norm[:, span].T
    norm_turned[...] = turned
    out[0] = dot(turned, d_out[...])
    out[1] = dot(mix[:, span].T, mixed[...])


def mixer_grads(norm_own, norm_more, mix_own, mix_more, y_own, y_side, w_out, w_mix):
    own, width = norm_own.shape
    cut = w_out.shape[1] // SIDE
    block = next(b for b in (256, 128) if width % b == 0)
    tokens = own + sum(math.prod(part.shape[:-1]) for part in norm_more)
    low = jnp.bfloat16
    row = lambda columns: pl.BlockSpec((block, columns), lambda i: (i, 0))
    operands = (norm_own, *norm_more, mix_own, *mix_more, y_own, y_side, w_out, w_mix)
    return pl.pallas_call(
        functools.partial(mixer_kernel, len(norm_more), len(mix_more)),
        grid=(width // block,),
        in_specs=[whole(norm_own.shape)] + [in_hbm()] * len(norm_more) + [whole(mix_own.shape)] + [in_hbm()] * len(mix_more)
        + [whole(y_own.shape), whole(y_side.shape)] + [in_hbm()] * 2,
        out_specs=[pl.BlockSpec((2, block, cut), lambda i: (0, i, 0)), row(tokens)],
        out_shape=[
            jax.ShapeDtypeStruct((2, width, cut), jnp.float32),
            jax.ShapeDtypeStruct((width, tokens), low),
        ],
        scratch_shapes=[pltpu.VMEM((tokens, width), low)] * 2
        + [pltpu.VMEM((tokens, cut), low)] * 2
        + [pltpu.VMEM((width, cut), low), pltpu.VMEM((cut, width), low), pltpu.SemaphoreType.DMA((2,))]
        + [pltpu.VMEM((2 * SIDE - 2, own // 2, width), jnp.float32)] * 2
        + [pltpu.SemaphoreType.DMA((2 * SIDE - 2,))] * 2,
        compiler_params=params(40),
        cost_estimate=spans(12),
    )(*operands)


SIDE = 4
MESH = pl.DeviceIdType.MESH


def remote(source, target, sends, recvs, at, device):
    return pltpu.make_async_remote_copy(
        src_ref=source, dst_ref=target, send_sem=sends.at[at], recv_sem=recvs.at[at],
        device_id=device, device_id_type=MESH,
    )


class Place:
    def __init__(self, count):
        here = lax.axis_index("seq")
        self.head = lax.axis_index("head")
        self.stride = count // SIDE
        self.groups = count // SIDE
        self.place, self.group = lax.rem(here, SIDE), here // SIDE
        self.z = here // self.stride
        base = here - self.place
        self.member = [(base + (self.place ^ k), self.head) for k in range(SIDE)]
        self.other = [
            (lax.rem(self.group + k, self.groups) * SIDE + self.place, self.head) for k in range(self.groups)
        ]
        self.core = (here, 1 - self.head)
        self.above = (lax.rem(here + self.stride, count), self.head)
        self.below = (lax.rem(here - self.stride + count, count), self.head)

    def greet(self):
        barrier = pltpu.get_barrier_semaphore()
        devices = self.member[1:] + self.other[1:] + [self.core]
        for device in devices:
            pl.semaphore_signal(barrier, inc=1, device_id=device, device_id_type=MESH)
        pl.semaphore_wait(barrier, len(devices))


class Line:
    def __init__(self, where, up_one, down_one, ring, rest, sends, recvs):
        self.where, self.up_one, self.down_one = where, up_one, down_one
        self.ring, self.rest, self.sends, self.recvs = ring, rest, sends, recvs

    def copies(self, step):
        w = self.where
        up = self.up_one if step == 2 else self.ring.at[SIDE - step]
        down = self.down_one if step == 2 else self.ring.at[step - 2]
        return (
            remote(up, self.ring.at[SIDE - 1 - step], self.sends, self.recvs, step - 1, w.above),
            remote(down, self.ring.at[step - 1], self.sends, self.recvs, SIDE - 2 + step, w.below),
        )

    def core(self, slot):
        return remote(self.ring.at[slot], self.rest.at[slot], self.sends, self.recvs, 2 * SIDE - 2 + slot, self.where.core)

    def start(self, step):
        up, down = self.copies(step)
        z = self.where.z
        pl.when((z >= step - 1) & (z < SIDE - 1))(up.start)
        pl.when((z <= SIDE - step) & (z > 0))(down.start)

    def arrive(self, step):
        up, down = self.copies(step)
        z = self.where.z

        @pl.when(z >= step)
        def _():
            up.wait_recv()
            self.core(SIDE - 1 - step).start()

        @pl.when(z <= SIDE - 1 - step)
        def _():
            down.wait_recv()
            self.core(step - 1).start()

    def cores_of_one(self):
        return (
            remote(self.up_one, self.rest.at[SIDE - 2], self.sends, self.recvs, 2 * SIDE - 2 + SIDE - 2, self.where.core),
            remote(self.down_one, self.rest.at[0], self.sends, self.recvs, 2 * SIDE - 2, self.where.core),
        )

    def start_cores_of_one(self):
        up, down = self.cores_of_one()
        pl.when(self.where.z >= 1)(up.start)
        pl.when(self.where.z <= SIDE - 2)(down.start)

    def finish_two(self):
        z = self.where.z
        up, down = self.copies(2)
        pl.when((z >= 1) & (z < SIDE - 1))(up.wait_send)
        pl.when((z <= SIDE - 2) & (z > 0))(down.wait_send)
        self.core(1).wait()
        pl.when(z >= 1)(self.core(SIDE - 2).wait)
        pl.when(z <= SIDE - 2)(self.core(0).wait)

    def finish_three(self):
        z = self.where.z
        up, down = self.copies(3)
        pl.when(z == SIDE - 2)(up.wait_send)
        pl.when(z == 1)(down.wait_send)
        for slot in range(SIDE - 1):
            self.core(slot).wait()


LINE_SEMS = 3 * (SIDE - 1)


class Side:
    def __init__(self, where, mine, side, rest, sends, recvs):
        self.where, self.mine, self.side, self.rest, self.sends, self.recvs = where, mine, side, rest, sends, recvs

    def near(self):
        return [
            remote(self.mine, self.side.at[k - 1], self.sends, self.recvs, k - 1, self.where.member[k]) for k in (1, 2)
        ]

    def far(self):
        half = self.side.shape[1] // 2
        top, low = pl.ds(0, half), pl.ds(half, half)
        return [
            remote(self.side.at[1, top], self.side.at[2, top], self.sends, self.recvs, 2, self.where.member[1]),
            remote(self.side.at[0, low], self.side.at[2, low], self.sends, self.recvs, 3, self.where.member[2]),
        ]

    def core(self, slot):
        return remote(self.side.at[slot], self.rest.at[slot], self.sends, self.recvs, 4 + slot, self.where.core)

    def start(self):
        for c in self.near():
            c.start()

    def turn(self):
        for c in self.near():
            c.wait_recv()
        for c in self.far():
            c.start()
        for slot in (0, 1):
            self.core(slot).start()

    def finish(self):
        for c in self.far():
            c.wait_recv()
        self.core(2).start()
        for c in self.near() + self.far():
            c.wait_send()
        for slot in range(3):
            self.core(slot).wait()


SIDE_SEMS = 7


def chain(where, reverse, summary, fall, rate_ref, out_ref, scratch, after_line, after_all):
    own, side, mine, line, back, done, sends, recvs = scratch
    streams, n, channels = out_ref.shape
    width = channels // SIDE
    rows = streams * n
    place, group, groups = where.place, where.group, where.groups
    sides = [remote(own.at[k], side.at[k], sends, recvs, k, where.member[k]) for k in range(1, SIDE)]

    def quarter(k, target):
        cols = pl.ds(pl.multiple_of((place ^ k) * width, 128), width)
        states = summary(cols)
        for s in range(streams):
            target[k, s * n : (s + 1) * n, :] = states[s]
            target[k, rows + s : rows + s + 1, :] = jnp.sum(fall[s, :, cols], axis=0, keepdims=True)
        target[k, rows + streams :, :] = jnp.zeros((target.shape[1] - rows - streams, width), jnp.float32)

    for k in range(1, SIDE):
        quarter(k, own)
        sides[k - 1].start()
    quarter(0, side)
    rate = rate_ref[:, pl.ds(pl.multiple_of(place * width, 128), width)]

    def through(steps):
        return jnp.concatenate([jnp.exp2(steps[s : s + 1] * rate) for s in range(streams)], axis=0)

    for c in sides:
        c.wait_recv()
    state, steps = jnp.zeros((rows, width), jnp.float32), jnp.zeros((streams, width), jnp.float32)
    before, passed = [None] * SIDE, [None] * SIDE
    for j in reversed(range(SIDE)) if reverse else range(SIDE):
        block = side[place ^ j]
        before[j], passed[j] = state, steps
        step = block[rows : rows + streams]
        state = through(step) * state + block[:rows]
        steps = steps + step
    mine[:rows, :] = state
    mine[rows : rows + streams, :] = steps
    mine[rows + streams :, :] = jnp.zeros((mine.shape[0] - rows - streams, width), jnp.float32)
    lines = [remote(mine, line.at[k], sends, recvs, SIDE + k, where.other[k]) for k in range(1, groups)]
    for c in lines:
        c.start()
    for c in lines:
        c.wait_recv()
    after_line()
    entering = jnp.zeros((rows, width), jnp.float32)
    for k in range(1, groups) if reverse else range(groups - 1, 0, -1):
        counts = (k > group) if reverse else (k <= group)
        block = line[k]
        new = through(block[rows : rows + streams]) * entering + block[:rows]
        entering = jnp.where(counts, new, entering)
    for j in range(SIDE):
        back[j] = through(passed[j]) * entering + before[j]
    backs = [
        remote(back.at[place ^ k], done.at[k], sends, recvs, SIDE + groups + k, where.member[k]) for k in range(1, SIDE)
    ]
    for c in backs:
        c.start()
    after_all()
    done[0] = back[place]
    for c in backs:
        c.wait_recv()
    for q in range(SIDE):
        out_ref[:, :, q * width : (q + 1) * width] = done[place ^ q].reshape(streams, n, width)
    for c in sides + lines + backs:
        c.wait_send()


def chain_scratch(streams, n, channels, groups):
    width = channels // SIDE
    rows = streams * n
    tall = rows + 8 * (-(-streams // 8))
    sems = pltpu.SemaphoreType.DMA((2 * SIDE + groups,))
    return [
        pltpu.VMEM((SIDE, tall, width), jnp.float32),
        pltpu.VMEM((SIDE, tall, width), jnp.float32),
        pltpu.VMEM((tall, width), jnp.float32),
        pltpu.VMEM((groups, tall, width), jnp.float32),
        pltpu.VMEM((SIDE, rows, width), jnp.float32),
        pltpu.VMEM((SIDE, rows, width), jnp.float32),
        sems,
        sems,
    ]


def blocks_of(channels):
    lanes = pieces(channels)
    return lanes, channels // lanes


def columns(i, lanes):
    return pl.ds(pl.multiple_of(i * lanes, lanes), lanes)


def forward_kernel(
    count, fall, gain, b_ref, c_ref, rate_ref, up_one, down_one, norm_near, norm_next,
    y_ref, first, ring, ring_rest, side_far, side_rest,
    line_send, line_recv, side_send, side_recv, *scratch,
):
    where = Place(count)
    streams, length, channels = fall.shape
    n = rate_ref.shape[0]
    lanes, blocks = blocks_of(channels)
    z = where.z
    where.greet()
    line = Line(where, up_one, down_one, ring, ring_rest, line_send, line_recv)

    def summary(cols):
        rate = rate_ref[:, cols]
        span = rate.shape[1]

        def chunk(i, states):
            base = pl.multiple_of(i * ROWS, ROWS)
            out = []
            for s in range(streams):
                state = states[s]
                d = fall[s, pl.ds(base, ROWS), cols]
                x = gain[s, pl.ds(base, ROWS), cols]
                for j in range(ROWS):
                    b = b_ref[s, pl.ds(pl.multiple_of((base + j) * n, n), n), :]
                    fade = jnp.exp2(d[j : j + 1] * rate)
                    state = fade * state + x[j : j + 1] * wide(b, span)
                out.append(state)
            return tuple(out)

        start = tuple(jnp.zeros((n, span), jnp.float32) for _ in range(streams))
        return lax.fori_loop(0, length // ROWS, chunk, start)

    half = norm_near.shape[0] // 2
    top, low = pl.ds(0, half), pl.ds(half, half)
    far = [
        remote(norm_next.at[top], side_far.at[top], side_send, side_recv, 0, where.member[1]),
        remote(norm_near.at[low], side_far.at[low], side_send, side_recv, 1, where.member[2]),
    ]
    cores = [
        remote(part, side_rest.at[k], side_send, side_recv, 2 + k, where.core)
        for k, part in enumerate((norm_near, norm_next, side_far))
    ]

    def after_line():
        line.start_cores_of_one()
        line.start(2)

    def after_all():
        for c in far + cores[:2]:
            c.start()

    chain(where, False, summary, fall, rate_ref, first, scratch, after_line, after_all)

    def run(i, _):
        cols = columns(i, lanes)
        rate = rate_ref[:, cols]

        def chunk(i, states):
            base = pl.multiple_of(i * ROWS, ROWS)
            out = []
            for s in range(streams):
                state = states[s]
                d = fall[s, pl.ds(base, ROWS), cols]
                x = gain[s, pl.ds(base, ROWS), cols]
                rows = []
                for j in range(ROWS):
                    at = pl.ds(pl.multiple_of((base + j) * n, n), n)
                    fade = jnp.exp2(d[j : j + 1] * rate)
                    state = fade * state + x[j : j + 1] * wide(b_ref[s, at, :], lanes)
                    rows.append(jnp.sum(state * wide(c_ref[s, at, :], lanes), axis=0, keepdims=True))
                y_ref[s, pl.ds(base, ROWS), cols] = jnp.concatenate(rows, axis=0)
                out.append(state)
            return tuple(out)

        lax.fori_loop(0, length // ROWS, chunk, tuple(first[s, :, cols] for s in range(streams)))
        return 0

    lax.fori_loop(0, blocks, run, 0)
    for c in far:
        c.wait_recv()
    cores[2].start()
    line.arrive(2)
    for c in far:
        c.wait_send()
    for c in cores:
        c.wait()
    line.finish_two()


def backward_kernel(
    count, fall, d_ref, v_ref, g_ref, b_ref, c_ref, rate_ref, first_ref, up_one, down_one, mix, grad_middle,
    dstep_ref, dvalue_ref, db_ref, dc_ref, decay_ref, ring, ring_rest, side, side_rest, grad_end, grad_rest,
    db_wide, dc_wide, last, path, fades, line_send, line_recv, side_send, side_recv, *scratch,
):
    where = Place(count)
    streams, length, channels = fall.shape
    n = rate_ref.shape[0]
    lanes, blocks = blocks_of(channels)
    chunks = length // ROWS
    width = channels // SIDE
    where.greet()
    line = Line(where, up_one, down_one, ring, ring_rest, line_send, line_recv)
    z = where.z
    rise = remote(grad_middle, grad_end, line_send, line_recv, LINE_SEMS, where.above)
    sink = remote(grad_middle, grad_end, line_send, line_recv, LINE_SEMS + 1, where.below)
    core = remote(grad_end, grad_rest, line_send, line_recv, LINE_SEMS + 2, where.core)
    square = Side(where, mix, side, side_rest, side_send, side_recv)
    half = ring.shape[1] // 2
    steps = []
    for part in range(2):
        at = pl.ds(part * half, half)
        steps.append(
            (
                remote(up_one.at[at], ring.at[1, at], line_send, line_recv, LINE_SEMS + 3 + 2 * part, where.above),
                remote(down_one.at[at], ring.at[1, at], line_send, line_recv, LINE_SEMS + 4 + 2 * part, where.below),
            )
        )

    def start_half(part):
        up, down = steps[part]
        pl.when((z >= 1) & (z < SIDE - 1))(up.start)
        pl.when((z <= SIDE - 2) & (z > 0))(down.start)

    start_half(0)
    line.start_cores_of_one()

    def summary(cols):
        rate = rate_ref[:, cols]
        span = rate.shape[1]

        def chunk(i, carry):
            base = pl.multiple_of((chunks - 1 - i) * ROWS, ROWS)
            out = []
            for s in range(streams):
                carried = carry[s]
                d = fall[s, pl.ds(base, ROWS), cols]
                g = g_ref[s, pl.ds(base, ROWS), cols]
                for j in reversed(range(ROWS)):
                    at = pl.ds(pl.multiple_of((base + j) * n, n), n)
                    fade = jnp.exp2(d[j : j + 1] * rate)
                    carried = fade * (g[j : j + 1] * wide(c_ref[s, at, :], span) + carried)
                out.append(carried)
            return tuple(out)

        start = tuple(jnp.zeros((n, span), jnp.float32) for _ in range(streams))
        return lax.fori_loop(0, chunks, chunk, start)

    def after_line():
        start_half(1)
        pl.when(z == SIDE - 2)(rise.start)
        pl.when(z == 1)(sink.start)

    def after_all():
        square.start()

    chain(where, True, summary, fall, rate_ref, last, scratch, after_line, after_all)
    db_wide[...] = jnp.zeros_like(db_wide)
    dc_wide[...] = jnp.zeros_like(dc_wide)

    def fold(tile):
        out = tile[:, :128]
        for k in range(1, lanes // 128):
            out = out + tile[:, k * 128 : (k + 1) * 128]
        return out

    def run(i, _):
        cols = columns(i, lanes)
        rate = rate_ref[:, cols]

        @pl.when(i == blocks // 3)
        def _():
            for up, down in steps:
                pl.when(z >= 2)(up.wait_recv)
                pl.when(z <= SIDE - 3)(down.wait_recv)
            line.core(1).start()
            line.start(3)

        @pl.when(i == blocks // 2)
        def _():
            square.turn()

        def ahead(i, states):
            base = pl.multiple_of(i * ROWS, ROWS)
            out = []
            for s in range(streams):
                state = states[s]
                d = fall[s, pl.ds(base, ROWS), cols]
                x = d_ref[s, pl.ds(base, ROWS), cols] * v_ref[s, pl.ds(base, ROWS), cols]
                for j in range(ROWS):
                    at = pl.ds(pl.multiple_of((base + j) * n, n), n)
                    path[s, at, :] = state
                    fade = jnp.exp2(d[j : j + 1] * rate)
                    fades[s, at, :] = fade
                    state = fade * state + x[j : j + 1] * wide(b_ref[s, at, :], lanes)
                out.append(state)
            return tuple(out)

        tails = lax.fori_loop(0, chunks, ahead, tuple(first_ref[s, :, cols] for s in range(streams)))

        def back(i, carry):
            base = pl.multiple_of((chunks - 1 - i) * ROWS, ROWS)
            out = []
            decay = carry[-1]
            for s in range(streams):
                state, carried = carry[s]
                d = d_ref[s, pl.ds(base, ROWS), cols]
                v = v_ref[s, pl.ds(base, ROWS), cols]
                g = g_ref[s, pl.ds(base, ROWS), cols]
                x = d * v
                weights, touches = [None] * ROWS, [None] * ROWS
                for j in reversed(range(ROWS)):
                    at = pl.ds(pl.multiple_of((base + j) * n, n), n)
                    gj = g[j : j + 1]
                    adjoint = gj * wide(c_ref[s, at, :], lanes) + carried
                    dc_wide[s, at, :] += fold(state * gj)
                    db_wide[s, at, :] += fold(adjoint * x[j : j + 1])
                    weights[j] = jnp.sum(adjoint * wide(b_ref[s, at, :], lanes), axis=0, keepdims=True)
                    carried = adjoint * fades[s, at, :]
                    state = path[s, at, :]
                    touch = carried * state
                    touches[j] = jnp.sum(touch * rate, axis=0, keepdims=True)
                    decay = decay + touch * d[j : j + 1]
                weighted = jnp.concatenate(weights, axis=0)
                at = pl.ds(base, ROWS)
                dstep_ref[s, at, cols] = weighted * v + jnp.concatenate(touches, axis=0) * LN2
                dvalue_ref[s, at, cols] = weighted * d
                out.append((state, carried))
            return tuple(out) + (decay,)

        start = tuple((tails[s], last[s, :, cols]) for s in range(streams))
        done = lax.fori_loop(0, chunks, back, start + (jnp.zeros((n, lanes), jnp.float32),))
        decay_ref[:, cols] = done[-1]
        return 0

    lax.fori_loop(0, blocks, run, 0)
    for s in range(streams):
        db_ref[s] = jnp.sum(db_wide[s].reshape(length, n, 128), axis=-1)
        dc_ref[s] = jnp.sum(dc_wide[s].reshape(length, n, 128), axis=-1)
    square.finish()
    line.arrive(3)
    pl.when(z == SIDE - 1)(rise.wait_recv)
    pl.when(z == 0)(sink.wait_recv)
    pl.when((z == 0) | (z == SIDE - 1))(core.start)
    line.finish_three()
    for up, down in steps:
        pl.when((z >= 1) & (z < SIDE - 1))(up.wait_send)
        pl.when((z <= SIDE - 2) & (z > 0))(down.wait_send)
    pl.when(z == SIDE - 2)(rise.wait_send)
    pl.when(z == 1)(sink.wait_send)
    pl.when((z == 0) | (z == SIDE - 1))(core.wait)


def in_vmem():
    return pl.BlockSpec(memory_space=pltpu.VMEM)


def in_hbm():
    return pl.BlockSpec(memory_space=pl.ANY)


def shaped(*shape):
    return jax.ShapeDtypeStruct(shape, jnp.float32)


def sems(count):
    return [pltpu.SemaphoreType.DMA((count,))] * 2


def scan_forward(fall, gain, b_wide, c_wide, rate, line, norm_near, norm_next):
    streams, length, channels = fall.shape
    n = rate.shape[0]
    count = lax.axis_size("seq")
    half, width = norm_near.shape
    three = shaped(SIDE - 1, half, width)
    return pl.pallas_call(
        functools.partial(forward_kernel, count),
        out_shape=[shaped(streams, length, channels), shaped(streams, n, channels), three, three, shaped(half, width), three],
        in_specs=[in_vmem()] * 5 + [in_hbm()] * 4,
        out_specs=[in_vmem()] * 2 + [in_hbm()] * 4,
        scratch_shapes=sems(LINE_SEMS) + sems(5)
        + chain_scratch(streams, n, channels, count // SIDE),
        compiler_params=pltpu.CompilerParams(
            collective_id=0, has_side_effects=True, vmem_limit_bytes=56 * 1024 * 1024
        ),
        cost_estimate=spans(40),
    )(fall, gain, b_wide, c_wide, rate, *line, norm_near, norm_next)


def scan_backward(fall, step, value, d_y, b_wide, c_wide, rate, first, line, mix, grad_middle):
    streams, length, channels = fall.shape
    n = rate.shape[0]
    count = lax.axis_size("seq")
    half, width = mix.shape
    lanes, _ = blocks_of(channels)
    three = shaped(SIDE - 1, half, width)
    tall = shaped(streams, length, n)
    flat = shaped(streams, length, channels)
    kept = pltpu.VMEM((streams, length * n, lanes), jnp.float32)
    return pl.pallas_call(
        functools.partial(backward_kernel, count),
        out_shape=[flat, flat, tall, tall, shaped(n, channels), three, three, three, three, shaped(half, width), shaped(half, width)],
        in_specs=[in_vmem()] * 8 + [in_hbm()] * 4,
        out_specs=[in_vmem()] * 5 + [in_hbm()] * 6,
        scratch_shapes=[
            pltpu.VMEM((streams, length * n, 128), jnp.float32),
            pltpu.VMEM((streams, length * n, 128), jnp.float32),
            pltpu.VMEM((streams, n, channels), jnp.float32),
            kept,
            kept,
        ]
        + sems(LINE_SEMS + 7) + sems(SIDE_SEMS)
        + chain_scratch(streams, n, channels, count // SIDE),
        compiler_params=pltpu.CompilerParams(
            collective_id=1, has_side_effects=True, vmem_limit_bytes=56 * 1024 * 1024
        ),
        cost_estimate=spans(62),
    )(fall, step, value, d_y, b_wide, c_wide, rate, first, *line, mix, grad_middle)


CHUNKS = 8
EARLY = 6


def fetch_line(z, up, down, middle, first, last, rest, rest_first, rest_last, stage, arrived):
    def copy(block, k):
        return pltpu.make_async_copy(block, stage.at[k], arrived.at[k])

    copy(middle, 1).start()
    copy(rest.at[1], 4).start()

    @pl.when(z >= 1)
    def _():
        copy(up, 2).start()
        copy(rest.at[2], 5).start()

    @pl.when(z < 1)
    def _():
        copy(last, 2).start()
        copy(rest_last, 5).start()

    @pl.when(z <= SIDE - 2)
    def _():
        copy(down, 0).start()
        copy(rest.at[0], 3).start()

    @pl.when(z > SIDE - 2)
    def _():
        copy(first, 0).start()
        copy(rest_first, 3).start()

    def put(target, own):
        rows, size = own.shape[0], stage.shape[1]
        target[:rows, :] = own[...].astype(target.dtype)
        for k in range(2 * SIDE - 2):
            copy(middle, k).wait()
            target[rows + k * size : rows + (k + 1) * size, :] = stage[k].astype(target.dtype)

    return put


def ffn_kernel(
    count, hid_own, hid_up, hid_down, hid_ring, hid_rest, grad_own, grad_up, grad_down, grad_middle, grad_rest, grad_end, grad_rest_end, wg, wu, wd, dg_own, du_own, act_own,
    mixer, out, near, passed,
    hid, grad, hid_cut, grad_cut, dg, du, act, stash, got, sent, sends, recvs, local, hid_stage, grad_stage, hid_got, grad_got,
):
    own, cut = hid_own.shape[0], hid_cut.shape[0]
    where = Place(count)
    z, place = where.z, where.place
    first = pl.program_id(0) == 0
    last = pl.program_id(0) == pl.num_programs(0) - 1
    odd, far = lax.rem(place, 2), place // 2
    early = [
        remote(
            stash.at[c, :, :, :, 1 - odd] if c % 2 == 0 else stash.at[c, :, :, 1 - far],
            near.at[c], sends, recvs, c, where.member[1 + c % 2],
        )
        for c in range(EARLY)
    ]
    tips, rising = (z == 0) | (z == SIDE - 1), z < SIDE // 2

    def along(source, target, at, up):
        return remote(source, target, sends, recvs, at, (jnp.where(up, where.above[0], where.below[0]), where.head))

    one = along(mixer.at[:, SIDE - 1 - z], got, EARLY, z == 0)
    fetch = pltpu.make_async_copy(mixer.at[:, lax.rem(z + 2, SIDE)], sent, local.at[0])
    way = jnp.where(rising, 0, 1)
    two = along(sent, passed.at[way], EARLY + 1 + way, rising)
    from_below = along(sent, passed.at[0], EARLY + 1, True)
    from_above = along(sent, passed.at[1], EARLY + 2, False)

    @pl.when(first)
    def _():
        ring, rest = hid_ring, hid_rest
        put_hid = fetch_line(
            z, hid_up, hid_down, ring.at[1], ring.at[0], ring.at[2], rest, rest.at[0], rest.at[2], hid_stage, hid_got
        )
        ends = (grad_middle, grad_end, grad_end, grad_rest, grad_rest_end, grad_rest_end)
        put_grad = fetch_line(z, grad_up, grad_down, *ends, grad_stage, grad_got)
        where.greet()
        fetch.start()
        pl.when(tips)(one.start)
        fetch.wait()
        pl.when(tips)(two.start)
        put_hid(hid, hid_own)
        put_grad(grad, grad_own)
        at = pl.ds(pl.multiple_of(z * cut, 128), cut)
        hid_cut[...] = hid[:, at].T
        grad_cut[...] = grad[:, at].T

    dg[:own, :] = dg_own[...]
    du[:own, :] = du_own[...]
    act[:own, :] = act_own[...]

    def turn(i, _):
        rows = pl.ds(pl.multiple_of(i * own, own), own)
        gate = dot(hid[rows, :], wg[...])
        up = dot(hid[rows, :], wu[...])
        d_act = dot_back(grad[rows, :], wd[...])
        sig = 1.0 / (1.0 + jnp.exp(-gate))
        silu = gate * sig
        dg[rows, :] = (d_act * up * (sig + silu * (1.0 - sig))).astype(dg.dtype)
        du[rows, :] = (d_act * silu).astype(du.dtype)
        act[rows, :] = (silu * up).astype(act.dtype)
        return 0

    lax.fori_loop(1, hid.shape[0] // own, turn, 0)
    out[0] = dot(hid_cut[...], dg[...])
    out[1] = dot(hid_cut[...], du[...])
    out[2] = dot(grad_cut[...], act[...])

    for c in range(EARLY):

        @pl.when(pl.program_id(0) == c)
        def _():
            for m in range(3):
                stash[c, m] = out[m].reshape(stash.shape[2:])
            early[c].start()

    @pl.when((pl.program_id(0) == pl.num_programs(0) // 2 + 1) & jnp.logical_not(tips))
    def _():
        one.wait_recv()
        sent[...] += got[...]
        two.start()

    @pl.when(last)
    def _():
        for c in early:
            c.wait()
        pl.when(tips)(one.wait_send)
        two.wait_send()

        @pl.when(jnp.logical_not(tips))
        def _():
            from_below.wait_recv()
            from_above.wait_recv()


def ffn_grads(hidden, out_grad, w_gate, w_up, w_down, d_gate, d_up, act, mixer):
    hid_own = hidden[0]
    own, width = hid_own.shape
    units = w_gate.shape[1]
    count = lax.axis_size("seq")
    cut = width // SIDE
    block = units // CHUNKS
    more = count // SIDE // SIDE
    rows = cut // (more * SIDE)
    tokens = own * SIDE
    low = jnp.bfloat16
    column = lambda rows: pl.BlockSpec((rows, block), lambda i: (0, i))
    tokens_in = (*hidden, *out_grad)
    return pl.pallas_call(
        functools.partial(ffn_kernel, count),
        grid=(units // block,),
        in_specs=[whole(a.shape) if a is hid_own or a is out_grad[0] else in_hbm() for a in tokens_in]
        + [column(width), column(width), pl.BlockSpec((block, width), lambda i: (i, 0))]
        + [column(own)] * 3
        + [in_hbm()],
        out_specs=[pl.BlockSpec((3, cut, block), lambda i: (0, 0, i))] + [in_hbm()] * 2,
        out_shape=[shaped(3, cut, units), shaped(EARLY, 3, more, 2, rows, block), shaped(2, 2, *mixer.shape[2:])],
        scratch_shapes=[pltpu.VMEM((tokens, width), low)] * 2
        + [pltpu.VMEM((cut, tokens), low)] * 2
        + [pltpu.VMEM((tokens, block), low)] * 3
        + [pltpu.VMEM((EARLY, 3, more, 2, 2, rows, block), jnp.float32)]
        + [pltpu.VMEM((2, *mixer.shape[2:]), jnp.float32)] * 2
        + sems(EARLY + 3) + [pltpu.SemaphoreType.DMA((1,))]
        + [pltpu.VMEM((2 * SIDE - 2, own // 2, width), jnp.float32)] * 2
        + [pltpu.SemaphoreType.DMA((2 * SIDE - 2,))] * 2,
        compiler_params=pltpu.CompilerParams(
            collective_id=2, has_side_effects=True, vmem_limit_bytes=56 * 1024 * 1024
        ),
        cost_estimate=spans(36),
    )(*tokens_in, w_gate, w_up, w_down, d_gate, d_up, act, mixer)


class Reduce:
    def __init__(self, where, blocks, got, passed, arrived, sends, recvs):
        self.where, self.blocks, self.got, self.passed, self.arrived = where, blocks, got, passed, arrived
        self.sends, self.recvs = sends, recvs

    def out(self, source, target, at, rising):
        w = self.where
        return remote(source, target, self.sends, self.recvs, at, (jnp.where(rising, w.above[0], w.below[0]), w.head))

    def one(self):
        return self.out(self.blocks.at[:, SIDE - 1 - self.where.z], self.got, 0, self.where.z == 0)

    def start_one(self):
        pl.when((self.where.z == 0) | (self.where.z == SIDE - 1))(self.one().start)

    def middle(self):
        return (self.where.z > 0) & (self.where.z < SIDE - 1)

    def two(self, source):
        rising = self.where.z < SIDE // 2
        return self.out(source, self.passed.at[jnp.where(rising, 0, 1)], jnp.where(rising, 1, 2), rising)

    def start_two(self):
        z = self.where.z

        @pl.when(self.middle())
        def _():
            self.one().wait_recv()
            self.got[...] += self.blocks[:, lax.rem(z + 2, SIDE)]
            self.two(self.got).start()

        @pl.when(jnp.logical_not(self.middle()))
        def _():
            self.two(self.blocks.at[:, lax.rem(z + 2, SIDE)]).start()

    def three(self, source, way):
        return self.out(source, self.arrived.at[way], 3 + way, way == 0)

    def start_three(self, wait):
        z = self.where.z

        @pl.when(self.middle())
        def _():
            for way in (0, 1):
                if wait:
                    self.two_from(way).wait_recv()
                self.passed[way] += self.blocks[:, z + 1 - 2 * way]
                self.three(self.passed.at[way], way).start()

        pl.when(z == 0)(self.three(self.blocks.at[:, 1], 0).start)
        pl.when(z == SIDE - 1)(self.three(self.blocks.at[:, SIDE - 2], 1).start)

    def two_from(self, way):
        return self.out(self.passed.at[way], self.passed.at[way], 1 + way, way == 0)

    def result(self, done):
        z = self.where.z
        done[...] = self.blocks[:, z].reshape(done.shape)
        for way in (0, 1):

            @pl.when((z >= 1) if way == 0 else (z <= SIDE - 2))
            def _():
                self.three(self.passed.at[way], way).wait_recv()
                done[...] += self.arrived[way].reshape(done.shape)

    def finish(self, first):
        z = self.where.z
        if first <= 1:
            pl.when((z == 0) | (z == SIDE - 1))(self.one().wait_send)
        if first <= 2:
            self.two(self.got).wait_send()
        pl.when(z <= SIDE - 2)(self.three(self.passed.at[0], 0).wait_send)
        pl.when(z >= 1)(self.three(self.passed.at[1], 1).wait_send)


REDUCE_SEMS = 5


def sum_kernel(
    count, ffn, mixer_in, passed_in, d_inner, near_in, turned, d_own, small,
    ffn_out, mixer_out, inner_out, small_out,
    d_all, kept, near, next_, mixer, m_passed, m_arrived, d_side, inner, i_got, i_passed, i_arrived, m_done, m_back, i_done, i_back, s_near, s_next, s_done, s_line,
    ffn_send, ffn_recv, m_send, m_recv, i_send, i_recv, back_send, back_recv, s_send, s_recv, d_send, d_recv, local,
):
    where = Place(count)
    place = where.place
    more = where.stride // SIDE
    span = near.shape[5]
    odd, far = lax.rem(place, 2), place // 2
    cols = [pl.ds(c * span, span) for c in range(CHUNKS)]
    loads = [pltpu.make_async_copy(mixer_in, mixer, local.at[0]), pltpu.make_async_copy(passed_in, m_passed, local.at[1])]
    keeps = [
        pltpu.make_async_copy(
            ffn.at[:, :, :, odd, :, cols[c]] if c % 2 == 0 else ffn.at[:, :, far, :, :, cols[c]], kept.at[c], local.at[3 + c]
        )
        for c in range(CHUNKS)
    ]
    nears = [pltpu.make_async_copy(near_in.at[c], near.at[c], local.at[3 + CHUNKS + c]) for c in range(EARLY)]
    for c in loads + nears + keeps:
        c.start()
    where.greet()
    first = {
        c: remote(
            ffn.at[:, :, :, 1 - odd, :, cols[c]] if c % 2 == 0 else ffn.at[:, :, 1 - far, :, :, cols[c]],
            near.at[c], ffn_send, ffn_recv, c, where.member[1 + c % 2],
        )
        for c in range(EARLY, CHUNKS)
    }
    size = inner.shape[3]
    quarters = [
        remote(
            d_inner.at[:, :, pl.ds(pl.multiple_of((place ^ k) * size, 128), size)], d_side.at[k - 1],
            d_send, d_recv, k - 1, where.member[k],
        )
        for k in range(1, SIDE)
    ]
    for c in quarters:
        c.start()
    for c in first.values():
        c.start()
    groups, half = where.groups, s_near.shape[3]
    s_rows = [pl.ds(0, half), pl.ds(half, half)]
    s_first = [
        remote(small.at[:, :, 1 - odd, s_rows[0]], s_near.at[0], s_send, s_recv, 0, where.member[1]),
        remote(small.at[:, 1 - far, :, s_rows[1]], s_near.at[1], s_send, s_recv, 1, where.member[2]),
    ]
    for c in s_first:
        c.start()
    second = {}

    def again(c):
        kept[c] += near[c]
        bit = far if c % 2 == 0 else odd
        second[c] = remote(
            kept.at[c, :, :, 1 - bit], next_.at[c], ffn_send, ffn_recv, CHUNKS + c, where.member[2 - c % 2]
        )
        second[c].start()

    line = Reduce(where, mixer, None, m_passed, m_arrived, m_send, m_recv)
    for c in loads:
        c.wait()
    line.start_three(False)
    for c in range(EARLY):
        nears[c].wait()
        keeps[c].wait()
        again(c)
    for c in quarters:
        c.wait_recv()
    own = d_own.shape[0]
    part = own // 2
    d_all[:own, :] = d_own[...]
    for k in range(SIDE - 1):
        for s in range(2):
            start = own + (s * (SIDE - 1) + k) * part
            d_all[start : start + part, :] = d_side[k, where.head if s == 0 else 1 - where.head].astype(d_all.dtype)
    for k in range(SIDE):
        at = slice(k * inner.shape[2], (k + 1) * inner.shape[2])
        inner[0, k] = dot(turned[at, :], d_all[...])
    other = Reduce(where, inner, i_got, i_passed, i_arrived, i_send, i_recv)
    other.start_one()
    other.start_two()
    for c in s_first:
        c.wait_recv()
    s_near[0] += small[:, :, odd, s_rows[0]]
    s_near[1] += small[:, far, :, s_rows[1]]
    s_second = [
        remote(s_near.at[0, :, 1 - far], s_next.at[0], s_send, s_recv, 2, where.member[2]),
        remote(s_near.at[1, :, 1 - odd], s_next.at[1], s_send, s_recv, 3, where.member[1]),
    ]
    for c in s_second:
        c.start()
    for c in range(EARLY, CHUNKS):
        keeps[c].wait()
        first[c].wait_recv()
        again(c)
    for c in s_second:
        c.wait_recv()
    s_done[:, :half] = s_near[0, :, far] + s_next[0]
    s_done[:, half:] = s_near[1, :, odd] + s_next[1]
    s_last = [
        remote(s_done.at[lax.rem(where.group + k, groups)], s_line.at[k], s_send, s_recv, 3 + k, where.other[k])
        for k in range(1, groups)
    ]
    for c in s_last:
        c.start()
    other.start_three(True)

    def spread(reduced, done, back, at):
        reduced.result(done)
        copies = [
            remote(done.at[:, :, place ^ k], back.at[k], back_send, back_recv, at + k, where.member[k])
            for k in range(1, SIDE)
        ]
        for c in copies:
            c.start()
        back[0] = done[:, :, place]
        return copies

    spreads = spread(line, m_done, m_back, 0)
    for c in range(CHUNKS):
        second[c].wait_recv()
        bit = far if c % 2 == 0 else odd
        ffn_out[:, :, :, c * span : (c + 1) * span] = kept[c, :, :, bit] + next_[c]
    spreads += spread(other, i_done, i_back, SIDE)
    for c in spreads:
        c.wait_recv()
    width = inner.shape[3]
    for q in range(SIDE):
        cols = slice(q * width, (q + 1) * width)
        mixer_out[:, :, :, cols] = m_back[place ^ q]
        inner_out[:, :, :, cols] = i_back[place ^ q]
    total = s_done[where.group]
    for k in range(1, groups):
        s_last[k - 1].wait_recv()
        total = total + s_line[k]
    small_out[...] = total
    for c in list(first.values()) + list(second.values()) + spreads + s_first + s_second + s_last:
        c.wait_send()
    for c in quarters:
        c.wait_send()
    line.finish(3)
    other.finish(1)


def sum_grads(ffn, mixer, passed, d_inner, near, turned, d_own, small):
    count = lax.axis_size("seq")
    more = count // SIDE // SIDE
    cut, units = ffn.shape[1:]
    rows = cut // (more * SIDE)
    size = mixer.shape[-1]
    f32 = jnp.float32
    v = lambda *shape: pltpu.VMEM(shape, f32)
    groups, tall = count // SIDE, small.shape[1]
    return pl.pallas_call(
        functools.partial(sum_kernel, count),
        out_shape=[shaped(3, more, rows, units), shaped(2, more, rows, size * SIDE), shaped(1, more, rows, size * SIDE),
                   shaped(tall, LANES)],
        in_specs=[in_hbm()] * 5 + [in_vmem()] * 3,
        out_specs=[in_vmem()] * 4,
        scratch_shapes=[
            pltpu.VMEM((turned.shape[1], size), jnp.bfloat16),
            v(CHUNKS, 3, more, 2, rows, units // CHUNKS),
            v(CHUNKS, 3, more, 2, rows, units // CHUNKS),
            v(CHUNKS, 3, more, rows, units // CHUNKS),
            v(2, SIDE, cut, size), v(2, 2, cut, size), v(2, 2, cut, size),
            v(SIDE - 1, *d_inner.shape[:2], size),
            v(1, SIDE, cut, size), v(1, cut, size), v(2, 1, cut, size), v(2, 1, cut, size),
            v(2, more, SIDE, rows, size), v(SIDE, 2, more, rows, size),
            v(1, more, SIDE, rows, size), v(SIDE, 1, more, rows, size),
            v(2, groups, 2, tall // 2, LANES), v(2, groups, tall // 2, LANES), v(groups, tall, LANES), v(groups, tall, LANES),
        ]
        + sems(2 * CHUNKS) + sems(REDUCE_SEMS) + sems(REDUCE_SEMS) + sems(2 * SIDE) + sems(3 + groups) + sems(SIDE) + [pltpu.SemaphoreType.DMA((3 + CHUNKS + EARLY,))],
        compiler_params=pltpu.CompilerParams(
            collective_id=3, has_side_effects=True, vmem_limit_bytes=58 * 1024 * 1024
        ),
        cost_estimate=spans(100),
    )(ffn.reshape(3, more, 2, 2, rows, units), mixer, passed, d_inner, near, turned, d_own, small.reshape(groups, 2, 2, tall, LANES))


def middle_kernel(
    count, hid, grad, wg, wu, wd, hidden, y,
    dg, du, act, ffn, d_hid, up_one, down_one, y_side, sends, recvs,
):
    where = Place(count)
    z, place = where.z, where.place
    width = y_side.shape[-1]
    quarters = [
        remote(
            y.at[:, :, pl.ds(pl.multiple_of((place ^ k) * width, 128), width)], y_side.at[k - 1],
            sends, recvs, k - 1, where.member[k],
        )
        for k in range(1, SIDE)
    ]
    mine = hidden.at[where.head]
    up = remote(mine, up_one, sends, recvs, SIDE - 1, where.above)
    down = remote(mine, down_one, sends, recvs, SIDE, where.below)

    @pl.when(pl.program_id(0) == 0)
    def _():
        where.greet()
        pl.when(z < SIDE - 1)(up.start)
        pl.when(z > 0)(down.start)
        for c in quarters:
            c.start()
        ffn[...] = jnp.zeros_like(ffn)
        d_hid[...] = jnp.zeros_like(d_hid)

    gate = dot(hid[...], wg[...])
    raised = dot(hid[...], wu[...])
    d_act = dot_back(grad[...], wd[...])
    sig = 1.0 / (1.0 + jnp.exp(-gate))
    silu = gate * sig
    dg[...] = (d_act * raised * (sig + silu * (1.0 - sig))).astype(dg.dtype)
    du[...] = (d_act * silu).astype(du.dtype)
    act[...] = (silu * raised).astype(act.dtype)
    ffn[...] += dot(act[...], wd[...])
    d_hid[...] += dot_back(dg[...], wg[...]) + dot_back(du[...], wu[...])

    @pl.when(pl.program_id(0) == pl.num_programs(0) - 1)
    def _():
        for c in quarters:
            c.wait()
        pl.when(z < SIDE - 1)(up.wait_send)
        pl.when(z > 0)(down.wait_send)
        pl.when(z > 0)(up.wait_recv)
        pl.when(z < SIDE - 1)(down.wait_recv)


def feed_forward(hid, grad, w_gate, w_up, w_down, hidden, y):
    own, width = hid.shape
    units = w_gate.shape[1]
    count = lax.axis_size("seq")
    streams, length, channels = y.shape
    block = next(b for b in (256, 128) if units % b == 0)
    column = lambda rows: pl.BlockSpec((rows, block), lambda i: (0, i))
    low = jax.ShapeDtypeStruct((own, units), jnp.bfloat16)
    flat = shaped(own, width)
    one = shaped(length, width)
    return pl.pallas_call(
        functools.partial(middle_kernel, count),
        grid=(units // block,),
        in_specs=[whole(hid.shape), whole(grad.shape), column(width), column(width),
                  pl.BlockSpec((block, width), lambda i: (i, 0)), in_hbm(), in_hbm()],
        out_specs=[column(own)] * 3 + [whole(flat.shape)] * 2 + [in_hbm()] * 3,
        out_shape=[low, low, low, flat, flat, one, one, shaped(SIDE - 1, streams, length, channels // SIDE)],
        scratch_shapes=sems(SIDE + 1),
        compiler_params=pltpu.CompilerParams(
            collective_id=4, has_side_effects=True, vmem_limit_bytes=56 * 1024 * 1024
        ),
        cost_estimate=spans(20),
    )(hid, grad, w_gate, w_up, w_down, hidden, y)


LANES = 128


def gather_kernel(places, w_step, log_decay, select, *refs):
    rows, out = refs[:-1], refs[-1]
    ranks, states = w_step.shape[0], log_decay.shape[0]
    size = w_step.shape[1] // places
    high = select.shape[0] // places
    low = ranks + states + 16
    out[...] = jnp.zeros_like(out)
    for p in range(places):
        cols = slice(p * size, (p + 1) * size)
        out[p, :ranks, :size] = w_step[:, cols]
        out[p, ranks : ranks + states, :size] = log_decay[:, cols]
        for k, row in enumerate(rows):
            out[p, ranks + states + k : ranks + states + k + 1, :size] = row[:, cols]
        for b in range(select.shape[1] // LANES):
            out[p, low + b * high : low + (b + 1) * high, :] = select[
                p * high : (p + 1) * high, b * LANES : (b + 1) * LANES
            ]


def gather_small(w_step, log_decay, select, rows):
    places = lax.axis_size("seq")
    channels = w_step.shape[1]
    tall = w_step.shape[0] + log_decay.shape[0] + 16 + select.shape[0] // places * (channels // LANES)
    tall = -(-tall // 16) * 16
    return pl.pallas_call(
        functools.partial(gather_kernel, places),
        out_shape=shaped(places, tall, LANES),
        in_specs=[in_vmem()] * (3 + len(rows)),
        out_specs=in_vmem(),
        compiler_params=params(12),
        cost_estimate=spans(4),
    )(w_step, log_decay, select, *[row.reshape(1, -1) for row in rows])


def place_kernel(rank, states, taps, high, size, gains, ffn, mixer, inner, small, *outs):
    gate, up, down, mixout, outgate, w_in, w_step, log_decay, conv_taps, w_select = outs[:10]
    gate[...] = ffn[0]
    up[...] = ffn[1]
    down[...] = ffn[2]
    outgate[...] = mixer[0]
    mixout[...] = mixer[1]
    w_in[...] = inner[0]
    w_step[...] = small[:rank, :size]
    at = rank + states
    log_decay[...] = small[rank:at, :size]
    conv_taps[...] = small[at : at + taps, :size]
    at += taps
    for k, row in enumerate(outs[10:15]):
        row[...] = small[at + k : at + k + 1, :size]
    outs[15][...] = small[at + 5 : at + 6, :gains]
    at = rank + states + 16
    for b in range(w_select.shape[1] // LANES):
        w_select[:, b * LANES : (b + 1) * LANES] = small[at + b * high : at + (b + 1) * high, :]


def place_all(rank, states, taps, high, gains, channels, ffn, mixer, inner, small):
    rows, units = ffn.shape[1:]
    size = channels // lax.axis_size("seq")
    width = mixer.shape[2]
    shapes = [(rows, units), (rows, units), (rows, units), (rows, width), (rows, width), (rows, width), (rank, size),
              (states, size), (taps, size), (high, channels)] + [(1, size)] * 5 + [(1, gains)]
    return pl.pallas_call(
        functools.partial(place_kernel, rank, states, taps, high, size, gains),
        out_shape=[shaped(*shape) for shape in shapes],
        in_specs=[in_vmem()] * 4,
        out_specs=[in_vmem()] * len(shapes),
        compiler_params=params(40),
        cost_estimate=spans(6),
    )(ffn, mixer, inner, small)


epsilon = 1e-06
CUT = 1e6


def links(step, wrap=False, axis="seq"):
    n = lax.axis_size(axis)
    return [(i, (i + step) % n) for i in range(n) if wrap or 0 <= i + step < n]


def swaps(bit, axis="seq"):
    return [(i, i ^ bit) for i in range(lax.axis_size(axis))]


def send(block, route, axis="seq"):
    return lax.ppermute(block, axis, route)


def head_sum(part):
    return part + send(part, swaps(1, "head"), "head")


def own_stream(block):
    return lax.dynamic_index_in_dim(block, lax.axis_index("head"), 0, keepdims=False)


def part_of(block, index, size, axis):
    return lax.dynamic_slice_in_dim(block, index * size, size, axis)


def after(block, *earlier):
    return lax.optimization_barrier((block,) + earlier)[0]


def matmul(left, right):
    return jnp.dot(left, right, preferred_element_type=jnp.float32)


def matmul_back(left, right):
    return lax.dot_general(
        left, right, (((left.ndim - 1,), (1,)), ((), ())), preferred_element_type=jnp.float32
    )


def weight_outer(left, right):
    axes = tuple(range(left.ndim - 1))
    return lax.dot_general(left, right, ((axes, axes), ((), ())), preferred_element_type=jnp.float32)


def norm_forward(v, gain):
    scale = lax.rsqrt(jnp.mean(v * v, axis=-1, keepdims=True) + epsilon)
    return (v * scale * gain, scale)


def norm_backward(v, scale, gain, upstream):
    weighted = upstream * gain
    d_input = scale * weighted - v * scale * scale * scale * jnp.mean(
        weighted * v, axis=-1, keepdims=True
    )
    d_gain = jnp.sum(upstream * v * scale, axis=(0, 1))
    return (d_input, d_gain)


def silu_slope(v):
    sig = jax.nn.sigmoid(v)
    return sig + v * sig * (1.0 - sig)


def across(small):
    streams, length, n = small.shape
    return jnp.broadcast_to(small.reshape(streams, length * n, 1), (streams, length * n, 128))


def body(
    tokens, doc_ids, out_grad, norm_mix, w_inner, w_outgate, conv_taps, conv_bias, w_select, select_gain,
    w_step, step_bias, log_decay, skip_gain, w_mixout, norm_ffn, w_gate, w_up, w_down,
):
    streams, length, width = tokens.shape
    channels = w_inner.shape[1]
    taps = conv_taps.shape[0]
    rank = w_step.shape[0]
    states = log_decay.shape[1]
    lead = taps - 1
    count = lax.axis_size("seq")
    stride = count // SIDE
    here = lax.axis_index("seq")
    z, place = here // stride, here % SIDE
    size = channels // SIDE
    low = jnp.bfloat16

    grad_in = out_grad.astype(jnp.float32)
    source = tokens.astype(jnp.float32)
    rim_ids = jnp.broadcast_to((doc_ids[:, length - lead :] + 1).astype(jnp.float32)[:, :, None], (streams, lead, 128))
    rim = send(jnp.concatenate([source[:, length - lead :], rim_ids], axis=2), links(1))
    mine_grad, source, rim = lax.optimization_barrier((own_stream(out_grad).astype(jnp.float32), source, rim))
    line_grad = [send(mine_grad, links(stride)), send(mine_grad, links(-stride))]
    normed, scale_mix = norm_forward(source, norm_mix)
    normed_low = normed.astype(low)
    mine_normed = own_stream(normed)
    norm_near, norm_next = send(mine_normed, swaps(1)), send(mine_normed, swaps(2))
    rim_normed, _ = norm_forward(rim[:, :, :width], norm_mix)
    ext_val = matmul(jnp.concatenate([rim_normed.astype(low), normed_low], axis=1), w_inner)
    outgate = matmul(normed_low, w_outgate)
    ext_ids = jnp.concatenate([rim[:, :, width].astype(jnp.int32) - 1, doc_ids], axis=1)
    masks = [
        (ext_ids[:, k : k + length] == doc_ids).astype(jnp.float32)[:, :, None] for k in range(taps)
    ]
    value_pre = conv_bias
    for k in range(taps):
        value_pre = value_pre + conv_taps[k] * ext_val[:, k : k + length] * masks[k]
    value = jax.nn.silu(value_pre)
    value_low = value.astype(low)
    select = head_sum(matmul(value_low, w_select))
    raw_step = select[..., :rank]
    raw_b = select[..., rank : rank + states]
    raw_c = select[..., rank + states :]
    step_n, step_scale = norm_forward(raw_step, select_gain[:rank])
    bsel, b_scale = norm_forward(raw_b, select_gain[rank : rank + states])
    csel, c_scale = norm_forward(raw_c, select_gain[rank + states :])
    step_low = step_n.astype(low)
    step_pre = matmul(step_low, w_step) + step_bias
    step = jax.nn.softplus(step_pre)
    keep = doc_ids == ext_ids[:, lead - 1 : lead - 1 + length]
    fall = jnp.where(keep[:, :, None], step, CUT)
    gain = step * value
    decay_rate = -jnp.exp(log_decay).T
    rate = decay_rate * LOG2E
    b_wide, c_wide = across(bsel), across(csel)
    outs, first, grad_ring, grad_rest, side_far, side_rest = scan_forward(
        fall, gain, b_wide, c_wide, rate, line_grad, norm_near, norm_next
    )
    y = outs + skip_gain * value
    gate_z = jax.nn.silu(outgate)
    mixed = y * gate_z
    mixed_low = mixed.astype(low)
    mix = head_sum(matmul(mixed_low, w_mixout))
    resid = source + mix
    hidden, scale_ffn = norm_forward(resid, norm_ffn)
    hidden_low = hidden.astype(low)
    flat = lambda block: block.reshape(-1, block.shape[-1])
    like = lambda block: block.reshape(streams, length, -1)
    d_gate, d_up, act_low, ffn, d_hidden, *line_hidden, y_side = feed_forward(
        flat(hidden_low), flat(out_grad), w_gate, w_up, w_down, hidden, y
    )
    output = (resid + head_sum(like(ffn))).astype(low)
    d_hidden = head_sum(like(d_hidden))
    d_resid_norm, grad_norm_ffn = norm_backward(resid, scale_ffn, norm_ffn, d_hidden)
    d_resid = grad_in + d_resid_norm
    d_mix = d_resid.astype(low)
    d_mixed = matmul_back(d_mix, w_mixout)
    d_y = d_mixed * gate_z
    d_outgate = (d_mixed * y * silu_slope(outgate)).astype(low)
    grad_skip_gain = jnp.sum(d_y * value, axis=(0, 1))
    (
        d_step, d_scan, d_bsel, d_csel, decay_sum, hid_ring, hid_rest, mix_side, mix_rest, grad_end, grad_rest_end,
    ) = scan_backward(
        fall, step, value, d_y, b_wide, c_wide, rate, first, line_hidden, own_stream(d_resid), grad_ring[1]
    )

    mixer, turned = mixer_grads(
        flat(normed_low), [norm_near, norm_next, side_far, side_rest], flat(d_mix), [mix_side, mix_rest],
        flat(part_of(y, place, size, 2)), y_side,
        w_outgate, w_mixout,
    )
    mixer = mixer.reshape(2, SIDE, width // SIDE, size)
    ffn, near, passed = ffn_grads(
        (flat(hidden_low), *line_hidden, hid_ring, hid_rest),
        (flat(out_grad), *line_grad, grad_ring[1], grad_rest, grad_end, grad_rest_end),
        w_gate, w_up, w_down, d_gate, d_up, act_low, mixer,
    )
    d_step = after(d_step, ffn)

    d_value = d_y * skip_gain + d_scan
    d_step_pre = (d_step * jax.nn.sigmoid(step_pre)).astype(low)
    grad_step_bias = jnp.sum(d_step_pre, axis=(0, 1), dtype=jnp.float32)
    grad_w_step = weight_outer(step_low, d_step_pre)
    d_small = head_sum(
        jnp.concatenate(
            [matmul_back(d_step_pre, w_step), d_bsel, d_csel], axis=-1
        )
    )
    d_raw_step, gain_step = norm_backward(
        raw_step, step_scale, select_gain[:rank], d_small[..., :rank]
    )
    d_raw_b, gain_b = norm_backward(
        raw_b, b_scale, select_gain[rank : rank + states], d_small[..., rank : rank + states]
    )
    d_raw_c, gain_c = norm_backward(
        raw_c, c_scale, select_gain[rank + states :], d_small[..., rank + states :]
    )
    grad_select_gain = jnp.concatenate([gain_step, gain_b, gain_c])
    d_select = jnp.concatenate([d_raw_step, d_raw_b, d_raw_c], axis=-1).astype(low)
    grad_w_select = weight_outer(d_select, value_low)
    d_value = d_value + matmul_back(d_select, w_select)
    d_value_pre = d_value * silu_slope(value_pre)
    grad_conv_bias = jnp.sum(d_value_pre, axis=(0, 1))
    tap_grads = []
    d_ext = jnp.zeros_like(ext_val)
    for k in range(taps):
        masked = d_value_pre * masks[k]
        tap_grads.append(jnp.sum(masked * ext_val[:, k : k + length], axis=(0, 1)))
        d_ext = d_ext + jnp.pad(masked * conv_taps[k], ((0, 0), (k, lead - k), (0, 0)))
    rim_grad = send(d_ext[:, :lead], links(-1))
    d_inner = (d_ext[:, lead:] + jnp.pad(rim_grad, ((0, 0), (length - lead, 0), (0, 0)))).astype(low)
    d_normed = head_sum(matmul_back(d_inner, w_inner) + matmul_back(d_outgate, w_outgate))
    d_source, grad_norm_mix = norm_backward(source, scale_mix, norm_mix, d_normed)
    tokens_grad = d_resid + d_source

    gains = grad_select_gain.reshape(count, -1)
    spread = jnp.pad(gains, ((0, 0), (0, channels // count - gains.shape[1]))).reshape(channels)
    pad = lambda v: jnp.pad(v, (0, channels - v.shape[0]))
    rows = tap_grads + [
        grad_conv_bias, grad_step_bias, grad_skip_gain, pad(grad_norm_mix), pad(grad_norm_ffn), spread
    ]
    grad_w_step = after(grad_w_step, tokens_grad)
    small = gather_small(grad_w_step, decay_sum * decay_rate, grad_w_select, rows)
    ffn, mixer, inner, tall = sum_grads(
        ffn, mixer, passed, d_inner.astype(jnp.float32), near, turned, flat(part_of(d_inner, place, size, 2)), small
    )
    if count > SIDE * SIDE:
        groups = [[a * stride + b + SIDE * k for k in range(stride // SIDE)] for a in range(SIDE) for b in range(SIDE)]
        ffn, mixer, inner = (
            lax.psum_scatter(part, "seq", scatter_dimension=1, axis_index_groups=groups) for part in (ffn, mixer, inner)
        )
    else:
        ffn, mixer, inner = (part[:, 0] for part in (ffn, mixer, inner))
    outs = place_all(
        rank, states, taps, grad_w_select.shape[0] // count, gains.shape[1], channels, ffn, mixer, inner, tall
    )
    gate, up, down, mixout, outgate, w_in, d_w_step, d_log_decay, d_taps, d_select = outs[:10]
    conv, bias, skip, mix_gain, ffn_gain, select_gains = (row[0] for row in outs[10:])
    return (
        output,
        tokens_grad,
        mix_gain,
        w_in,
        outgate,
        d_taps,
        conv,
        d_select.T,
        select_gains,
        d_w_step,
        bias,
        d_log_decay.T,
        skip,
        mixout.T,
        ffn_gain,
        gate,
        up,
        down.T,
    )


def solution(mesh):
    in_specs = (
        P(None, "seq", None),
        P(None, "seq"),
        P(None, "seq", None),
        P(),
        P(None, "head"),
        P(None, "head"),
        P(None, "head"),
        P("head"),
        P("head", None),
        P(),
        P(None, "head"),
        P("head"),
        P("head", None),
        P("head"),
        P("head", None),
        P(),
        P(None, "head"),
        P(None, "head"),
        P("head", None),
    )
    out_specs = (
        P(None, "seq", None),
        P(None, "seq", None),
        P("seq"),
        P("seq", "head"),
        P("seq", "head"),
        P(None, ("head", "seq")),
        P(("head", "seq")),
        P("head", "seq"),
        P("seq"),
        P(None, ("head", "seq")),
        P(("head", "seq")),
        P(("head", "seq"), None),
        P(("head", "seq")),
        P("head", "seq"),
        P("seq"),
        P("seq", "head"),
        P("seq", "head"),
        P("head", "seq"),
    )
    return jax.shard_map(body, mesh=mesh, in_specs=in_specs, out_specs=out_specs, check_vma=False)
```

```python
import functools
import math

import jax
import jax.numpy as jnp
from jax import lax
from jax.experimental import pallas as pl
from jax.experimental.pallas import tpu as pltpu
from jax.sharding import PartitionSpec as P

LOG2E = math.log2(math.e)
LN2 = math.log(2.0)
ROWS = 8


def params(limit=48):
    return pltpu.CompilerParams(vmem_limit_bytes=limit * 1024 * 1024)


def wide(tile, lanes):
    return jnp.concatenate([tile] * (lanes // tile.shape[1]), axis=1)


def pieces(lanes):
    return next(w for w in (256, 128) if lanes % w == 0)


def spans(us):
    return pl.CostEstimate(flops=int(us * 1.1e8), bytes_accessed=int(us * 3.0e5), transcendentals=0)


def fetch_tokens(blocks, stage, arrived):
    copies = [pltpu.make_async_copy(block, stage.at[k], arrived.at[k]) for k, block in enumerate(blocks)]
    for c in copies:
        c.start()

    def put(target, own):
        rows, size = own.shape[0], stage.shape[1]
        target[:rows, :] = own[...].astype(target.dtype)
        for k, c in enumerate(copies):
            c.wait()
            target[rows + k * size : rows + (k + 1) * size, :] = stage[k].astype(target.dtype)

    return put


def parts_of(refs):
    return [part for ref in refs for part in ([ref.at[k] for k in range(ref.shape[0])] if len(ref.shape) == 3 else [ref])]


def dot(left, right):
    return jnp.dot(left, right, preferred_element_type=jnp.float32)


def dot_back(left, right):
    return lax.dot_general(left, right, (((1,), (1,)), ((), ())), preferred_element_type=jnp.float32)


def whole(shape):
    return pl.BlockSpec(shape, lambda i: (0,) * len(shape), pipeline_mode=pl.Buffered(1))


def mixer_kernel(more_norm, more_mix, *refs):
    at = iter(range(len(refs)))
    take = lambda count: [refs[next(at)] for _ in range(count)]
    (norm_own,), norm_more = take(1), take(more_norm)
    (mix_own,), mix_more = take(1), take(more_mix)
    y_own, y_side = take(2)
    w_out, w_mix = take(2)
    out, norm_turned = take(2)
    norm, mix, mixed, d_out, wo, wm, local, norm_stage, mix_stage, norm_got, mix_got = take(11)
    own = norm_own.shape[0]
    half = own // 2

    @pl.when(pl.program_id(0) == 0)
    def _():
        size = wo.shape[1]
        at = pl.ds(pl.multiple_of(lax.rem(lax.axis_index("seq"), SIDE) * size, 128), size)
        loads = [
            pltpu.make_async_copy(w_out.at[:, at], wo, local.at[0]),
            pltpu.make_async_copy(w_mix.at[at], wm, local.at[1]),
        ]
        for c in loads:
            c.start()
        put_norm = fetch_tokens(parts_of(norm_more), norm_stage, norm_got)
        put_mix = fetch_tokens(parts_of(mix_more), mix_stage, mix_got)
        put_norm(norm, norm_own)
        put_mix(mix, mix_own)
        for c in loads:
            c.wait()

        def finish(rows, y):
            outgate = dot(norm[rows, :], wo[...])
            d_mixed = dot_back(mix[rows, :], wm[...])
            sig = 1.0 / (1.0 + jnp.exp(-outgate))
            silu = outgate * sig
            mixed[rows, :] = (y * silu).astype(mixed.dtype)
            d_out[rows, :] = (d_mixed * y * (sig + silu * (1.0 - sig))).astype(d_out.dtype)

        finish(slice(0, own), y_own[...])
        sides = y_side.shape[0]
        head = lax.axis_index("head")
        for k in range(sides):
            for s in range(2):
                start = own + (s * sides + k) * half
                finish(slice(start, start + half), y_side[k, head if s == 0 else 1 - head])

    rows = norm_turned.shape[0]
    span = pl.ds(pl.multiple_of(pl.program_id(0) * rows, rows), rows)
    turned = norm[:, span].T
    norm_turned[...] = turned
    out[0] = dot(turned, d_out[...])
    out[1] = dot(mix[:, span].T, mixed[...])


def mixer_grads(norm_own, norm_more, mix_own, mix_more, y_own, y_side, w_out, w_mix):
    own, width = norm_own.shape
    cut = w_out.shape[1] // SIDE
    block = next(b for b in (256, 128) if width % b == 0)
    tokens = own + sum(math.prod(part.shape[:-1]) for part in norm_more)
    low = jnp.bfloat16
    row = lambda columns: pl.BlockSpec((block, columns), lambda i: (i, 0))
    operands = (norm_own, *norm_more, mix_own, *mix_more, y_own, y_side, w_out, w_mix)
    return pl.pallas_call(
        functools.partial(mixer_kernel, len(norm_more), len(mix_more)),
        grid=(width // block,),
        in_specs=[whole(norm_own.shape)] + [in_hbm()] * len(norm_more) + [whole(mix_own.shape)] + [in_hbm()] * len(mix_more)
        + [whole(y_own.shape), whole(y_side.shape)] + [in_hbm()] * 2,
        out_specs=[pl.BlockSpec((2, block, cut), lambda i: (0, i, 0)), row(tokens)],
        out_shape=[
            jax.ShapeDtypeStruct((2, width, cut), jnp.float32),
            jax.ShapeDtypeStruct((width, tokens), low),
        ],
        scratch_shapes=[pltpu.VMEM((tokens, width), low)] * 2
        + [pltpu.VMEM((tokens, cut), low)] * 2
        + [pltpu.VMEM((width, cut), low), pltpu.VMEM((cut, width), low), pltpu.SemaphoreType.DMA((2,))]
        + [pltpu.VMEM((2 * SIDE - 2, own // 2, width), jnp.float32)] * 2
        + [pltpu.SemaphoreType.DMA((2 * SIDE - 2,))] * 2,
        compiler_params=params(40),
        cost_estimate=spans(12),
    )(*operands)


SIDE = 4
MESH = pl.DeviceIdType.MESH


def remote(source, target, sends, recvs, at, device):
    return pltpu.make_async_remote_copy(
        src_ref=source, dst_ref=target, send_sem=sends.at[at], recv_sem=recvs.at[at],
        device_id=device, device_id_type=MESH,
    )


class Place:
    def __init__(self, count):
        here = lax.axis_index("seq")
        self.head = lax.axis_index("head")
        self.stride = count // SIDE
        self.groups = count // SIDE
        self.place, self.group = lax.rem(here, SIDE), here // SIDE
        self.z = here // self.stride
        base = here - self.place
        self.member = [(base + (self.place ^ k), self.head) for k in range(SIDE)]
        self.other = [
            (lax.rem(self.group + k, self.groups) * SIDE + self.place, self.head) for k in range(self.groups)
        ]
        self.core = (here, 1 - self.head)
        self.above = (lax.rem(here + self.stride, count), self.head)
        self.below = (lax.rem(here - self.stride + count, count), self.head)

    def greet(self):
        barrier = pltpu.get_barrier_semaphore()
        devices = self.member[1:] + self.other[1:] + [self.core]
        for device in devices:
            pl.semaphore_signal(barrier, inc=1, device_id=device, device_id_type=MESH)
        pl.semaphore_wait(barrier, len(devices))


class Line:
    def __init__(self, where, up_one, down_one, ring, rest, sends, recvs):
        self.where, self.up_one, self.down_one = where, up_one, down_one
        self.ring, self.rest, self.sends, self.recvs = ring, rest, sends, recvs

    def copies(self, step):
        w = self.where
        up = self.up_one if step == 2 else self.ring.at[SIDE - step]
        down = self.down_one if step == 2 else self.ring.at[step - 2]
        return (
            remote(up, self.ring.at[SIDE - 1 - step], self.sends, self.recvs, step - 1, w.above),
            remote(down, self.ring.at[step - 1], self.sends, self.recvs, SIDE - 2 + step, w.below),
        )

    def core(self, slot):
        return remote(self.ring.at[slot], self.rest.at[slot], self.sends, self.recvs, 2 * SIDE - 2 + slot, self.where.core)

    def start(self, step):
        up, down = self.copies(step)
        z = self.where.z
        pl.when((z >= step - 1) & (z < SIDE - 1))(up.start)
        pl.when((z <= SIDE - step) & (z > 0))(down.start)

    def arrive(self, step):
        up, down = self.copies(step)
        z = self.where.z

        @pl.when(z >= step)
        def _():
            up.wait_recv()
            self.core(SIDE - 1 - step).start()

        @pl.when(z <= SIDE - 1 - step)
        def _():
            down.wait_recv()
            self.core(step - 1).start()

    def cores_of_one(self):
        return (
            remote(self.up_one, self.rest.at[SIDE - 2], self.sends, self.recvs, 2 * SIDE - 2 + SIDE - 2, self.where.core),
            remote(self.down_one, self.rest.at[0], self.sends, self.recvs, 2 * SIDE - 2, self.where.core),
        )

    def start_cores_of_one(self):
        up, down = self.cores_of_one()
        pl.when(self.where.z >= 1)(up.start)
        pl.when(self.where.z <= SIDE - 2)(down.start)

    def finish_two(self):
        z = self.where.z
        up, down = self.copies(2)
        pl.when((z >= 1) & (z < SIDE - 1))(up.wait_send)
        pl.when((z <= SIDE - 2) & (z > 0))(down.wait_send)
        self.core(1).wait()
        pl.when(z >= 1)(self.core(SIDE - 2).wait)
        pl.when(z <= SIDE - 2)(self.core(0).wait)

    def finish_three(self):
        z = self.where.z
        up, down = self.copies(3)
        pl.when(z == SIDE - 2)(up.wait_send)
        pl.when(z == 1)(down.wait_send)
        for slot in range(SIDE - 1):
            self.core(slot).wait()


LINE_SEMS = 3 * (SIDE - 1)


class Side:
    def __init__(self, where, mine, side, rest, sends, recvs):
        self.where, self.mine, self.side, self.rest, self.sends, self.recvs = where, mine, side, rest, sends, recvs

    def near(self):
        return [
            remote(self.mine, self.side.at[k - 1], self.sends, self.recvs, k - 1, self.where.member[k]) for k in (1, 2)
        ]

    def far(self):
        half = self.side.shape[1] // 2
        top, low = pl.ds(0, half), pl.ds(half, half)
        return [
            remote(self.side.at[1, top], self.side.at[2, top], self.sends, self.recvs, 2, self.where.member[1]),
            remote(self.side.at[0, low], self.side.at[2, low], self.sends, self.recvs, 3, self.where.member[2]),
        ]

    def core(self, slot):
        return remote(self.side.at[slot], self.rest.at[slot], self.sends, self.recvs, 4 + slot, self.where.core)

    def start(self):
        for c in self.near():
            c.start()

    def turn(self):
        for c in self.near():
            c.wait_recv()
        for c in self.far():
            c.start()
        for slot in (0, 1):
            self.core(slot).start()

    def finish(self):
        for c in self.far():
            c.wait_recv()
        self.core(2).start()
        for c in self.near() + self.far():
            c.wait_send()
        for slot in range(3):
            self.core(slot).wait()


SIDE_SEMS = 7


def chain(where, reverse, summary, fall, rate_ref, out_ref, scratch, after_line, after_all):
    own, side, mine, line, back, done, sends, recvs = scratch
    streams, n, channels = out_ref.shape
    width = channels // SIDE
    rows = streams * n
    place, group, groups = where.place, where.group, where.groups
    sides = [remote(own.at[k], side.at[k], sends, recvs, k, where.member[k]) for k in range(1, SIDE)]

    def quarter(k, target):
        cols = pl.ds(pl.multiple_of((place ^ k) * width, 128), width)
        states = summary(cols)
        for s in range(streams):
            target[k, s * n : (s + 1) * n, :] = states[s]
            target[k, rows + s : rows + s + 1, :] = jnp.sum(fall[s, :, cols], axis=0, keepdims=True)
        target[k, rows + streams :, :] = jnp.zeros((target.shape[1] - rows - streams, width), jnp.float32)

    for k in range(1, SIDE):
        quarter(k, own)
        sides[k - 1].start()
    quarter(0, side)
    rate = rate_ref[:, pl.ds(pl.multiple_of(place * width, 128), width)]

    def through(steps):
        return jnp.concatenate([jnp.exp2(steps[s : s + 1] * rate) for s in range(streams)], axis=0)

    for c in sides:
        c.wait_recv()
    state, steps = jnp.zeros((rows, width), jnp.float32), jnp.zeros((streams, width), jnp.float32)
    before, passed = [None] * SIDE, [None] * SIDE
    for j in reversed(range(SIDE)) if reverse else range(SIDE):
        block = side[place ^ j]
        before[j], passed[j] = state, steps
        step = block[rows : rows + streams]
        state = through(step) * state + block[:rows]
        steps = steps + step
    mine[:rows, :] = state
    mine[rows : rows + streams, :] = steps
    mine[rows + streams :, :] = jnp.zeros((mine.shape[0] - rows - streams, width), jnp.float32)
    lines = [remote(mine, line.at[k], sends, recvs, SIDE + k, where.other[k]) for k in range(1, groups)]
    for c in lines:
        c.start()
    for c in lines:
        c.wait_recv()
    after_line()
    entering = jnp.zeros((rows, width), jnp.float32)
    for k in range(1, groups) if reverse else range(groups - 1, 0, -1):
        counts = (k > group) if reverse else (k <= group)
        block = line[k]
        new = through(block[rows : rows + streams]) * entering + block[:rows]
        entering = jnp.where(counts, new, entering)
    for j in range(SIDE):
        back[j] = through(passed[j]) * entering + before[j]
    backs = [
        remote(back.at[place ^ k], done.at[k], sends, recvs, SIDE + groups + k, where.member[k]) for k in range(1, SIDE)
    ]
    for c in backs:
        c.start()
    after_all()
    done[0] = back[place]
    for c in backs:
        c.wait_recv()
    for q in range(SIDE):
        out_ref[:, :, q * width : (q + 1) * width] = done[place ^ q].reshape(streams, n, width)
    for c in sides + lines + backs:
        c.wait_send()


def chain_scratch(streams, n, channels, groups):
    width = channels // SIDE
    rows = streams * n
    tall = rows + 8 * (-(-streams // 8))
    sems = pltpu.SemaphoreType.DMA((2 * SIDE + groups,))
    return [
        pltpu.VMEM((SIDE, tall, width), jnp.float32),
        pltpu.VMEM((SIDE, tall, width), jnp.float32),
        pltpu.VMEM((tall, width), jnp.float32),
        pltpu.VMEM((groups, tall, width), jnp.float32),
        pltpu.VMEM((SIDE, rows, width), jnp.float32),
        pltpu.VMEM((SIDE, rows, width), jnp.float32),
        sems,
        sems,
    ]


def blocks_of(channels):
    lanes = pieces(channels)
    return lanes, channels // lanes


def columns(i, lanes):
    return pl.ds(pl.multiple_of(i * lanes, lanes), lanes)


def forward_kernel(
    count, fall, gain, b_ref, c_ref, rate_ref, up_one, down_one, norm_near, norm_next,
    y_ref, first, ring, ring_rest, side_far, side_rest,
    line_send, line_recv, side_send, side_recv, *scratch,
):
    where = Place(count)
    streams, length, channels = fall.shape
    n = rate_ref.shape[0]
    lanes, blocks = blocks_of(channels)
    z = where.z
    where.greet()
    line = Line(where, up_one, down_one, ring, ring_rest, line_send, line_recv)

    def summary(cols):
        rate = rate_ref[:, cols]
        span = rate.shape[1]

        def chunk(i, states):
            base = pl.multiple_of(i * ROWS, ROWS)
            out = []
            for s in range(streams):
                state = states[s]
                d = fall[s, pl.ds(base, ROWS), cols]
                x = gain[s, pl.ds(base, ROWS), cols]
                for j in range(ROWS):
                    b = b_ref[s, pl.ds(pl.multiple_of((base + j) * n, n), n), :]
                    fade = jnp.exp2(d[j : j + 1] * rate)
                    state = fade * state + x[j : j + 1] * wide(b, span)
                out.append(state)
            return tuple(out)

        start = tuple(jnp.zeros((n, span), jnp.float32) for _ in range(streams))
        return lax.fori_loop(0, length // ROWS, chunk, start)

    half = norm_near.shape[0] // 2
    top, low = pl.ds(0, half), pl.ds(half, half)
    far = [
        remote(norm_next.at[top], side_far.at[top], side_send, side_recv, 0, where.member[1]),
        remote(norm_near.at[low], side_far.at[low], side_send, side_recv, 1, where.member[2]),
    ]
    cores = [
        remote(part, side_rest.at[k], side_send, side_recv, 2 + k, where.core)
        for k, part in enumerate((norm_near, norm_next, side_far))
    ]

    def after_line():
        line.start_cores_of_one()
        line.start(2)

    def after_all():
        for c in far + cores[:2]:
            c.start()

    chain(where, False, summary, fall, rate_ref, first, scratch, after_line, after_all)

    def run(i, _):
        cols = columns(i, lanes)
        rate = rate_ref[:, cols]

        def chunk(i, states):
            base = pl.multiple_of(i * ROWS, ROWS)
            out = []
            for s in range(streams):
                state = states[s]
                d = fall[s, pl.ds(base, ROWS), cols]
                x = gain[s, pl.ds(base, ROWS), cols]
                rows = []
                for j in range(ROWS):
                    at = pl.ds(pl.multiple_of((base + j) * n, n), n)
                    fade = jnp.exp2(d[j : j + 1] * rate)
                    state = fade * state + x[j : j + 1] * wide(b_ref[s, at, :], lanes)
                    rows.append(jnp.sum(state * wide(c_ref[s, at, :], lanes), axis=0, keepdims=True))
                y_ref[s, pl.ds(base, ROWS), cols] = jnp.concatenate(rows, axis=0)
                out.append(state)
            return tuple(out)

        lax.fori_loop(0, length // ROWS, chunk, tuple(first[s, :, cols] for s in range(streams)))
        return 0

    lax.fori_loop(0, blocks, run, 0)
    for c in far:
        c.wait_recv()
    cores[2].start()
    line.arrive(2)
    for c in far:
        c.wait_send()
    for c in cores:
        c.wait()
    line.finish_two()


def backward_kernel(
    count, fall, d_ref, v_ref, g_ref, b_ref, c_ref, rate_ref, first_ref, up_one, down_one, mix, grad_middle,
    dstep_ref, dvalue_ref, db_ref, dc_ref, decay_ref, ring, ring_rest, side, side_rest, grad_end, grad_rest,
    db_wide, dc_wide, last, path, fades, line_send, line_recv, side_send, side_recv, *scratch,
):
    where = Place(count)
    streams, length, channels = fall.shape
    n = rate_ref.shape[0]
    lanes, blocks = blocks_of(channels)
    chunks = length // ROWS
    width = channels // SIDE
    where.greet()
    line = Line(where, up_one, down_one, ring, ring_rest, line_send, line_recv)
    z = where.z
    rise = remote(grad_middle, grad_end, line_send, line_recv, LINE_SEMS, where.above)
    sink = remote(grad_middle, grad_end, line_send, line_recv, LINE_SEMS + 1, where.below)
    core = remote(grad_end, grad_rest, line_send, line_recv, LINE_SEMS + 2, where.core)
    square = Side(where, mix, side, side_rest, side_send, side_recv)
    half = ring.shape[1] // 2
    steps = []
    for part in range(2):
        at = pl.ds(part * half, half)
        steps.append(
            (
                remote(up_one.at[at], ring.at[1, at], line_send, line_recv, LINE_SEMS + 3 + 2 * part, where.above),
                remote(down_one.at[at], ring.at[1, at], line_send, line_recv, LINE_SEMS + 4 + 2 * part, where.below),
            )
        )

    def start_half(part):
        up, down = steps[part]
        pl.when((z >= 1) & (z < SIDE - 1))(up.start)
        pl.when((z <= SIDE - 2) & (z > 0))(down.start)

    start_half(0)
    line.start_cores_of_one()

    def summary(cols):
        rate = rate_ref[:, cols]
        span = rate.shape[1]

        def chunk(i, carry):
            base = pl.multiple_of((chunks - 1 - i) * ROWS, ROWS)
            out = []
            for s in range(streams):
                carried = carry[s]
                d = fall[s, pl.ds(base, ROWS), cols]
                g = g_ref[s, pl.ds(base, ROWS), cols]
                for j in reversed(range(ROWS)):
                    at = pl.ds(pl.multiple_of((base + j) * n, n), n)
                    fade = jnp.exp2(d[j : j + 1] * rate)
                    carried = fade * (g[j : j + 1] * wide(c_ref[s, at, :], span) + carried)
                out.append(carried)
            return tuple(out)

        start = tuple(jnp.zeros((n, span), jnp.float32) for _ in range(streams))
        return lax.fori_loop(0, chunks, chunk, start)

    def after_line():
        start_half(1)
        pl.when(z == SIDE - 2)(rise.start)
        pl.when(z == 1)(sink.start)

    def after_all():
        square.start()

    chain(where, True, summary, fall, rate_ref, last, scratch, after_line, after_all)
    db_wide[...] = jnp.zeros_like(db_wide)
    dc_wide[...] = jnp.zeros_like(dc_wide)

    def fold(tile):
        out = tile[:, :128]
        for k in range(1, lanes // 128):
            out = out + tile[:, k * 128 : (k + 1) * 128]
        return out

    def run(i, _):
        cols = columns(i, lanes)
        rate = rate_ref[:, cols]

        @pl.when(i == blocks // 3)
        def _():
            for up, down in steps:
                pl.when(z >= 2)(up.wait_recv)
                pl.when(z <= SIDE - 3)(down.wait_recv)
            line.core(1).start()
            line.start(3)

        @pl.when(i == blocks // 2)
        def _():
            square.turn()

        def ahead(i, states):
            base = pl.multiple_of(i * ROWS, ROWS)
            out = []
            for s in range(streams):
                state = states[s]
                d = fall[s, pl.ds(base, ROWS), cols]
                x = d_ref[s, pl.ds(base, ROWS), cols] * v_ref[s, pl.ds(base, ROWS), cols]
                for j in range(ROWS):
                    at = pl.ds(pl.multiple_of((base + j) * n, n), n)
                    path[s, at, :] = state
                    fade = jnp.exp2(d[j : j + 1] * rate)
                    fades[s, at, :] = fade
                    state = fade * state + x[j : j + 1] * wide(b_ref[s, at, :], lanes)
                out.append(state)
            return tuple(out)

        tails = lax.fori_loop(0, chunks, ahead, tuple(first_ref[s, :, cols] for s in range(streams)))

        def back(i, carry):
            base = pl.multiple_of((chunks - 1 - i) * ROWS, ROWS)
            out = []
            decay = carry[-1]
            for s in range(streams):
                state, carried = carry[s]
                d = d_ref[s, pl.ds(base, ROWS), cols]
                v = v_ref[s, pl.ds(base, ROWS), cols]
                g = g_ref[s, pl.ds(base, ROWS), cols]
                x = d * v
                weights, touches = [None] * ROWS, [None] * ROWS
                for j in reversed(range(ROWS)):
                    at = pl.ds(pl.multiple_of((base + j) * n, n), n)
                    gj = g[j : j + 1]
                    adjoint = gj * wide(c_ref[s, at, :], lanes) + carried
                    dc_wide[s, at, :] += fold(state * gj)
                    db_wide[s, at, :] += fold(adjoint * x[j : j + 1])
                    weights[j] = jnp.sum(adjoint * wide(b_ref[s, at, :], lanes), axis=0, keepdims=True)
                    carried = adjoint * fades[s, at, :]
                    state = path[s, at, :]
                    touch = carried * state
                    touches[j] = jnp.sum(touch * rate, axis=0, keepdims=True)
                    decay = decay + touch * d[j : j + 1]
                weighted = jnp.concatenate(weights, axis=0)
                at = pl.ds(base, ROWS)
                dstep_ref[s, at, cols] = weighted * v + jnp.concatenate(touches, axis=0) * LN2
                dvalue_ref[s, at, cols] = weighted * d
                out.append((state, carried))
            return tuple(out) + (decay,)

        start = tuple((tails[s], last[s, :, cols]) for s in range(streams))
        done = lax.fori_loop(0, chunks, back, start + (jnp.zeros((n, lanes), jnp.float32),))
        decay_ref[:, cols] = done[-1]
        return 0

    lax.fori_loop(0, blocks, run, 0)
    for s in range(streams):
        db_ref[s] = jnp.sum(db_wide[s].reshape(length, n, 128), axis=-1)
        dc_ref[s] = jnp.sum(dc_wide[s].reshape(length, n, 128), axis=-1)
    square.finish()
    line.arrive(3)
    pl.when(z == SIDE - 1)(rise.wait_recv)
    pl.when(z == 0)(sink.wait_recv)
    pl.when((z == 0) | (z == SIDE - 1))(core.start)
    line.finish_three()
    for up, down in steps:
        pl.when((z >= 1) & (z < SIDE - 1))(up.wait_send)
        pl.when((z <= SIDE - 2) & (z > 0))(down.wait_send)
    pl.when(z == SIDE - 2)(rise.wait_send)
    pl.when(z == 1)(sink.wait_send)
    pl.when((z == 0) | (z == SIDE - 1))(core.wait)


def in_vmem():
    return pl.BlockSpec(memory_space=pltpu.VMEM)


def in_hbm():
    return pl.BlockSpec(memory_space=pl.ANY)


def shaped(*shape):
    return jax.ShapeDtypeStruct(shape, jnp.float32)


def sems(count):
    return [pltpu.SemaphoreType.DMA((count,))] * 2


def scan_forward(fall, gain, b_wide, c_wide, rate, line, norm_near, norm_next):
    streams, length, channels = fall.shape
    n = rate.shape[0]
    count = lax.axis_size("seq")
    half, width = norm_near.shape
    three = shaped(SIDE - 1, half, width)
    return pl.pallas_call(
        functools.partial(forward_kernel, count),
        out_shape=[shaped(streams, length, channels), shaped(streams, n, channels), three, three, shaped(half, width), three],
        in_specs=[in_vmem()] * 5 + [in_hbm()] * 4,
        out_specs=[in_vmem()] * 2 + [in_hbm()] * 4,
        scratch_shapes=sems(LINE_SEMS) + sems(5)
        + chain_scratch(streams, n, channels, count // SIDE),
        compiler_params=pltpu.CompilerParams(
            collective_id=0, has_side_effects=True, vmem_limit_bytes=56 * 1024 * 1024
        ),
        cost_estimate=spans(40),
    )(fall, gain, b_wide, c_wide, rate, *line, norm_near, norm_next)


def scan_backward(fall, step, value, d_y, b_wide, c_wide, rate, first, line, mix, grad_middle):
    streams, length, channels = fall.shape
    n = rate.shape[0]
    count = lax.axis_size("seq")
    half, width = mix.shape
    lanes, _ = blocks_of(channels)
    three = shaped(SIDE - 1, half, width)
    tall = shaped(streams, length, n)
    flat = shaped(streams, length, channels)
    kept = pltpu.VMEM((streams, length * n, lanes), jnp.float32)
    return pl.pallas_call(
        functools.partial(backward_kernel, count),
        out_shape=[flat, flat, tall, tall, shaped(n, channels), three, three, three, three, shaped(half, width), shaped(half, width)],
        in_specs=[in_vmem()] * 8 + [in_hbm()] * 4,
        out_specs=[in_vmem()] * 5 + [in_hbm()] * 6,
        scratch_shapes=[
            pltpu.VMEM((streams, length * n, 128), jnp.float32),
            pltpu.VMEM((streams, length * n, 128), jnp.float32),
            pltpu.VMEM((streams, n, channels), jnp.float32),
            kept,
            kept,
        ]
        + sems(LINE_SEMS + 7) + sems(SIDE_SEMS)
        + chain_scratch(streams, n, channels, count // SIDE),
        compiler_params=pltpu.CompilerParams(
            collective_id=1, has_side_effects=True, vmem_limit_bytes=56 * 1024 * 1024
        ),
        cost_estimate=spans(62),
    )(fall, step, value, d_y, b_wide, c_wide, rate, first, *line, mix, grad_middle)


CHUNKS = 8
EARLY = 6


def fetch_line(z, up, down, middle, first, last, rest, rest_first, rest_last, stage, arrived):
    def copy(block, k):
        return pltpu.make_async_copy(block, stage.at[k], arrived.at[k])

    copy(middle, 1).start()
    copy(rest.at[1], 4).start()

    @pl.when(z >= 1)
    def _():
        copy(up, 2).start()
        copy(rest.at[2], 5).start()

    @pl.when(z < 1)
    def _():
        copy(last, 2).start()
        copy(rest_last, 5).start()

    @pl.when(z <= SIDE - 2)
    def _():
        copy(down, 0).start()
        copy(rest.at[0], 3).start()

    @pl.when(z > SIDE - 2)
    def _():
        copy(first, 0).start()
        copy(rest_first, 3).start()

    def put(target, own):
        rows, size = own.shape[0], stage.shape[1]
        target[:rows, :] = own[...].astype(target.dtype)
        for k in range(2 * SIDE - 2):
            copy(middle, k).wait()
            target[rows + k * size : rows + (k + 1) * size, :] = stage[k].astype(target.dtype)

    return put


def ffn_kernel(
    count, hid_own, hid_up, hid_down, hid_ring, hid_rest, grad_own, grad_up, grad_down, grad_middle, grad_rest, grad_end, grad_rest_end, wg, wu, wd, dg_own, du_own, act_own,
    mixer, out, near, passed,
    hid, grad, hid_cut, grad_cut, dg, du, act, stash, got, sent, sends, recvs, local, hid_stage, grad_stage, hid_got, grad_got,
):
    own, cut = hid_own.shape[0], hid_cut.shape[0]
    where = Place(count)
    z, place = where.z, where.place
    first = pl.program_id(0) == 0
    last = pl.program_id(0) == pl.num_programs(0) - 1
    odd, far = lax.rem(place, 2), place // 2
    early = [
        remote(
            stash.at[c, :, :, :, 1 - odd] if c % 2 == 0 else stash.at[c, :, :, 1 - far],
            near.at[c], sends, recvs, c, where.member[1 + c % 2],
        )
        for c in range(EARLY)
    ]
    tips, rising = (z == 0) | (z == SIDE - 1), z < SIDE // 2

    def along(source, target, at, up):
        return remote(source, target, sends, recvs, at, (jnp.where(up, where.above[0], where.below[0]), where.head))

    one = along(mixer.at[:, SIDE - 1 - z], got, EARLY, z == 0)
    fetch = pltpu.make_async_copy(mixer.at[:, lax.rem(z + 2, SIDE)], sent, local.at[0])
    way = jnp.where(rising, 0, 1)
    two = along(sent, passed.at[way], EARLY + 1 + way, rising)
    from_below = along(sent, passed.at[0], EARLY + 1, True)
    from_above = along(sent, passed.at[1], EARLY + 2, False)

    @pl.when(first)
    def _():
        ring, rest = hid_ring, hid_rest
        put_hid = fetch_line(
            z, hid_up, hid_down, ring.at[1], ring.at[0], ring.at[2], rest, rest.at[0], rest.at[2], hid_stage, hid_got
        )
        ends = (grad_middle, grad_end, grad_end, grad_rest, grad_rest_end, grad_rest_end)
        put_grad = fetch_line(z, grad_up, grad_down, *ends, grad_stage, grad_got)
        where.greet()
        fetch.start()
        pl.when(tips)(one.start)
        fetch.wait()
        pl.when(tips)(two.start)
        put_hid(hid, hid_own)
        put_grad(grad, grad_own)
        at = pl.ds(pl.multiple_of(z * cut, 128), cut)
        hid_cut[...] = hid[:, at].T
        grad_cut[...] = grad[:, at].T

    dg[:own, :] = dg_own[...]
    du[:own, :] = du_own[...]
    act[:own, :] = act_own[...]

    def turn(i, _):
        rows = pl.ds(pl.multiple_of(i * own, own), own)
        gate = dot(hid[rows, :], wg[...])
        up = dot(hid[rows, :], wu[...])
        d_act = dot_back(grad[rows, :], wd[...])
        sig = 1.0 / (1.0 + jnp.exp(-gate))
        silu = gate * sig
        dg[rows, :] = (d_act * up * (sig + silu * (1.0 - sig))).astype(dg.dtype)
        du[rows, :] = (d_act * silu).astype(du.dtype)
        act[rows, :] = (silu * up).astype(act.dtype)
        return 0

    lax.fori_loop(1, hid.shape[0] // own, turn, 0)
    out[0] = dot(hid_cut[...], dg[...])
    out[1] = dot(hid_cut[...], du[...])
    out[2] = dot(grad_cut[...], act[...])

    for c in range(EARLY):

        @pl.when(pl.program_id(0) == c)
        def _():
            for m in range(3):
                stash[c, m] = out[m].reshape(stash.shape[2:])
            early[c].start()

    @pl.when((pl.program_id(0) == pl.num_programs(0) // 2 + 1) & jnp.logical_not(tips))
    def _():
        one.wait_recv()
        sent[...] += got[...]
        two.start()

    @pl.when(last)
    def _():
        for c in early:
            c.wait()
        pl.when(tips)(one.wait_send)
        two.wait_send()

        @pl.when(jnp.logical_not(tips))
        def _():
            from_below.wait_recv()
            from_above.wait_recv()


def ffn_grads(hidden, out_grad, w_gate, w_up, w_down, d_gate, d_up, act, mixer):
    hid_own = hidden[0]
    own, width = hid_own.shape
    units = w_gate.shape[1]
    count = lax.axis_size("seq")
    cut = width // SIDE
    block = units // CHUNKS
    more = count // SIDE // SIDE
    rows = cut // (more * SIDE)
    tokens = own * SIDE
    low = jnp.bfloat16
    column = lambda rows: pl.BlockSpec((rows, block), lambda i: (0, i))
    tokens_in = (*hidden, *out_grad)
    return pl.pallas_call(
        functools.partial(ffn_kernel, count),
        grid=(units // block,),
        in_specs=[whole(a.shape) if a is hid_own or a is out_grad[0] else in_hbm() for a in tokens_in]
        + [column(width), column(width), pl.BlockSpec((block, width), lambda i: (i, 0))]
        + [column(own)] * 3
        + [in_hbm()],
        out_specs=[pl.BlockSpec((3, cut, block), lambda i: (0, 0, i))] + [in_hbm()] * 2,
        out_shape=[shaped(3, cut, units), shaped(EARLY, 3, more, 2, rows, block), shaped(2, 2, *mixer.shape[2:])],
        scratch_shapes=[pltpu.VMEM((tokens, width), low)] * 2
        + [pltpu.VMEM((cut, tokens), low)] * 2
        + [pltpu.VMEM((tokens, block), low)] * 3
        + [pltpu.VMEM((EARLY, 3, more, 2, 2, rows, block), jnp.float32)]
        + [pltpu.VMEM((2, *mixer.shape[2:]), jnp.float32)] * 2
        + sems(EARLY + 3) + [pltpu.SemaphoreType.DMA((1,))]
        + [pltpu.VMEM((2 * SIDE - 2, own // 2, width), jnp.float32)] * 2
        + [pltpu.SemaphoreType.DMA((2 * SIDE - 2,))] * 2,
        compiler_params=pltpu.CompilerParams(
            collective_id=2, has_side_effects=True, vmem_limit_bytes=56 * 1024 * 1024
        ),
        cost_estimate=spans(36),
    )(*tokens_in, w_gate, w_up, w_down, d_gate, d_up, act, mixer)


class Reduce:
    def __init__(self, where, blocks, got, passed, arrived, sends, recvs):
        self.where, self.blocks, self.got, self.passed, self.arrived = where, blocks, got, passed, arrived
        self.sends, self.recvs = sends, recvs

    def out(self, source, target, at, rising):
        w = self.where
        return remote(source, target, self.sends, self.recvs, at, (jnp.where(rising, w.above[0], w.below[0]), w.head))

    def one(self):
        return self.out(self.blocks.at[:, SIDE - 1 - self.where.z], self.got, 0, self.where.z == 0)

    def start_one(self):
        pl.when((self.where.z == 0) | (self.where.z == SIDE - 1))(self.one().start)

    def middle(self):
        return (self.where.z > 0) & (self.where.z < SIDE - 1)

    def two(self, source):
        rising = self.where.z < SIDE // 2
        return self.out(source, self.passed.at[jnp.where(rising, 0, 1)], jnp.where(rising, 1, 2), rising)

    def start_two(self):
        z = self.where.z

        @pl.when(self.middle())
        def _():
            self.one().wait_recv()
            self.got[...] += self.blocks[:, lax.rem(z + 2, SIDE)]
            self.two(self.got).start()

        @pl.when(jnp.logical_not(self.middle()))
        def _():
            self.two(self.blocks.at[:, lax.rem(z + 2, SIDE)]).start()

    def three(self, source, way):
        return self.out(source, self.arrived.at[way], 3 + way, way == 0)

    def start_three(self, wait):
        z = self.where.z

        @pl.when(self.middle())
        def _():
            for way in (0, 1):
                if wait:
                    self.two_from(way).wait_recv()
                self.passed[way] += self.blocks[:, z + 1 - 2 * way]
                self.three(self.passed.at[way], way).start()

        pl.when(z == 0)(self.three(self.blocks.at[:, 1], 0).start)
        pl.when(z == SIDE - 1)(self.three(self.blocks.at[:, SIDE - 2], 1).start)

    def two_from(self, way):
        return self.out(self.passed.at[way], self.passed.at[way], 1 + way, way == 0)

    def result(self, done):
        z = self.where.z
        done[...] = self.blocks[:, z].reshape(done.shape)
        for way in (0, 1):

            @pl.when((z >= 1) if way == 0 else (z <= SIDE - 2))
            def _():
                self.three(self.passed.at[way], way).wait_recv()
                done[...] += self.arrived[way].reshape(done.shape)

    def finish(self, first):
        z = self.where.z
        if first <= 1:
            pl.when((z == 0) | (z == SIDE - 1))(self.one().wait_send)
        if first <= 2:
            self.two(self.got).wait_send()
        pl.when(z <= SIDE - 2)(self.three(self.passed.at[0], 0).wait_send)
        pl.when(z >= 1)(self.three(self.passed.at[1], 1).wait_send)


REDUCE_SEMS = 5


def sum_kernel(
    count, ffn, mixer_in, passed_in, d_inner, near_in, turned, small,
    ffn_out, mixer_out, inner_out, small_out,
    d_all, kept, near, next_, mixer, m_passed, m_arrived, d_side, inner, i_got, i_passed, i_arrived, m_done, m_back, i_done, i_back, s_near, s_next, s_done, s_line,
    ffn_send, ffn_recv, m_send, m_recv, i_send, i_recv, back_send, back_recv, s_send, s_recv, d_send, d_recv, local,
):
    where = Place(count)
    place = where.place
    more = where.stride // SIDE
    span = near.shape[5]
    odd, far = lax.rem(place, 2), place // 2
    cols = [pl.ds(c * span, span) for c in range(CHUNKS)]
    loads = [pltpu.make_async_copy(mixer_in, mixer, local.at[0]), pltpu.make_async_copy(passed_in, m_passed, local.at[1])]
    keeps = [
        pltpu.make_async_copy(
            ffn.at[:, :, :, odd, :, cols[c]] if c % 2 == 0 else ffn.at[:, :, far, :, :, cols[c]], kept.at[c], local.at[3 + c]
        )
        for c in range(CHUNKS)
    ]
    nears = [pltpu.make_async_copy(near_in.at[c], near.at[c], local.at[3 + CHUNKS + c]) for c in range(EARLY)]
    for c in loads + nears + keeps:
        c.start()
    where.greet()
    first = {
        c: remote(
            ffn.at[:, :, :, 1 - odd, :, cols[c]] if c % 2 == 0 else ffn.at[:, :, 1 - far, :, :, cols[c]],
            near.at[c], ffn_send, ffn_recv, c, where.member[1 + c % 2],
        )
        for c in range(EARLY, CHUNKS)
    }
    size = inner.shape[3]
    quarters = [
        remote(
            d_inner.at[:, :, pl.ds(pl.multiple_of((place ^ k) * size, 128), size)], d_side.at[k - 1],
            d_send, d_recv, k - 1, where.member[k],
        )
        for k in range(1, SIDE)
    ]
    own_quarter = pltpu.make_async_copy(
        d_inner.at[:, :, pl.ds(pl.multiple_of(place * size, 128), size)], d_side.at[SIDE - 1], local.at[local.shape[0] - 1]
    )
    own_quarter.start()
    for c in quarters:
        c.start()
    for c in first.values():
        c.start()
    groups, half = where.groups, s_near.shape[3]
    s_rows = [pl.ds(0, half), pl.ds(half, half)]
    s_first = [
        remote(small.at[:, :, 1 - odd, s_rows[0]], s_near.at[0], s_send, s_recv, 0, where.member[1]),
        remote(small.at[:, 1 - far, :, s_rows[1]], s_near.at[1], s_send, s_recv, 1, where.member[2]),
    ]
    for c in s_first:
        c.start()
    second = {}

    def again(c):
        kept[c] += near[c]
        bit = far if c % 2 == 0 else odd
        second[c] = remote(
            kept.at[c, :, :, 1 - bit], next_.at[c], ffn_send, ffn_recv, CHUNKS + c, where.member[2 - c % 2]
        )
        second[c].start()

    line = Reduce(where, mixer, None, m_passed, m_arrived, m_send, m_recv)
    for c in loads:
        c.wait()
    line.start_three(False)
    for c in range(EARLY):
        nears[c].wait()
        keeps[c].wait()
        again(c)
    for c in quarters:
        c.wait_recv()
    part = d_side.shape[2]
    own = 2 * part
    own_quarter.wait()
    d_all[:own, :] = d_side[SIDE - 1].reshape(own, size).astype(d_all.dtype)
    for k in range(SIDE - 1):
        for s in range(2):
            start = own + (s * (SIDE - 1) + k) * part
            d_all[start : start + part, :] = d_side[k, where.head if s == 0 else 1 - where.head].astype(d_all.dtype)
    for k in range(SIDE):
        at = slice(k * inner.shape[2], (k + 1) * inner.shape[2])
        inner[0, k] = dot(turned[at, :], d_all[...])
    other = Reduce(where, inner, i_got, i_passed, i_arrived, i_send, i_recv)
    other.start_one()
    other.start_two()
    for c in s_first:
        c.wait_recv()
    s_near[0] += small[:, :, odd, s_rows[0]]
    s_near[1] += small[:, far, :, s_rows[1]]
    s_second = [
        remote(s_near.at[0, :, 1 - far], s_next.at[0], s_send, s_recv, 2, where.member[2]),
        remote(s_near.at[1, :, 1 - odd], s_next.at[1], s_send, s_recv, 3, where.member[1]),
    ]
    for c in s_second:
        c.start()
    for c in range(EARLY, CHUNKS):
        keeps[c].wait()
        first[c].wait_recv()
        again(c)
    for c in s_second:
        c.wait_recv()
    s_done[:, :half] = s_near[0, :, far] + s_next[0]
    s_done[:, half:] = s_near[1, :, odd] + s_next[1]
    s_last = [
        remote(s_done.at[lax.rem(where.group + k, groups)], s_line.at[k], s_send, s_recv, 3 + k, where.other[k])
        for k in range(1, groups)
    ]
    for c in s_last:
        c.start()
    other.start_three(True)

    def spread(reduced, done, back, at):
        reduced.result(done)
        copies = [
            remote(done.at[:, :, place ^ k], back.at[k], back_send, back_recv, at + k, where.member[k])
            for k in range(1, SIDE)
        ]
        for c in copies:
            c.start()
        back[0] = done[:, :, place]
        return copies

    spreads = spread(line, m_done, m_back, 0)
    for c in range(CHUNKS):
        second[c].wait_recv()
        bit = far if c % 2 == 0 else odd
        ffn_out[:, :, :, c * span : (c + 1) * span] = kept[c, :, :, bit] + next_[c]
    spreads += spread(other, i_done, i_back, SIDE)
    for c in spreads:
        c.wait_recv()
    width = inner.shape[3]
    for q in range(SIDE):
        cols = slice(q * width, (q + 1) * width)
        mixer_out[:, :, :, cols] = m_back[place ^ q]
        inner_out[:, :, :, cols] = i_back[place ^ q]
    total = s_done[where.group]
    for k in range(1, groups):
        s_last[k - 1].wait_recv()
        total = total + s_line[k]
    small_out[...] = total
    for c in list(first.values()) + list(second.values()) + spreads + s_first + s_second + s_last:
        c.wait_send()
    for c in quarters:
        c.wait_send()
    line.finish(3)
    other.finish(1)


def sum_grads(ffn, mixer, passed, d_inner, near, turned, small):
    count = lax.axis_size("seq")
    more = count // SIDE // SIDE
    cut, units = ffn.shape[1:]
    rows = cut // (more * SIDE)
    size = mixer.shape[-1]
    f32 = jnp.float32
    v = lambda *shape: pltpu.VMEM(shape, f32)
    groups, tall = count // SIDE, small.shape[1]
    return pl.pallas_call(
        functools.partial(sum_kernel, count),
        out_shape=[shaped(3, more, rows, units), shaped(2, more, rows, size * SIDE), shaped(1, more, rows, size * SIDE),
                   shaped(tall, LANES)],
        in_specs=[in_hbm()] * 5 + [in_vmem()] * 2,
        out_specs=[in_vmem()] * 4,
        scratch_shapes=[
            pltpu.VMEM((turned.shape[1], size), jnp.bfloat16),
            v(CHUNKS, 3, more, 2, rows, units // CHUNKS),
            v(CHUNKS, 3, more, 2, rows, units // CHUNKS),
            v(CHUNKS, 3, more, rows, units // CHUNKS),
            v(2, SIDE, cut, size), v(2, 2, cut, size), v(2, 2, cut, size),
            v(SIDE, *d_inner.shape[:2], size),
            v(1, SIDE, cut, size), v(1, cut, size), v(2, 1, cut, size), v(2, 1, cut, size),
            v(2, more, SIDE, rows, size), v(SIDE, 2, more, rows, size),
            v(1, more, SIDE, rows, size), v(SIDE, 1, more, rows, size),
            v(2, groups, 2, tall // 2, LANES), v(2, groups, tall // 2, LANES), v(groups, tall, LANES), v(groups, tall, LANES),
        ]
        + sems(2 * CHUNKS) + sems(REDUCE_SEMS) + sems(REDUCE_SEMS) + sems(2 * SIDE) + sems(3 + groups) + sems(SIDE) + [pltpu.SemaphoreType.DMA((4 + CHUNKS + EARLY,))],
        compiler_params=pltpu.CompilerParams(
            collective_id=3, has_side_effects=True, vmem_limit_bytes=58 * 1024 * 1024
        ),
        cost_estimate=spans(100),
    )(ffn.reshape(3, more, 2, 2, rows, units), mixer, passed, d_inner, near, turned, small.reshape(groups, 2, 2, tall, LANES))


def middle_kernel(
    count, hid, grad, wg, wu, wd, hidden, y,
    dg, du, act, ffn, d_hid, up_one, down_one, y_side, sends, recvs,
):
    where = Place(count)
    z, place = where.z, where.place
    width = y_side.shape[-1]
    quarters = [
        remote(
            y.at[:, :, pl.ds(pl.multiple_of((place ^ k) * width, 128), width)], y_side.at[k - 1],
            sends, recvs, k - 1, where.member[k],
        )
        for k in range(1, SIDE)
    ]
    mine = hidden.at[where.head]
    up = remote(mine, up_one, sends, recvs, SIDE - 1, where.above)
    down = remote(mine, down_one, sends, recvs, SIDE, where.below)

    @pl.when(pl.program_id(0) == 0)
    def _():
        where.greet()
        pl.when(z < SIDE - 1)(up.start)
        pl.when(z > 0)(down.start)
        for c in quarters:
            c.start()
        ffn[...] = jnp.zeros_like(ffn)
        d_hid[...] = jnp.zeros_like(d_hid)

    gate = dot(hid[...], wg[...])
    raised = dot(hid[...], wu[...])
    d_act = dot_back(grad[...], wd[...])
    sig = 1.0 / (1.0 + jnp.exp(-gate))
    silu = gate * sig
    dg[...] = (d_act * raised * (sig + silu * (1.0 - sig))).astype(dg.dtype)
    du[...] = (d_act * silu).astype(du.dtype)
    act[...] = (silu * raised).astype(act.dtype)
    ffn[...] += dot(act[...], wd[...])
    d_hid[...] += dot_back(dg[...], wg[...]) + dot_back(du[...], wu[...])

    @pl.when(pl.program_id(0) == pl.num_programs(0) - 1)
    def _():
        for c in quarters:
            c.wait()
        pl.when(z < SIDE - 1)(up.wait_send)
        pl.when(z > 0)(down.wait_send)
        pl.when(z > 0)(up.wait_recv)
        pl.when(z < SIDE - 1)(down.wait_recv)


def feed_forward(hid, grad, w_gate, w_up, w_down, hidden, y):
    own, width = hid.shape
    units = w_gate.shape[1]
    count = lax.axis_size("seq")
    streams, length, channels = y.shape
    block = next(b for b in (256, 128) if units % b == 0)
    column = lambda rows: pl.BlockSpec((rows, block), lambda i: (0, i))
    low = jax.ShapeDtypeStruct((own, units), jnp.bfloat16)
    flat = shaped(own, width)
    one = shaped(length, width)
    return pl.pallas_call(
        functools.partial(middle_kernel, count),
        grid=(units // block,),
        in_specs=[whole(hid.shape), whole(grad.shape), column(width), column(width),
                  pl.BlockSpec((block, width), lambda i: (i, 0)), in_hbm(), in_hbm()],
        out_specs=[column(own)] * 3 + [whole(flat.shape)] * 2 + [in_hbm()] * 3,
        out_shape=[low, low, low, flat, flat, one, one, shaped(SIDE - 1, streams, length, channels // SIDE)],
        scratch_shapes=sems(SIDE + 1),
        compiler_params=pltpu.CompilerParams(
            collective_id=4, has_side_effects=True, vmem_limit_bytes=56 * 1024 * 1024
        ),
        cost_estimate=spans(20),
    )(hid, grad, w_gate, w_up, w_down, hidden, y)


LANES = 128


def gather_kernel(places, w_step, log_decay, select, *refs):
    rows, out = refs[:-1], refs[-1]
    ranks, states = w_step.shape[0], log_decay.shape[0]
    size = w_step.shape[1] // places
    high = select.shape[0] // places
    low = ranks + states + 16
    out[...] = jnp.zeros_like(out)
    for p in range(places):
        cols = slice(p * size, (p + 1) * size)
        out[p, :ranks, :size] = w_step[:, cols]
        out[p, ranks : ranks + states, :size] = log_decay[:, cols]
        for k, row in enumerate(rows):
            out[p, ranks + states + k : ranks + states + k + 1, :size] = row[:, cols]
        for b in range(select.shape[1] // LANES):
            out[p, low + b * high : low + (b + 1) * high, :] = select[
                p * high : (p + 1) * high, b * LANES : (b + 1) * LANES
            ]


def gather_small(w_step, log_decay, select, rows):
    places = lax.axis_size("seq")
    channels = w_step.shape[1]
    tall = w_step.shape[0] + log_decay.shape[0] + 16 + select.shape[0] // places * (channels // LANES)
    tall = -(-tall // 16) * 16
    return pl.pallas_call(
        functools.partial(gather_kernel, places),
        out_shape=shaped(places, tall, LANES),
        in_specs=[in_vmem()] * (3 + len(rows)),
        out_specs=in_vmem(),
        compiler_params=params(12),
        cost_estimate=spans(4),
    )(w_step, log_decay, select, *[row.reshape(1, -1) for row in rows])


def place_kernel(rank, states, taps, high, size, gains, ffn, mixer, inner, small, *outs):
    gate, up, down, mixout, outgate, w_in, w_step, log_decay, conv_taps, w_select = outs[:10]
    gate[...] = ffn[0]
    up[...] = ffn[1]
    down[...] = ffn[2]
    outgate[...] = mixer[0]
    mixout[...] = mixer[1]
    w_in[...] = inner[0]
    w_step[...] = small[:rank, :size]
    at = rank + states
    log_decay[...] = small[rank:at, :size]
    conv_taps[...] = small[at : at + taps, :size]
    at += taps
    for k, row in enumerate(outs[10:15]):
        row[...] = small[at + k : at + k + 1, :size]
    outs[15][...] = small[at + 5 : at + 6, :gains]
    at = rank + states + 16
    for b in range(w_select.shape[1] // LANES):
        w_select[:, b * LANES : (b + 1) * LANES] = small[at + b * high : at + (b + 1) * high, :]


def place_all(rank, states, taps, high, gains, channels, ffn, mixer, inner, small):
    rows, units = ffn.shape[1:]
    size = channels // lax.axis_size("seq")
    width = mixer.shape[2]
    shapes = [(rows, units), (rows, units), (rows, units), (rows, width), (rows, width), (rows, width), (rank, size),
              (states, size), (taps, size), (high, channels)] + [(1, size)] * 5 + [(1, gains)]
    return pl.pallas_call(
        functools.partial(place_kernel, rank, states, taps, high, size, gains),
        out_shape=[shaped(*shape) for shape in shapes],
        in_specs=[in_vmem()] * 4,
        out_specs=[in_vmem()] * len(shapes),
        compiler_params=params(40),
        cost_estimate=spans(6),
    )(ffn, mixer, inner, small)


epsilon = 1e-06
CUT = 1e6


def links(step, wrap=False, axis="seq"):
    n = lax.axis_size(axis)
    return [(i, (i + step) % n) for i in range(n) if wrap or 0 <= i + step < n]


def swaps(bit, axis="seq"):
    return [(i, i ^ bit) for i in range(lax.axis_size(axis))]


def send(block, route, axis="seq"):
    return lax.ppermute(block, axis, route)


def head_sum(part):
    return part + send(part, swaps(1, "head"), "head")


def own_stream(block):
    return lax.dynamic_index_in_dim(block, lax.axis_index("head"), 0, keepdims=False)


def part_of(block, index, size, axis):
    return lax.dynamic_slice_in_dim(block, index * size, size, axis)


def after(block, *earlier):
    return lax.optimization_barrier((block,) + earlier)[0]


def matmul(left, right):
    return jnp.dot(left, right, preferred_element_type=jnp.float32)


def matmul_back(left, right):
    return lax.dot_general(
        left, right, (((left.ndim - 1,), (1,)), ((), ())), preferred_element_type=jnp.float32
    )


def weight_outer(left, right):
    axes = tuple(range(left.ndim - 1))
    return lax.dot_general(left, right, ((axes, axes), ((), ())), preferred_element_type=jnp.float32)


def norm_forward(v, gain):
    scale = lax.rsqrt(jnp.mean(v * v, axis=-1, keepdims=True) + epsilon)
    return (v * scale * gain, scale)


def norm_backward(v, scale, gain, upstream):
    weighted = upstream * gain
    d_input = scale * weighted - v * scale * scale * scale * jnp.mean(
        weighted * v, axis=-1, keepdims=True
    )
    d_gain = jnp.sum(upstream * v * scale, axis=(0, 1))
    return (d_input, d_gain)


def silu_slope(v):
    sig = jax.nn.sigmoid(v)
    return sig + v * sig * (1.0 - sig)


def across(small):
    streams, length, n = small.shape
    return jnp.broadcast_to(small.reshape(streams, length * n, 1), (streams, length * n, 128))


def body(
    tokens, doc_ids, out_grad, norm_mix, w_inner, w_outgate, conv_taps, conv_bias, w_select, select_gain,
    w_step, step_bias, log_decay, skip_gain, w_mixout, norm_ffn, w_gate, w_up, w_down,
):
    streams, length, width = tokens.shape
    channels = w_inner.shape[1]
    taps = conv_taps.shape[0]
    rank = w_step.shape[0]
    states = log_decay.shape[1]
    lead = taps - 1
    count = lax.axis_size("seq")
    stride = count // SIDE
    here = lax.axis_index("seq")
    z, place = here // stride, here % SIDE
    size = channels // SIDE
    low = jnp.bfloat16

    grad_in = out_grad.astype(jnp.float32)
    source = tokens.astype(jnp.float32)
    rim_ids = jnp.broadcast_to((doc_ids[:, length - lead :] + 1).astype(jnp.float32)[:, :, None], (streams, lead, 128))
    rim = send(jnp.concatenate([source[:, length - lead :], rim_ids], axis=2), links(1))
    mine_grad, source, rim = lax.optimization_barrier((own_stream(out_grad).astype(jnp.float32), source, rim))
    line_grad = [send(mine_grad, links(stride)), send(mine_grad, links(-stride))]
    normed, scale_mix = norm_forward(source, norm_mix)
    normed_low = normed.astype(low)
    mine_normed = own_stream(normed)
    norm_near, norm_next = send(mine_normed, swaps(1)), send(mine_normed, swaps(2))
    rim_normed, _ = norm_forward(rim[:, :, :width], norm_mix)
    ext_val = matmul(jnp.concatenate([rim_normed.astype(low), normed_low], axis=1), w_inner)
    outgate = matmul(normed_low, w_outgate)
    ext_ids = jnp.concatenate([rim[:, :, width].astype(jnp.int32) - 1, doc_ids], axis=1)
    masks = [
        (ext_ids[:, k : k + length] == doc_ids).astype(jnp.float32)[:, :, None] for k in range(taps)
    ]
    value_pre = conv_bias
    for k in range(taps):
        value_pre = value_pre + conv_taps[k] * ext_val[:, k : k + length] * masks[k]
    value = jax.nn.silu(value_pre)
    value_low = value.astype(low)
    select = head_sum(matmul(value_low, w_select))
    raw_step = select[..., :rank]
    raw_b = select[..., rank : rank + states]
    raw_c = select[..., rank + states :]
    step_n, step_scale = norm_forward(raw_step, select_gain[:rank])
    bsel, b_scale = norm_forward(raw_b, select_gain[rank : rank + states])
    csel, c_scale = norm_forward(raw_c, select_gain[rank + states :])
    step_low = step_n.astype(low)
    step_pre = matmul(step_low, w_step) + step_bias
    step = jax.nn.softplus(step_pre)
    keep = doc_ids == ext_ids[:, lead - 1 : lead - 1 + length]
    fall = jnp.where(keep[:, :, None], step, CUT)
    gain = step * value
    decay_rate = -jnp.exp(log_decay).T
    rate = decay_rate * LOG2E
    b_wide, c_wide = across(bsel), across(csel)
    outs, first, grad_ring, grad_rest, side_far, side_rest = scan_forward(
        fall, gain, b_wide, c_wide, rate, line_grad, norm_near, norm_next
    )
    y = outs + skip_gain * value
    gate_z = jax.nn.silu(outgate)
    mixed = y * gate_z
    mixed_low = mixed.astype(low)
    mix = head_sum(matmul(mixed_low, w_mixout))
    resid = source + mix
    hidden, scale_ffn = norm_forward(resid, norm_ffn)
    hidden_low = hidden.astype(low)
    flat = lambda block: block.reshape(-1, block.shape[-1])
    like = lambda block: block.reshape(streams, length, -1)
    d_gate, d_up, act_low, ffn, d_hidden, *line_hidden, y_side = feed_forward(
        flat(hidden_low), flat(out_grad), w_gate, w_up, w_down, hidden, y
    )
    output = (resid + head_sum(like(ffn))).astype(low)
    d_hidden = head_sum(like(d_hidden))
    d_resid_norm, grad_norm_ffn = norm_backward(resid, scale_ffn, norm_ffn, d_hidden)
    d_resid = grad_in + d_resid_norm
    d_mix = d_resid.astype(low)
    d_mixed = matmul_back(d_mix, w_mixout)
    d_y = d_mixed * gate_z
    d_outgate = (d_mixed * y * silu_slope(outgate)).astype(low)
    grad_skip_gain = jnp.sum(d_y * value, axis=(0, 1))
    (
        d_step, d_scan, d_bsel, d_csel, decay_sum, hid_ring, hid_rest, mix_side, mix_rest, grad_end, grad_rest_end,
    ) = scan_backward(
        fall, step, value, d_y, b_wide, c_wide, rate, first, line_hidden, own_stream(d_resid), grad_ring[1]
    )

    mixer, turned = mixer_grads(
        flat(normed_low), [norm_near, norm_next, side_far, side_rest], flat(d_mix), [mix_side, mix_rest],
        flat(part_of(y, place, size, 2)), y_side,
        w_outgate, w_mixout,
    )
    mixer = mixer.reshape(2, SIDE, width // SIDE, size)
    ffn, near, passed = ffn_grads(
        (flat(hidden_low), *line_hidden, hid_ring, hid_rest),
        (flat(out_grad), *line_grad, grad_ring[1], grad_rest, grad_end, grad_rest_end),
        w_gate, w_up, w_down, d_gate, d_up, act_low, mixer,
    )
    d_step = after(d_step, ffn)

    d_value = d_y * skip_gain + d_scan
    d_step_pre = (d_step * jax.nn.sigmoid(step_pre)).astype(low)
    grad_step_bias = jnp.sum(d_step_pre, axis=(0, 1), dtype=jnp.float32)
    grad_w_step = weight_outer(step_low, d_step_pre)
    d_small = head_sum(
        jnp.concatenate(
            [matmul_back(d_step_pre, w_step), d_bsel, d_csel], axis=-1
        )
    )
    d_raw_step, gain_step = norm_backward(
        raw_step, step_scale, select_gain[:rank], d_small[..., :rank]
    )
    d_raw_b, gain_b = norm_backward(
        raw_b, b_scale, select_gain[rank : rank + states], d_small[..., rank : rank + states]
    )
    d_raw_c, gain_c = norm_backward(
        raw_c, c_scale, select_gain[rank + states :], d_small[..., rank + states :]
    )
    grad_select_gain = jnp.concatenate([gain_step, gain_b, gain_c])
    d_select = jnp.concatenate([d_raw_step, d_raw_b, d_raw_c], axis=-1).astype(low)
    grad_w_select = weight_outer(d_select, value_low)
    d_value = d_value + matmul_back(d_select, w_select)
    d_value_pre = d_value * silu_slope(value_pre)
    grad_conv_bias = jnp.sum(d_value_pre, axis=(0, 1))
    tap_grads = []
    d_ext = jnp.zeros_like(ext_val)
    for k in range(taps):
        masked = d_value_pre * masks[k]
        tap_grads.append(jnp.sum(masked * ext_val[:, k : k + length], axis=(0, 1)))
        d_ext = d_ext + jnp.pad(masked * conv_taps[k], ((0, 0), (k, lead - k), (0, 0)))
    rim_grad = send(d_ext[:, :lead], links(-1))
    d_inner = (d_ext[:, lead:] + jnp.pad(rim_grad, ((0, 0), (length - lead, 0), (0, 0)))).astype(low)
    d_normed = head_sum(matmul_back(d_inner, w_inner) + matmul_back(d_outgate, w_outgate))
    d_source, grad_norm_mix = norm_backward(source, scale_mix, norm_mix, d_normed)
    tokens_grad = d_resid + d_source

    gains = grad_select_gain.reshape(count, -1)
    spread = jnp.pad(gains, ((0, 0), (0, channels // count - gains.shape[1]))).reshape(channels)
    pad = lambda v: jnp.pad(v, (0, channels - v.shape[0]))
    rows = tap_grads + [
        grad_conv_bias, grad_step_bias, grad_skip_gain, pad(grad_norm_mix), pad(grad_norm_ffn), spread
    ]
    grad_w_step = after(grad_w_step, tokens_grad)
    small = gather_small(grad_w_step, decay_sum * decay_rate, grad_w_select, rows)
    ffn, mixer, inner, tall = sum_grads(
        ffn, mixer, passed, d_inner.astype(jnp.float32), near, turned, small
    )
    if count > SIDE * SIDE:
        groups = [[a * stride + b + SIDE * k for k in range(stride // SIDE)] for a in range(SIDE) for b in range(SIDE)]
        ffn, mixer, inner = (
            lax.psum_scatter(part, "seq", scatter_dimension=1, axis_index_groups=groups) for part in (ffn, mixer, inner)
        )
    else:
        ffn, mixer, inner = (part[:, 0] for part in (ffn, mixer, inner))
    outs = place_all(
        rank, states, taps, grad_w_select.shape[0] // count, gains.shape[1], channels, ffn, mixer, inner, tall
    )
    gate, up, down, mixout, outgate, w_in, d_w_step, d_log_decay, d_taps, d_select = outs[:10]
    conv, bias, skip, mix_gain, ffn_gain, select_gains = (row[0] for row in outs[10:])
    return (
        output,
        tokens_grad,
        mix_gain,
        w_in,
        outgate,
        d_taps,
        conv,
        d_select.T,
        select_gains,
        d_w_step,
        bias,
        d_log_decay.T,
        skip,
        mixout.T,
        ffn_gain,
        gate,
        up,
        down.T,
    )


def solution(mesh):
    in_specs = (
        P(None, "seq", None),
        P(None, "seq"),
        P(None, "seq", None),
        P(),
        P(None, "head"),
        P(None, "head"),
        P(None, "head"),
        P("head"),
        P("head", None),
        P(),
        P(None, "head"),
        P("head"),
        P("head", None),
        P("head"),
        P("head", None),
        P(),
        P(None, "head"),
        P(None, "head"),
        P("head", None),
    )
    out_specs = (
        P(None, "seq", None),
        P(None, "seq", None),
        P("seq"),
        P("seq", "head"),
        P("seq", "head"),
        P(None, ("head", "seq")),
        P(("head", "seq")),
        P("head", "seq"),
        P("seq"),
        P(None, ("head", "seq")),
        P(("head", "seq")),
        P(("head", "seq"), None),
        P(("head", "seq")),
        P("head", "seq"),
        P("seq"),
        P("seq", "head"),
        P("seq", "head"),
        P("head", "seq"),
    )
    return jax.shard_map(body, mesh=mesh, in_specs=in_specs, out_specs=out_specs, check_vma=False)
```
